128 devices in a mesh: dp: 32 (over y, x_hi, z), mp: 4 (over x_lo, core).
Axes of the slice: x: 4 (x_hi: 2, x_lo: 2; x = x_hi * 2 + x_lo), y: 4, z: 4, core: 2. Of those that a mesh axis runs over, the one named last changes fastest.
Arguments:
- block_input: bfloat16 [16384, 2048], P(('dp', 'mp')), may hold values from -6 to 6
- cotangent: bfloat16 [16384, 2048], P(('dp', 'mp')), may hold values from -6 to 6
- pad_mask: int32 [32, 2, 256], P('dp'), may hold values from 0 to 1, as said below
- seq_counts: int32 [32], P('dp'), may hold values from 1 to 2, as said below
- gain_mix: float32 [2048], replicated, may hold values from 0.5 to 1.5
- query_weight: bfloat16 [2048, 2048], replicated, may hold values from -0.375 to 0.375
- key_weight: bfloat16 [2048, 2048], replicated, may hold values from -0.375 to 0.375
- value_weight: bfloat16 [2048, 2048], replicated, may hold values from -0.125 to 0.125
- slot_weight: bfloat16 [2048, 256], replicated, may hold values from -0.25 to 0.25
- out_weight: bfloat16 [2048, 2048], replicated, may hold values from -0.375 to 0.375
- gain_ffn: float32 [2048], replicated, may hold values from 0.5 to 1.5
- gate_weight: bfloat16 [2048, 5632], P('dp', 'mp'), may hold values from -0.125 to 0.125
- up_weight: bfloat16 [2048, 5632], P('dp', 'mp'), may hold values from -0.125 to 0.125
- down_weight: bfloat16 [5632, 2048], P('mp', 'dp'), may hold values from -0.109375 to 0.109375
Outputs:
- block_output: float32 [16384, 2048], P(('dp', 'mp'))
- input_grad: float32 [16384, 2048], P(('dp', 'mp'))
- gain_mix_grad: float32 [2048], replicated
- query_grad: float32 [2048, 2048], P(('dp', 'mp'))
- key_grad: float32 [2048, 2048], P(('dp', 'mp'))
- value_grad: float32 [2048, 2048], P(('dp', 'mp'))
- slot_grad: float32 [2048, 256], P(('dp', 'mp'))
- out_grad: float32 [2048, 2048], P(('dp', 'mp'))
- gain_ffn_grad: float32 [2048], replicated
- gate_grad: float32 [2048, 5632], P('dp', 'mp')
- up_grad: float32 [2048, 5632], P('dp', 'mp')
- down_grad: float32 [5632, 2048], P('mp', 'dp')
The draws below stay inside these ranges and needn't reach their ends.
Inputs may be any that keep to these rules, and one draw needn't show every extreme that they name: `pad_mask`: each sequence's ones form a prefix of 128 positions or more; the first sequence of every index of dp is all ones. `seq_counts`: index 0 of dp holds 2 live sequences.
All inputs are finite; a program needn't handle non-finite values.
Results may differ from the reference program's by a relative error of at most 0.025.
Values may be sent and summed in bfloat16 or wider, within the bound.
No kernel may reach another device: no remote copies, remote signals or barrier semaphores. Data moves between devices by JAX's collectives and lax.ppermute only.
A program may use at most 256 MiB of HBM per device.

```python
import jax
import jax.numpy as jnp
from jax import lax

D = 2048
HEADS = 4
HEAD_DIM = 512
SLOTS = 64
FF = 5632
SEQ_LEN = 256
SEQS = 2
GROUPS = 32
TOKENS = 16384
N_MP = 4


def draw_pad_mask(key, part):
    key = jax.random.fold_in(key, 11)
    lengths = jax.random.randint(key, (GROUPS, SEQS), SEQ_LEN // 2, SEQ_LEN + 1)
    lengths = lengths.at[:, 0].set(SEQ_LEN)
    places = jnp.arange(SEQ_LEN)[None, None, :]
    return (places < lengths[:, :, None]).astype(jnp.int32)


def draw_seq_counts(key, part):
    key = jax.random.fold_in(key, 23)
    counts = jax.random.randint(key, (GROUPS,), 1, SEQS + 1)
    return counts.at[0].set(SEQS)


def block_levels(own_key, shape, shards, smallest, largest):
    def one(axis_at, parts):
        draws = jax.random.uniform(jax.random.fold_in(jax.random.fold_in(own_key, 6), axis_at), (parts,), jnp.float32, smallest / len(shards), largest / len(shards))
        return jnp.repeat(jnp.exp(draws), shape[axis_at] // parts).reshape((-1,) + (1,) * (len(shape) - axis_at - 1))

    loudness = one(*shards[0])
    for cut in shards[1:]:
        loudness = loudness * one(*cut)
    return loudness


def normal_values(own_key, extent, scale, bound, pieces=(), held_as=jnp.bfloat16):
    factor_of = block_levels(own_key, extent, pieces, -0.22, 0.18) if pieces else 1.0
    entries = jax.random.normal(own_key, extent, jnp.float32) * scale * factor_of
    return jnp.minimum(jnp.maximum(entries, -bound), bound).astype(held_as)


def setup_inputs(seed: int = 0) -> dict:
    seeds = jax.random.split(jax.random.key(seed), 15)
    return {
        "block_input": normal_values(seeds[0], (TOKENS, D), 1.0, 6.0, ((0, 128),)),
        "cotangent": normal_values(seeds[1], (TOKENS, D), 1.0, 6.0, ((0, 128),)),
        "pad_mask": draw_pad_mask(jax.random.fold_in(seeds[14], 71), 0),
        "seq_counts": draw_seq_counts(jax.random.fold_in(seeds[14], 71), 0),
        "gain_mix": jnp.clip(1.0 + 0.1 * jax.random.normal(seeds[4], (D,), jnp.float32), 0.5, 1.5),
        "query_weight": normal_values(seeds[5], (D, D), (D // 8) ** -0.5, 0.375),
        "key_weight": normal_values(seeds[6], (D, D), (D // 8) ** -0.5, 0.375),
        "value_weight": normal_values(seeds[7], (D, D), D ** -0.5, 0.125),
        "slot_weight": normal_values(seeds[8], (D, HEADS * SLOTS), (D // 4) ** -0.5, 0.25),
        "out_weight": normal_values(seeds[9], (D, D), (D // 8) ** -0.5, 0.375),
        "gain_ffn": jnp.clip(1.0 + 0.1 * jax.random.normal(seeds[10], (D,), jnp.float32), 0.5, 1.5),
        "gate_weight": normal_values(seeds[11], (D, FF), D ** -0.5, 0.125, ((0, 32), (1, 4))),
        "up_weight": normal_values(seeds[12], (D, FF), D ** -0.5, 0.125, ((0, 32), (1, 4))),
        "down_weight": normal_values(seeds[13], (FF, D), (FF // 2) ** -0.5, 0.109375, ((0, 4), (1, 32))),
    }


EPS = 1e-05
GATE_SCALE = 0.125

@jax.custom_vjp
def low(v):
    return lax.optimization_barrier(v.astype(jnp.bfloat16)).astype(jnp.float32)

@jax.custom_vjp
def low_back(v):
    return v

def low_keep(v):
    return (low(v), None)

def low_pass(kept, grad):
    return (grad,)

def back_keep(v):
    return (v, None)

def back_low(kept, grad):
    return (low(grad),)
low.defvjp(low_keep, low_pass)
low_back.defvjp(back_keep, back_low)

def precise(left, right):
    return jnp.dot(left, right, precision=lax.Precision.HIGHEST)

def rms(values, gain):
    return values * lax.rsqrt(lax.optimization_barrier(jnp.mean(values * values, axis=-1, keepdims=True)) + EPS) * gain

def mix_sequence(normed, keep_rows, query_weight, key_weight, value_weight, slot_weight):
    length = normed.shape[0]
    query_pre = low_back(precise(normed, query_weight))
    queries = low(jax.nn.silu(query_pre)).reshape(length, HEADS, HEAD_DIM)
    key_pre = low_back(precise(normed, key_weight))
    keys_all = low(jax.nn.silu(key_pre)).reshape(length, HEADS, HEAD_DIM)
    values_all = low(low_back(precise(normed, value_weight))).reshape(length, HEADS, HEAD_DIM)
    slot_pre = low_back(precise(normed, slot_weight))
    log_decay = keep_rows[:, None] * jax.nn.log_sigmoid(slot_pre) * GATE_SCALE
    written = -jnp.expm1(log_decay)
    running = jnp.cumsum(log_decay, axis=0)
    lower = (jnp.arange(length)[:, None] >= jnp.arange(length)[None, :])[:, :, None]
    spread = jnp.where(lower, running[:, None, :] - running[None, :, :], 0.0)
    carried = jnp.where(lower, jnp.exp(spread), 0.0)
    weights = carried * written[None, :, :]
    pairs = low_back(jnp.einsum('thd,jhd->tjh', queries, keys_all, precision=lax.Precision.HIGHEST))
    pairs_wide = jnp.repeat(pairs, SLOTS, axis=2)
    scores = HEAD_DIM ** (-0.5) * lax.optimization_barrier(jnp.sum(weights * pairs_wide, axis=1))
    probs = jax.nn.softmax(scores.reshape(length, HEADS, SLOTS), axis=-1).reshape(length, HEADS * SLOTS)
    mixing = lax.optimization_barrier(jnp.sum((probs[:, None, :] * weights).reshape(length, length, HEADS, SLOTS), axis=-1))
    mixing = low(mixing)
    mixed = jnp.einsum('tjh,jhd->thd', mixing, values_all, precision=lax.Precision.HIGHEST)
    return mixed.reshape(length, D)

def group_forward(params, inputs_group, keep_group):
    gain_mix, query_weight, key_weight, value_weight, slot_weight, out_weight, gain_ffn, gate_weight, up_weight, down_weight = params
    normed = low(rms(inputs_group, gain_mix))

    def one_sequence(items):
        return mix_sequence(items[0], items[1], query_weight, key_weight, value_weight, slot_weight)
    mixed = lax.map(jax.checkpoint(one_sequence), (normed.reshape(-1, SEQ_LEN, D), keep_group.reshape(-1, SEQ_LEN)))
    mixed = low_back(low(mixed.reshape(-1, D)))
    branch = low_back(precise(mixed, out_weight))
    hidden = inputs_group + keep_group[:, None] * branch
    ffn_in = low(rms(hidden, gain_ffn))
    gate_pre = low_back(precise(ffn_in, gate_weight))
    up_pre = low_back(precise(ffn_in, up_weight))
    inner = low(jax.nn.silu(gate_pre) * up_pre)
    down = low_back(precise(inner, down_weight))
    return hidden + keep_group[:, None] * down

def to_sequence(array):
    quarter = SEQ_LEN // N_MP
    return array.reshape(GROUPS, N_MP, SEQS, quarter, D).transpose(0, 2, 1, 3, 4).reshape(GROUPS, SEQS * SEQ_LEN, D)

def from_sequence(array):
    quarter = SEQ_LEN // N_MP
    return array.reshape(GROUPS, SEQS, N_MP, quarter, D).transpose(0, 2, 1, 3, 4).reshape(TOKENS, D)

def reference(block_input, cotangent, pad_mask, seq_counts, gain_mix, query_weight, key_weight, value_weight, slot_weight, out_weight, gain_ffn, gate_weight, up_weight, down_weight):
    params = tuple((item.astype(jnp.float32) for item in (gain_mix, query_weight, key_weight, value_weight, slot_weight, out_weight, gain_ffn, gate_weight, up_weight, down_weight)))
    live = (jnp.arange(SEQS)[None, :, None] < seq_counts[:, None, None]).astype(jnp.int32)
    keep = (pad_mask * live).astype(jnp.float32).reshape(GROUPS, SEQS * SEQ_LEN)
    inputs = to_sequence(block_input.astype(jnp.float32))

    def forward(params, inputs):

        def step(carry, items):
            return (carry, jax.checkpoint(group_forward)(params, items[0], items[1]))
        unused, outputs = lax.scan(step, jnp.zeros((), jnp.float32), (inputs, keep))
        return outputs
    outputs, pullback = jax.vjp(forward, params, inputs)
    param_grads, input_grads = pullback(to_sequence(cotangent.astype(jnp.float32)))
    return (from_sequence(outputs), from_sequence(input_grads), param_grads[0], param_grads[1], param_grads[2], param_grads[3], param_grads[4], param_grads[5], param_grads[6], param_grads[7], param_grads[8], param_grads[9])
```

```python
import jax
import jax.numpy as jnp
from jax import lax
from jax.experimental import pallas as pl
from jax.experimental.pallas import tpu as pltpu
from jax.sharding import PartitionSpec as P

HEAD_DIM = 512
SLOTS = 64
LENGTH = 256
RUN = 64
RUNS = 4
SEQS = 2
LEVELS = (128, 64, 32, 16, 8, 4, 2, 1)
SCALE = HEAD_DIM ** (-0.5)
GATE_SCALE = 0.125
F32 = jnp.float32
BF16 = jnp.bfloat16


def mm(left, right):
    return jnp.dot(left, right, preferred_element_type=F32)


def mm_cols(left, right):
    return lax.dot_general(left, right, (((1,), (1,)), ((), ())), preferred_element_type=F32)


def mm_rows(left, right):
    return lax.dot_general(left, right, (((0,), (0,)), ((), ())), preferred_element_type=F32)


def halves(value):
    high = value.astype(BF16)
    return high, (value - high.astype(F32)).astype(BF16)


def fine_product(left, right):
    left_high, left_low = halves(left)
    right_high, right_low = halves(right)
    rows, width = left.shape[0], right.shape[1]
    out = mm(
        jnp.concatenate([left_high, left_low], axis=0),
        jnp.concatenate([right_high, right_low], axis=1),
    )
    return out[:rows, :width] + out[:rows, width:] + out[rows:, :width]


def fine_cols_product(left, right):
    left_high, left_low = halves(left)
    right_high, right_low = halves(right)
    return mm_cols(
        jnp.concatenate([left_high, left_low, left_high], axis=1),
        jnp.concatenate([right_high, right_high, right_low], axis=1),
    )


def decay_tables(slot_pre, keep):
    log_gate = jnp.minimum(slot_pre, 0.0) - jnp.log1p(jnp.exp(-jnp.abs(slot_pre)))
    log_decay = keep * log_gate * GATE_SCALE
    half = jnp.tanh(-0.5 * log_decay)
    written = 2.0 * half / (1.0 + half)
    rows = lax.broadcasted_iota(jnp.int32, log_decay.shape, 0)
    running = log_decay
    shift = 1
    while shift < LENGTH:
        running = running + jnp.where(rows >= shift, pltpu.roll(running, shift, 0), 0.0)
        shift *= 2
    return log_decay, written, running


def later_sum(value):
    rows = lax.broadcasted_iota(jnp.int32, value.shape, 0)
    shift = 1
    while shift < LENGTH:
        value = value + jnp.where(rows < LENGTH - shift, pltpu.roll(value, LENGTH - shift, 0), 0.0)
        shift *= 2
    return value


def level_factors(running):
    rows = lax.broadcasted_iota(jnp.int32, running.shape, 0)
    last = running
    factors = {}
    size = 1
    while size < LENGTH:
        odd = (rows & size) != 0
        before = pltpu.roll(last, size, 0)
        factor = jnp.exp(jnp.where(odd, running - before, last - running))
        factors[size] = (jnp.where(odd, factor, 0.0), jnp.where(odd, 0.0, factor))
        last = jnp.where(odd, last, pltpu.roll(last, LENGTH - size, 0))
        size *= 2
    return factors


def level_map(flip):
    rows = lax.broadcasted_iota(jnp.int32, (LENGTH, LENGTH), 0)
    cols = lax.broadcasted_iota(jnp.int32, (LENGTH, LENGTH), 1)
    later = rows < cols if flip else rows > cols
    return jnp.where(later, rows ^ cols, 0), rows == cols


def at_level(where_map, size):
    return (where_map >= size) & (where_map < 2 * size)


def gather_rows(ref, rank, seq, start, width):
    parts = []
    for run in range(RUNS):
        first = pl.multiple_of(((rank ^ run) * SEQS + seq) * RUN, RUN)
        parts.append(ref[pl.ds(first, RUN), start : start + width])
    return jnp.concatenate(parts, axis=0)


def spread_rows(ref, rank, seq, start, width, value):
    for run in range(RUNS):
        first = pl.multiple_of(((rank ^ run) * SEQS + seq) * RUN, RUN)
        ref[pl.ds(first, RUN), start : start + width] = value[run * RUN : (run + 1) * RUN]


def sigmoid(value):
    return 1.0 / (1.0 + jnp.exp(-value))


def silu(value):
    return value * sigmoid(value)


def silu_slope(pre):
    sigma = sigmoid(pre)
    return sigma * (1.0 + pre * (1.0 - sigma))


def mixer_forward_kernel(rank_ref, pre_ref, keep_ref, mixed_ref, mixing_ref, probs_ref, past_ref):
    rank = rank_ref[0]
    seq = pl.program_id(0)
    queries = silu(gather_rows(pre_ref, rank, seq, 0, HEAD_DIM)).astype(BF16)
    keys = silu(gather_rows(pre_ref, rank, seq, HEAD_DIM, HEAD_DIM)).astype(BF16)
    values = gather_rows(pre_ref, rank, seq, 2 * HEAD_DIM, HEAD_DIM).astype(BF16)
    slot_pre = gather_rows(pre_ref, rank, seq, 3 * HEAD_DIM, SLOTS)
    _, written, running = decay_tables(slot_pre, keep_ref[0])
    factors = level_factors(running)
    where_map, own = level_map(False)
    pairs = mm_cols(queries, keys)
    own_pairs = jnp.sum(jnp.where(own, pairs, 0.0), axis=1, keepdims=True)
    past = jnp.zeros((LENGTH, SLOTS), F32)
    for size in LEVELS:
        after, before = factors[size]
        past = past + after * fine_product(
            jnp.where(at_level(where_map, size), pairs, 0.0), before * written
        )
    past = SCALE * past
    scores = past + SCALE * own_pairs * written
    grown = jnp.exp(scores - jnp.max(scores, axis=1, keepdims=True))
    probs = grown / jnp.sum(grown, axis=1, keepdims=True)
    mixing = jnp.where(own, jnp.sum(probs * written, axis=1, keepdims=True), 0.0)
    for size in LEVELS:
        after, before = factors[size]
        mixing = jnp.where(
            at_level(where_map, size),
            fine_cols_product(probs * after, before * written),
            mixing,
        )
    mixing = mixing.astype(BF16)
    mixed = mm(mixing, values).astype(BF16)
    spread_rows(mixed_ref, rank, seq, 0, HEAD_DIM, mixed)
    mixing_ref[0] = mixing
    probs_ref[0] = probs
    past_ref[0] = past


def mixer_backward_kernel(
    rank_ref, pre_ref, keep_ref, mixing_ref, probs_ref, past_ref, cot_ref, out_ref
):
    rank = rank_ref[0]
    seq = pl.program_id(0)
    query_pre = gather_rows(pre_ref, rank, seq, 0, HEAD_DIM)
    key_pre = gather_rows(pre_ref, rank, seq, HEAD_DIM, HEAD_DIM)
    queries = silu(query_pre).astype(BF16)
    keys = silu(key_pre).astype(BF16)
    values = gather_rows(pre_ref, rank, seq, 2 * HEAD_DIM, HEAD_DIM).astype(BF16)
    slot_pre = gather_rows(pre_ref, rank, seq, 3 * HEAD_DIM, SLOTS)
    cot = gather_rows(cot_ref, rank, seq, 0, HEAD_DIM)
    keep = keep_ref[0]
    log_decay, written, running = decay_tables(slot_pre, keep)
    factors = level_factors(running)
    where_map, own = level_map(False)
    where_flip, _ = level_map(True)
    probs = probs_ref[0]
    past = past_ref[0]
    mixing = mixing_ref[0]
    spread_rows(
        out_ref, rank, seq, 2 * HEAD_DIM, HEAD_DIM, mm_rows(mixing, cot).astype(BF16)
    )
    pairs_flip = mm_cols(keys, queries) * SCALE
    cot_flip = mm_cols(values, cot)
    mixing_cot = mm_cols(cot, values)
    own_cot = jnp.sum(jnp.where(own, mixing_cot, 0.0), axis=1, keepdims=True)
    own_pairs = jnp.sum(jnp.where(own, pairs_flip, 0.0), axis=1, keepdims=True)
    past_cot = jnp.zeros((LENGTH, SLOTS), F32)
    for size in LEVELS:
        after, before = factors[size]
        past_cot = past_cot + after * fine_product(
            jnp.where(at_level(where_map, size), mixing_cot, 0.0), before * written
        )
    probs_cot = past_cot + own_cot * written
    scores_cot = probs * (probs_cot - jnp.sum(probs * probs_cot, axis=1, keepdims=True))
    row_flow = probs * past_cot + scores_cot * past
    pairs_cot = jnp.where(own, jnp.sum(scores_cot * written, axis=1, keepdims=True), 0.0)
    ahead = jnp.zeros((LENGTH, SLOTS), F32)
    both_flip = jnp.concatenate([cot_flip, pairs_flip], axis=1)
    where_both = jnp.concatenate([where_flip, where_flip], axis=1)
    for size in LEVELS:
        after, before = factors[size]
        pairs_cot = jnp.where(
            at_level(where_map, size),
            fine_cols_product(scores_cot * after, before * written),
            pairs_cot,
        )
        ahead = ahead + before * fine_product(
            jnp.where(at_level(where_both, size), both_flip, 0.0),
            jnp.concatenate([probs * after, scores_cot * after], axis=0),
        )
    pairs_low = (SCALE * pairs_cot).astype(BF16)
    query_cot = (mm(pairs_low, keys) * silu_slope(query_pre)).astype(BF16)
    spread_rows(out_ref, rank, seq, 0, HEAD_DIM, query_cot)
    key_cot = (mm_rows(pairs_low, queries) * silu_slope(key_pre)).astype(BF16)
    spread_rows(out_ref, rank, seq, HEAD_DIM, HEAD_DIM, key_cot)
    running_cot = row_flow - written * ahead
    written_cot = ahead + own_cot * probs + scores_cot * own_pairs
    decay_cot = later_sum(running_cot) - written_cot * jnp.exp(log_decay)
    slot_cot = decay_cot * keep * GATE_SCALE * sigmoid(-slot_pre)
    padded = jnp.concatenate([slot_cot, jnp.zeros((LENGTH, SLOTS), F32)], axis=1).astype(BF16)
    spread_rows(out_ref, rank, seq, 3 * HEAD_DIM, 2 * SLOTS, padded)


def whole(shape):
    zeros = (0,) * len(shape)
    return pl.BlockSpec(shape, lambda seq: zeros)


def one_seq(shape):
    return pl.BlockSpec((1,) + shape, lambda seq: (seq, 0, 0))


TOKENS = RUNS * SEQS * RUN
WIDE = 3 * HEAD_DIM + 2 * SLOTS
RANK_SPEC = pl.BlockSpec(memory_space=pltpu.SMEM)


def mixer_forward(rank, pre, keep):
    return pl.pallas_call(
        mixer_forward_kernel,
        grid=(SEQS,),
        in_specs=[RANK_SPEC, whole((TOKENS, WIDE)), one_seq((LENGTH, 1))],
        out_specs=[
            whole((TOKENS, HEAD_DIM)),
            one_seq((LENGTH, LENGTH)),
            one_seq((LENGTH, SLOTS)),
            one_seq((LENGTH, SLOTS)),
        ],
        out_shape=[
            jax.ShapeDtypeStruct((TOKENS, HEAD_DIM), BF16),
            jax.ShapeDtypeStruct((SEQS, LENGTH, LENGTH), BF16),
            jax.ShapeDtypeStruct((SEQS, LENGTH, SLOTS), F32),
            jax.ShapeDtypeStruct((SEQS, LENGTH, SLOTS), F32),
        ],
        compiler_params=pltpu.CompilerParams(
            vmem_limit_bytes=48 * 1024 * 1024, dimension_semantics=("arbitrary",)
        ),
        name="mixer_forward",
    )(rank, pre, keep)


def mixer_backward(rank, pre, keep, mixing, probs, past, cot):
    return pl.pallas_call(
        mixer_backward_kernel,
        grid=(SEQS,),
        in_specs=[
            RANK_SPEC,
            whole((TOKENS, WIDE)),
            one_seq((LENGTH, 1)),
            one_seq((LENGTH, LENGTH)),
            one_seq((LENGTH, SLOTS)),
            one_seq((LENGTH, SLOTS)),
            whole((TOKENS, HEAD_DIM)),
        ],
        out_specs=whole((TOKENS, WIDE)),
        out_shape=jax.ShapeDtypeStruct((TOKENS, WIDE), BF16),
        compiler_params=pltpu.CompilerParams(
            vmem_limit_bytes=48 * 1024 * 1024, dimension_semantics=("arbitrary",)
        ),
        name="mixer_backward",
    )(rank, pre, keep, mixing, probs, past, cot)


EPS = 1e-05
WIDTH = 2048
K_TILE = 512
ALL_SLOTS = 4 * SLOTS
ROWS_OWN = SEQS * RUN
TILE = 256
TILES = 3
HIDDEN = TILE * TILES


def cost(flops, bytes_accessed):
    return pl.CostEstimate(flops=flops, bytes_accessed=bytes_accessed, transcendentals=0)


def project_kernel(
    rank_ref, own_ref, near_ref, far_ref, farthest_ref, gain_ref,
    query_ref, key_ref, value_ref, slot_ref, pre_ref, normed_ref, slots_ref,
):
    step = pl.program_id(0)

    @pl.when(step == 0)
    def _():
        for i, ref in enumerate((own_ref, near_ref, far_ref, farthest_ref)):
            rows = ref[...].astype(F32)
            root = lax.rsqrt(jnp.mean(rows * rows, axis=1, keepdims=True) + EPS)
            normed_ref[i * ROWS_OWN : (i + 1) * ROWS_OWN] = (rows * root * gain_ref[...]).astype(
                BF16
            )
        pre_ref[...] = jnp.zeros_like(pre_ref)
        slots_ref[...] = jnp.zeros_like(slots_ref)

    left = normed_ref[:, pl.ds(pl.multiple_of(step * K_TILE, K_TILE), K_TILE)]
    for i, ref in enumerate((query_ref, key_ref, value_ref)):
        pre_ref[:, i * HEAD_DIM : (i + 1) * HEAD_DIM] += mm(left, ref[...])
    slots_ref[...] += mm(left, slot_ref[...])

    @pl.when(step == WIDTH // K_TILE - 1)
    def _():
        mine = jnp.zeros((TOKENS, SLOTS), F32)
        for head in range(4):
            mine = jnp.where(
                rank_ref[0] == head, slots_ref[:, head * SLOTS : (head + 1) * SLOTS], mine
            )
        pre_ref[:, 3 * HEAD_DIM :] = jnp.concatenate([mine, jnp.zeros_like(mine)], axis=1)


def project(rank, pieces, gain, query_weight, key_weight, value_weight, slot_weight):
    piece = pl.BlockSpec((ROWS_OWN, WIDTH), lambda k, rank: (0, 0))
    weight = pl.BlockSpec((K_TILE, HEAD_DIM), lambda k, rank: (k, rank[0]))
    return pl.pallas_call(
        project_kernel,
        grid_spec=pltpu.PrefetchScalarGridSpec(
            num_scalar_prefetch=1,
            grid=(WIDTH // K_TILE,),
            in_specs=[piece] * 4
            + [
                pl.BlockSpec((1, WIDTH), lambda k, rank: (0, 0)),
                weight,
                weight,
                weight,
                pl.BlockSpec((K_TILE, ALL_SLOTS), lambda k, rank: (k, 0)),
            ],
            out_specs=[
                pl.BlockSpec((TOKENS, WIDE), lambda k, rank: (0, 0)),
                pl.BlockSpec((TOKENS, WIDTH), lambda k, rank: (0, 0)),
            ],
            scratch_shapes=[pltpu.VMEM((TOKENS, ALL_SLOTS), F32)],
        ),
        out_shape=[
            jax.ShapeDtypeStruct((TOKENS, WIDE), F32),
            jax.ShapeDtypeStruct((TOKENS, WIDTH), BF16),
        ],
        compiler_params=pltpu.CompilerParams(
            vmem_limit_bytes=48 * 1024 * 1024, dimension_semantics=("arbitrary",)
        ),
        cost_estimate=cost(2 * TOKENS * WIDTH * 1792, 16 * 1024 * 1024),
        name="project",
    )(rank, *pieces, gain, query_weight, key_weight, value_weight, slot_weight)


def unproject_kernel(rank_ref, cots_ref, query_ref, key_ref, value_ref, slot_ref, out_ref):
    total = mm_cols(cots_ref[:, :HEAD_DIM], query_ref[...])
    total += mm_cols(cots_ref[:, HEAD_DIM : 2 * HEAD_DIM], key_ref[...])
    total += mm_cols(cots_ref[:, 2 * HEAD_DIM : 3 * HEAD_DIM], value_ref[...])
    slots = cots_ref[:, 3 * HEAD_DIM : 3 * HEAD_DIM + SLOTS]
    spread = jnp.concatenate(
        [jnp.where(rank_ref[0] == head, slots, jnp.zeros_like(slots)) for head in range(4)],
        axis=1,
    )
    out_ref[...] = (total + mm_cols(spread, slot_ref[...])).astype(BF16)


def unproject(rank, cots, query_weight, key_weight, value_weight, slot_weight):
    weight = pl.BlockSpec((K_TILE, HEAD_DIM), lambda k, rank: (k, rank[0]))
    return pl.pallas_call(
        unproject_kernel,
        grid_spec=pltpu.PrefetchScalarGridSpec(
            num_scalar_prefetch=1,
            grid=(WIDTH // K_TILE,),
            in_specs=[
                pl.BlockSpec((TOKENS, WIDE), lambda k, rank: (0, 0)),
                weight,
                weight,
                weight,
                pl.BlockSpec((K_TILE, ALL_SLOTS), lambda k, rank: (k, 0)),
            ],
            out_specs=pl.BlockSpec((TOKENS, K_TILE), lambda k, rank: (0, k)),
        ),
        out_shape=jax.ShapeDtypeStruct((TOKENS, WIDTH), BF16),
        compiler_params=pltpu.CompilerParams(
            vmem_limit_bytes=48 * 1024 * 1024, dimension_semantics=("arbitrary",)
        ),
        cost_estimate=cost(2 * TOKENS * WIDTH * 1792, 11 * 1024 * 1024),
        name="unproject",
    )(rank, cots, query_weight, key_weight, value_weight, slot_weight)


def ffn_kernel(
    own_ref, left_ref, right_ref, first_ref, second_ref, away_ref, cot_ref, pair_ref, down_ref,
    inner_ref, cots_ref, rows_ref,
):
    @pl.when(pl.program_id(0) == 0)
    def _():
        start = 0
        for ref in (own_ref, left_ref, right_ref, first_ref, second_ref, away_ref):
            rows_ref[start : start + ref.shape[0]] = ref[...]
            start += ref.shape[0]

    for half in range(2):
        rows = slice(half * TOKENS, (half + 1) * TOKENS)
        both = mm(rows_ref[rows], pair_ref[...])
        gate_pre, up_pre = both[:, :TILE], both[:, TILE:]
        inner_cot = mm(cot_ref[rows], down_ref[...])
        sigma = sigmoid(gate_pre)
        gate_act = gate_pre * sigma
        inner_ref[rows] = (gate_act * up_pre).astype(BF16)
        slope = sigma * (1.0 + gate_pre * (1.0 - sigma))
        cots_ref[rows, :TILE] = (inner_cot * up_pre * slope).astype(BF16)
        cots_ref[rows, TILE:] = (inner_cot * gate_act).astype(BF16)


def ffn(pieces, cot, weights):
    def fixed(rows):
        return pl.BlockSpec((rows, WIDTH), lambda n: (0, 0))

    both = 2 * TOKENS
    return pl.pallas_call(
        ffn_kernel,
        grid=(TILES,),
        in_specs=[fixed(piece.shape[0]) for piece in pieces]
        + [
            fixed(both),
            pl.BlockSpec((WIDTH, 2 * TILE), lambda n: (0, n)),
            pl.BlockSpec((WIDTH, TILE), lambda n: (0, 2 * TILES + n)),
        ],
        out_specs=[
            pl.BlockSpec((both, TILE), lambda n: (0, n)),
            pl.BlockSpec((both, 2 * TILE), lambda n: (0, n)),
            fixed(both),
        ],
        out_shape=[
            jax.ShapeDtypeStruct((both, HIDDEN), BF16),
            jax.ShapeDtypeStruct((both, 2 * HIDDEN), BF16),
            jax.ShapeDtypeStruct((both, WIDTH), BF16),
        ],
        compiler_params=pltpu.CompilerParams(
            vmem_limit_bytes=56 * 1024 * 1024, dimension_semantics=("arbitrary",)
        ),
        cost_estimate=cost(6 * both * WIDTH * HIDDEN, 26 * 1024 * 1024),
        name="ffn",
    )(*pieces, cot, weights, weights)


AXES = ("y", "xh", "z", "xl", "c")
DP = ("y", "xh", "z")
MP = ("xl", "c")
RING = ("xh", "xl")
PLANE = ("y", "z")
SWAP = ((0, 1), (1, 0))


def rms_forward(values, gain):
    inv_root = lax.rsqrt(jnp.mean(values * values, axis=-1, keepdims=True) + EPS)
    unit_rows = values * inv_root
    return unit_rows * gain, unit_rows, inv_root


def rms_backward(incoming, gain, unit_rows, inv_root):
    scaled = incoming * gain
    return inv_root * (scaled - unit_rows * jnp.mean(scaled * unit_rows, axis=-1, keepdims=True))


def to_plane_order(rows):
    count, width = rows.shape
    return rows.reshape(count, 4, 2, 4, width // 32).transpose(0, 1, 3, 2, 4).reshape(count, width)


def from_plane_order(rows):
    count, width = rows.shape
    return rows.reshape(count, 4, 4, 2, width // 32).transpose(0, 1, 3, 2, 4).reshape(count, width)


def other_core(value):
    return lax.ppermute(value, "c", SWAP)


def other_chip(value):
    return lax.ppermute(value, "xl", SWAP)


def along_ring(value, step):
    return lax.ppermute(value, RING, [(i, (i + step) % 4) for i in range(4)])


def gather_four(own):
    far = other_chip(own)
    return own, other_core(own), far, other_core(far)


def sum_four(rows):
    own, near, far, farthest = jnp.split(rows, 4, axis=0)
    own, far = own.astype(F32), far.astype(F32)
    got = other_core(jnp.concatenate([near, farthest], axis=0)).astype(F32)
    quarter = own.shape[0]
    far_sum = (far + got[quarter:]).astype(BF16)
    return own + got[:quarter] + other_chip(far_sum).astype(F32)


def gather_eight(own):
    half = own.shape[0] // 2
    left = along_ring(own, 1)
    right = along_ring(own, -1)
    opposite = [along_ring(left[:half], 1), along_ring(right[half:], -1)]
    near = [own, left, right] + opposite
    return near + [other_core(jnp.concatenate(near, axis=0))]


def sum_eight(rows):
    near, away = jnp.split(rows, 2, axis=0)
    near = near.astype(F32) + other_core(away).astype(F32)
    own, left, right, opposite = jnp.split(near, 4, axis=0)
    half = own.shape[0] // 2
    opposite = opposite.astype(BF16)
    from_left = along_ring(opposite[:half], 1).astype(F32)
    from_right = along_ring(opposite[half:], -1).astype(F32)
    right = jnp.concatenate([right[:half] + from_left, right[half:]], axis=0).astype(BF16)
    left = jnp.concatenate([left[:half], left[half:] + from_right], axis=0).astype(BF16)
    return own + along_ring(right, 1).astype(F32) + along_ring(left, -1).astype(F32)


def sum_all(value):
    for axis in ("c", "xl", "xh"):
        value = value + lax.ppermute(value, axis, SWAP)
    for axis in PLANE:
        for step in (1, 2):
            value = value + lax.ppermute(value, axis, [(i, i ^ step) for i in range(4)])
    return value


def on_device(
    block_input,
    cotangent,
    pad_mask,
    seq_counts,
    gain_mix,
    query_weight,
    key_weight,
    value_weight,
    slot_weight,
    out_weight,
    gain_ffn,
    gate_weight,
    up_weight,
    down_weight,
):
    rows_own, width = block_input.shape
    rank = lax.axis_index(MP)
    side = lax.axis_index("xh")
    live = (jnp.arange(SEQS) < seq_counts[0]).astype(jnp.int32)
    keep_seq = (pad_mask[0] * live[:, None]).astype(F32)
    keep_own = lax.dynamic_slice_in_dim(keep_seq, rank * RUN, RUN, 1).reshape(rows_own, 1)

    rank_array = rank.reshape(1).astype(jnp.int32)
    input_pieces = gather_four(block_input)

    hidden_part = gate_weight.shape[1] // 2
    owned = jnp.stack([gate_weight, up_weight, down_weight.T])
    kept = lax.dynamic_slice_in_dim(owned, side * hidden_part, hidden_part, 2)
    given = lax.dynamic_slice_in_dim(owned, (1 - side) * hidden_part, hidden_part, 2)
    got = lax.ppermute(given, "xh", SWAP)
    paired = jnp.concatenate(
        [jnp.where(side == 0, kept, got), jnp.where(side == 0, got, kept)], axis=1
    )
    paired = jnp.pad(paired, ((0, 0), (0, 0), (0, HIDDEN - hidden_part)))
    paired = paired.reshape(3, 128, TILES, TILE)
    columns = [paired[i, :, n] for n in range(TILES) for i in range(2)]
    columns += [paired[2, :, n] for n in range(TILES)]
    weights = lax.all_gather(jnp.concatenate(columns, axis=1), PLANE, axis=0, tiled=True)

    cot_own = to_plane_order(cotangent)
    cot_start, _ = lax.optimization_barrier((cot_own * keep_own.astype(BF16), input_pieces[2]))
    down_cot = jnp.concatenate(gather_eight(cot_start), axis=0)

    gain_ffn_plane = to_plane_order(gain_ffn[None])
    input_own = block_input.astype(F32)
    _, unit_mix, root_mix = rms_forward(input_own, gain_mix)
    mixer_weights = (query_weight, key_weight, value_weight, slot_weight)
    pre, normed_four = project(rank_array, input_pieces, gain_mix[None], *mixer_weights)
    keep_column = keep_seq[:, :, None]
    mixed_four, mixing, probs, past = mixer_forward(rank_array, pre, keep_column)
    blocks = jnp.split(mixed_four, 4, axis=0)
    mixed_parts = jnp.stack(
        [
            blocks[0],
            other_core(blocks[1]),
            other_chip(blocks[2]),
            lax.ppermute(blocks[3], MP, [(i, 3 - i) for i in range(4)]),
        ]
    )
    mixed_own = jnp.concatenate(
        [
            lax.dynamic_index_in_dim(mixed_parts, rank ^ head, keepdims=False)
            for head in range(4)
        ],
        axis=1,
    )
    mixed_own, down_cot = lax.optimization_barrier((mixed_own, down_cot))
    branch = mm(mixed_own, out_weight)
    hidden_own = to_plane_order(input_own + keep_own * branch)
    normed_ffn, unit_ffn, root_ffn = rms_forward(hidden_own, gain_ffn_plane)
    pieces = gather_eight(normed_ffn.astype(BF16))
    inner, cots, ffn_in = ffn(pieces, down_cot, weights)
    ffn_grads = jnp.concatenate(
        [mm_rows(ffn_in, cots).astype(BF16), mm_rows(down_cot, inner).astype(BF16)], axis=1
    )
    ffn_grads = lax.psum_scatter(ffn_grads, PLANE, scatter_dimension=0, tiled=True)
    ffn_cot = sum_eight(mm_cols(cots, weights[:, : 2 * HIDDEN]).astype(BF16))
    ffn_own = sum_eight(mm_cols(inner, weights[:, 2 * HIDDEN :]).astype(BF16))
    block_output = from_plane_order(hidden_own + keep_own * ffn_own)
    hidden_cot = cot_own.astype(F32) + rms_backward(ffn_cot, gain_ffn_plane, unit_ffn, root_ffn)
    gain_ffn_part = jnp.sum(ffn_cot * unit_ffn, axis=0)
    branch_cot = from_plane_order((keep_own * hidden_cot).astype(BF16))
    branch_four = jnp.concatenate(gather_four(branch_cot), axis=0)
    out_rows = lax.dynamic_slice_in_dim(out_weight, rank * HEAD_DIM, HEAD_DIM, 0)
    mixed_cot = mm_cols(branch_four, out_rows).astype(BF16)
    head_cots = mixer_backward(rank_array, pre, keep_column, mixing, probs, past, mixed_cot)
    normed_cot = sum_four(unproject(rank_array, head_cots, *mixer_weights))
    input_grad = from_plane_order(hidden_cot) + rms_backward(
        normed_cot, gain_mix, unit_mix, root_mix
    )
    gain_mix_part = jnp.sum(normed_cot * unit_mix, axis=0)

    head_grads = mm_rows(normed_four, head_cots).astype(BF16)
    mixed_all = jnp.concatenate(gather_four(mixed_own), axis=0)
    out_grad = mm_rows(
        mixed_all, lax.dynamic_slice_in_dim(branch_four, rank * HEAD_DIM, HEAD_DIM, 1)
    ).astype(BF16)
    mixer_grads = jnp.concatenate([out_grad, head_grads], axis=1)
    mixer_grads = (
        mixer_grads.reshape(4, 2, 4, width // 32, HEAD_DIM + WIDE)
        .transpose(0, 2, 1, 3, 4)
        .reshape(width, HEAD_DIM + WIDE)
    )
    mixer_sums = lax.psum_scatter(mixer_grads, PLANE, scatter_dimension=0, tiled=True)
    rows_out = rows_own // 8
    pieces = lax.all_to_all(
        mixer_sums.reshape(8, rows_out, HEAD_DIM + WIDE), RING + ("c",), 0, 0
    )
    pieces = pieces.reshape(2, 4, rows_out, HEAD_DIM + WIDE).astype(F32).sum(0).transpose(1, 0, 2)

    def columns(start, count):
        return pieces[:, :, start : start + count].reshape(rows_out, 4 * count)

    ffn_grads = ffn_grads.reshape(128, 3 * TILES, TILE)
    gate_grad, up_grad, down_grad = [
        jnp.concatenate([ffn_grads[:, n] for n in tiles], axis=1)[:, :hidden_part]
        for tiles in ((0, 2, 4), (1, 3, 5), (6, 7, 8))
    ]

    def finish(grad):
        keeps = lax.dynamic_slice_in_dim(grad, side * 64, 64, 0)
        gives = lax.dynamic_slice_in_dim(grad, (1 - side) * 64, 64, 0)
        gets = lax.ppermute(gives, "xh", SWAP)
        return jnp.concatenate(
            [jnp.where(side == 0, keeps, gets), jnp.where(side == 0, gets, keeps)], axis=1
        ).astype(F32)

    gain_sums = sum_all(
        jnp.stack([gain_mix_part, from_plane_order(gain_ffn_part[None])[0]]).reshape(32, 128)
    ).reshape(2, width)
    return (
        block_output,
        input_grad,
        gain_sums[0],
        columns(HEAD_DIM, HEAD_DIM),
        columns(2 * HEAD_DIM, HEAD_DIM),
        columns(3 * HEAD_DIM, HEAD_DIM),
        columns(4 * HEAD_DIM, SLOTS),
        columns(0, HEAD_DIM),
        gain_sums[1],
        finish(gate_grad),
        finish(up_grad),
        finish(down_grad).T,
    )


def solution(mesh):
    fine = jax.sharding.Mesh(mesh.devices.reshape(4, 2, 4, 2, 2), AXES)
    rows = P(AXES, None)
    return jax.shard_map(
        on_device,
        mesh=fine,
        in_specs=(
            rows,
            rows,
            P(DP, None, None),
            P(DP),
            P(),
            P(),
            P(),
            P(),
            P(),
            P(),
            P(),
            P(DP, MP),
            P(DP, MP),
            P(MP, DP),
        ),
        out_specs=(
            rows,
            rows,
            P(),
            rows,
            rows,
            rows,
            rows,
            rows,
            P(),
            P(DP, MP),
            P(DP, MP),
            P(MP, DP),
        ),
        check_vma=False,
    )
```

```python
import functools

import jax
import jax.numpy as jnp
from jax import lax
from jax.experimental import pallas as pl
from jax.experimental.pallas import tpu as pltpu
from jax.sharding import PartitionSpec as P

HEAD_DIM = 512
SLOTS = 64
LENGTH = 256
RUN = 64
RUNS = 4
SEQS = 2
LEVELS = (128, 64, 32, 16, 8, 4, 2, 1)
SCALE = HEAD_DIM ** (-0.5)
GATE_SCALE = 0.125
F32 = jnp.float32
BF16 = jnp.bfloat16


def mm(left, right):
    return jnp.dot(left, right, preferred_element_type=F32)


def mm_cols(left, right):
    return lax.dot_general(left, right, (((1,), (1,)), ((), ())), preferred_element_type=F32)


def mm_rows(left, right):
    return lax.dot_general(left, right, (((0,), (0,)), ((), ())), preferred_element_type=F32)


def halves(value):
    high = value.astype(BF16)
    return high, (value - high.astype(F32)).astype(BF16)


def fine_product(left, right):
    left_high, left_low = halves(left)
    right_high, right_low = halves(right)
    rows, width = left.shape[0], right.shape[1]
    out = mm(
        jnp.concatenate([left_high, left_low], axis=0),
        jnp.concatenate([right_high, right_low], axis=1),
    )
    return out[:rows, :width] + out[:rows, width:] + out[rows:, :width]


def fine_cols_product(left, right):
    left_high, left_low = halves(left)
    right_high, right_low = halves(right)
    return mm_cols(
        jnp.concatenate([left_high, left_low, left_high], axis=1),
        jnp.concatenate([right_high, right_high, right_low], axis=1),
    )


def decay_tables(slot_pre, keep):
    log_gate = jnp.minimum(slot_pre, 0.0) - jnp.log1p(jnp.exp(-jnp.abs(slot_pre)))
    log_decay = keep * log_gate * GATE_SCALE
    half = jnp.tanh(-0.5 * log_decay)
    written = 2.0 * half / (1.0 + half)
    rows = lax.broadcasted_iota(jnp.int32, log_decay.shape, 0)
    running = log_decay
    shift = 1
    while shift < LENGTH:
        running = running + jnp.where(rows >= shift, pltpu.roll(running, shift, 0), 0.0)
        shift *= 2
    return log_decay, written, running


def later_sum(value):
    rows = lax.broadcasted_iota(jnp.int32, value.shape, 0)
    shift = 1
    while shift < LENGTH:
        value = value + jnp.where(rows < LENGTH - shift, pltpu.roll(value, LENGTH - shift, 0), 0.0)
        shift *= 2
    return value


def level_factors(running):
    rows = lax.broadcasted_iota(jnp.int32, running.shape, 0)
    last = running
    factors = {}
    size = 1
    while size < LENGTH:
        odd = (rows & size) != 0
        before = pltpu.roll(last, size, 0)
        factor = jnp.exp(jnp.where(odd, running - before, last - running))
        factors[size] = (jnp.where(odd, factor, 0.0), jnp.where(odd, 0.0, factor))
        last = jnp.where(odd, last, pltpu.roll(last, LENGTH - size, 0))
        size *= 2
    return factors


def level_map(flip):
    rows = lax.broadcasted_iota(jnp.int32, (LENGTH, LENGTH), 0)
    cols = lax.broadcasted_iota(jnp.int32, (LENGTH, LENGTH), 1)
    later = rows < cols if flip else rows > cols
    return jnp.where(later, rows ^ cols, 0), rows == cols


def at_level(where_map, size):
    return (where_map >= size) & (where_map < 2 * size)


def gather_rows(ref, rank, seq, start, width):
    parts = []
    for run in range(RUNS):
        first = pl.multiple_of(((rank ^ run) * SEQS + seq) * RUN, RUN)
        parts.append(ref[pl.ds(first, RUN), start : start + width])
    return jnp.concatenate(parts, axis=0)


def spread_rows(ref, rank, seq, start, width, value):
    for run in range(RUNS):
        first = pl.multiple_of(((rank ^ run) * SEQS + seq) * RUN, RUN)
        ref[pl.ds(first, RUN), start : start + width] = value[run * RUN : (run + 1) * RUN]


def sigmoid(value):
    return 1.0 / (1.0 + jnp.exp(-value))


def silu(value):
    return value * sigmoid(value)


def silu_slope(pre):
    sigma = sigmoid(pre)
    return sigma * (1.0 + pre * (1.0 - sigma))


def mixer_forward_kernel(rank_ref, pre_ref, keep_ref, mixed_ref, mixing_ref, probs_ref, past_ref):
    rank = rank_ref[0]
    seq = pl.program_id(0)
    queries = silu(gather_rows(pre_ref, rank, seq, 0, HEAD_DIM)).astype(BF16)
    keys = silu(gather_rows(pre_ref, rank, seq, HEAD_DIM, HEAD_DIM)).astype(BF16)
    values = gather_rows(pre_ref, rank, seq, 2 * HEAD_DIM, HEAD_DIM).astype(BF16)
    slot_pre = gather_rows(pre_ref, rank, seq, 3 * HEAD_DIM, SLOTS)
    _, written, running = decay_tables(slot_pre, keep_ref[0])
    factors = level_factors(running)
    where_map, own = level_map(False)
    pairs = mm_cols(queries, keys)
    own_pairs = jnp.sum(jnp.where(own, pairs, 0.0), axis=1, keepdims=True)
    past = jnp.zeros((LENGTH, SLOTS), F32)
    for size in LEVELS:
        after, before = factors[size]
        past = past + after * fine_product(
            jnp.where(at_level(where_map, size), pairs, 0.0), before * written
        )
    past = SCALE * past
    scores = past + SCALE * own_pairs * written
    grown = jnp.exp(scores - jnp.max(scores, axis=1, keepdims=True))
    probs = grown / jnp.sum(grown, axis=1, keepdims=True)
    mixing = jnp.where(own, jnp.sum(probs * written, axis=1, keepdims=True), 0.0)
    for size in LEVELS:
        after, before = factors[size]
        mixing = jnp.where(
            at_level(where_map, size),
            fine_cols_product(probs * after, before * written),
            mixing,
        )
    mixing = mixing.astype(BF16)
    mixed = mm(mixing, values).astype(BF16)
    spread_rows(mixed_ref, rank, seq, 0, HEAD_DIM, mixed)
    mixing_ref[0] = mixing
    probs_ref[0] = probs
    past_ref[0] = past


def mixer_backward_kernel(
    rank_ref, pre_ref, keep_ref, mixing_ref, probs_ref, past_ref, cot_ref, out_ref
):
    rank = rank_ref[0]
    seq = pl.program_id(0)
    query_pre = gather_rows(pre_ref, rank, seq, 0, HEAD_DIM)
    key_pre = gather_rows(pre_ref, rank, seq, HEAD_DIM, HEAD_DIM)
    queries = silu(query_pre).astype(BF16)
    keys = silu(key_pre).astype(BF16)
    values = gather_rows(pre_ref, rank, seq, 2 * HEAD_DIM, HEAD_DIM).astype(BF16)
    slot_pre = gather_rows(pre_ref, rank, seq, 3 * HEAD_DIM, SLOTS)
    cot = gather_rows(cot_ref, rank, seq, 0, HEAD_DIM)
    keep = keep_ref[0]
    log_decay, written, running = decay_tables(slot_pre, keep)
    factors = level_factors(running)
    where_map, own = level_map(False)
    where_flip, _ = level_map(True)
    probs = probs_ref[0]
    past = past_ref[0]
    mixing = mixing_ref[0]
    spread_rows(
        out_ref, rank, seq, 2 * HEAD_DIM, HEAD_DIM, mm_rows(mixing, cot).astype(BF16)
    )
    pairs_flip = mm_cols(keys, queries) * SCALE
    cot_flip = mm_cols(values, cot)
    mixing_cot = mm_cols(cot, values)
    own_cot = jnp.sum(jnp.where(own, mixing_cot, 0.0), axis=1, keepdims=True)
    own_pairs = jnp.sum(jnp.where(own, pairs_flip, 0.0), axis=1, keepdims=True)
    past_cot = jnp.zeros((LENGTH, SLOTS), F32)
    for size in LEVELS:
        after, before = factors[size]
        past_cot = past_cot + after * fine_product(
            jnp.where(at_level(where_map, size), mixing_cot, 0.0), before * written
        )
    probs_cot = past_cot + own_cot * written
    scores_cot = probs * (probs_cot - jnp.sum(probs * probs_cot, axis=1, keepdims=True))
    row_flow = probs * past_cot + scores_cot * past
    pairs_cot = jnp.where(own, jnp.sum(scores_cot * written, axis=1, keepdims=True), 0.0)
    ahead = jnp.zeros((LENGTH, SLOTS), F32)
    both_flip = jnp.concatenate([cot_flip, pairs_flip], axis=1)
    where_both = jnp.concatenate([where_flip, where_flip], axis=1)
    for size in LEVELS:
        after, before = factors[size]
        pairs_cot = jnp.where(
            at_level(where_map, size),
            fine_cols_product(scores_cot * after, before * written),
            pairs_cot,
        )
        ahead = ahead + before * fine_product(
            jnp.where(at_level(where_both, size), both_flip, 0.0),
            jnp.concatenate([probs * after, scores_cot * after], axis=0),
        )
    pairs_low = (SCALE * pairs_cot).astype(BF16)
    query_cot = (mm(pairs_low, keys) * silu_slope(query_pre)).astype(BF16)
    spread_rows(out_ref, rank, seq, 0, HEAD_DIM, query_cot)
    key_cot = (mm_rows(pairs_low, queries) * silu_slope(key_pre)).astype(BF16)
    spread_rows(out_ref, rank, seq, HEAD_DIM, HEAD_DIM, key_cot)
    running_cot = row_flow - written * ahead
    written_cot = ahead + own_cot * probs + scores_cot * own_pairs
    decay_cot = later_sum(running_cot) - written_cot * jnp.exp(log_decay)
    slot_cot = decay_cot * keep * GATE_SCALE * sigmoid(-slot_pre)
    padded = jnp.concatenate([slot_cot, jnp.zeros((LENGTH, SLOTS), F32)], axis=1).astype(BF16)
    spread_rows(out_ref, rank, seq, 3 * HEAD_DIM, 2 * SLOTS, padded)


def cost(microseconds):
    return pl.CostEstimate(
        flops=int(microseconds * 1.1e9), bytes_accessed=1 << 20, transcendentals=0
    )


def whole(shape):
    zeros = (0,) * len(shape)
    return pl.BlockSpec(shape, lambda seq: zeros)


def one_seq(shape):
    return pl.BlockSpec((1,) + shape, lambda seq: (seq, 0, 0))


TOKENS = RUNS * SEQS * RUN
WIDE = 3 * HEAD_DIM + 2 * SLOTS
RANK_SPEC = pl.BlockSpec(memory_space=pltpu.SMEM)


def mixer_forward(rank, pre, keep):
    return pl.pallas_call(
        mixer_forward_kernel,
        grid=(SEQS,),
        in_specs=[RANK_SPEC, whole((TOKENS, WIDE)), one_seq((LENGTH, 1))],
        out_specs=[
            whole((TOKENS, HEAD_DIM)),
            one_seq((LENGTH, LENGTH)),
            one_seq((LENGTH, SLOTS)),
            one_seq((LENGTH, SLOTS)),
        ],
        out_shape=[
            jax.ShapeDtypeStruct((TOKENS, HEAD_DIM), BF16),
            jax.ShapeDtypeStruct((SEQS, LENGTH, LENGTH), BF16),
            jax.ShapeDtypeStruct((SEQS, LENGTH, SLOTS), F32),
            jax.ShapeDtypeStruct((SEQS, LENGTH, SLOTS), F32),
        ],
        compiler_params=pltpu.CompilerParams(
            vmem_limit_bytes=48 * 1024 * 1024, dimension_semantics=("arbitrary",)
        ),
        cost_estimate=cost(5),
        name="mixer_forward",
    )(rank, pre, keep)


def mixer_backward(rank, pre, keep, mixing, probs, past, cot):
    return pl.pallas_call(
        mixer_backward_kernel,
        grid=(SEQS,),
        in_specs=[
            RANK_SPEC,
            whole((TOKENS, WIDE)),
            one_seq((LENGTH, 1)),
            one_seq((LENGTH, LENGTH)),
            one_seq((LENGTH, SLOTS)),
            one_seq((LENGTH, SLOTS)),
            whole((TOKENS, HEAD_DIM)),
        ],
        out_specs=whole((TOKENS, WIDE)),
        out_shape=jax.ShapeDtypeStruct((TOKENS, WIDE), BF16),
        compiler_params=pltpu.CompilerParams(
            vmem_limit_bytes=48 * 1024 * 1024, dimension_semantics=("arbitrary",)
        ),
        cost_estimate=cost(10),
        name="mixer_backward",
    )(rank, pre, keep, mixing, probs, past, cot)


EPS = 1e-05
WIDTH = 2048
K_TILE = 512
ALL_SLOTS = 4 * SLOTS
ROWS_OWN = SEQS * RUN
TILE = 256
TILES = 3
HIDDEN = TILE * TILES


def project_kernel(
    rank_ref, own_ref, near_ref, far_ref, farthest_ref, gain_ref,
    query_ref, key_ref, value_ref, slot_ref, pre_ref, normed_ref, slots_ref,
):
    step = pl.program_id(0)

    @pl.when(step == 0)
    def _():
        for i, ref in enumerate((own_ref, near_ref, far_ref, farthest_ref)):
            rows = ref[...].astype(F32)
            root = lax.rsqrt(jnp.mean(rows * rows, axis=1, keepdims=True) + EPS)
            normed_ref[i * ROWS_OWN : (i + 1) * ROWS_OWN] = (rows * root * gain_ref[...]).astype(
                BF16
            )
        pre_ref[...] = jnp.zeros_like(pre_ref)
        slots_ref[...] = jnp.zeros_like(slots_ref)

    left = normed_ref[:, pl.ds(pl.multiple_of(step * K_TILE, K_TILE), K_TILE)]
    for i, ref in enumerate((query_ref, key_ref, value_ref)):
        pre_ref[:, i * HEAD_DIM : (i + 1) * HEAD_DIM] += mm(left, ref[...])
    slots_ref[...] += mm(left, slot_ref[...])

    @pl.when(step == WIDTH // K_TILE - 1)
    def _():
        mine = jnp.zeros((TOKENS, SLOTS), F32)
        for head in range(4):
            mine = jnp.where(
                rank_ref[0] == head, slots_ref[:, head * SLOTS : (head + 1) * SLOTS], mine
            )
        pre_ref[:, 3 * HEAD_DIM :] = jnp.concatenate([mine, jnp.zeros_like(mine)], axis=1)


def project(rank, pieces, gain, query_weight, key_weight, value_weight, slot_weight):
    piece = pl.BlockSpec((ROWS_OWN, WIDTH), lambda k, rank: (0, 0))
    weight = pl.BlockSpec((K_TILE, HEAD_DIM), lambda k, rank: (k, rank[0]))
    return pl.pallas_call(
        project_kernel,
        grid_spec=pltpu.PrefetchScalarGridSpec(
            num_scalar_prefetch=1,
            grid=(WIDTH // K_TILE,),
            in_specs=[piece] * 4
            + [
                pl.BlockSpec((1, WIDTH), lambda k, rank: (0, 0)),
                weight,
                weight,
                weight,
                pl.BlockSpec((K_TILE, ALL_SLOTS), lambda k, rank: (k, 0)),
            ],
            out_specs=[
                pl.BlockSpec((TOKENS, WIDE), lambda k, rank: (0, 0)),
                pl.BlockSpec((TOKENS, WIDTH), lambda k, rank: (0, 0)),
            ],
            scratch_shapes=[pltpu.VMEM((TOKENS, ALL_SLOTS), F32)],
        ),
        out_shape=[
            jax.ShapeDtypeStruct((TOKENS, WIDE), F32),
            jax.ShapeDtypeStruct((TOKENS, WIDTH), BF16),
        ],
        compiler_params=pltpu.CompilerParams(
            vmem_limit_bytes=48 * 1024 * 1024, dimension_semantics=("arbitrary",)
        ),
        cost_estimate=cost(10),
        name="project",
    )(rank, *pieces, gain, query_weight, key_weight, value_weight, slot_weight)


def unproject_kernel(
    rank_ref, cots_ref, normed_ref, query_ref, key_ref, value_ref, slot_ref,
    own_ref, near_ref, far_ref, farthest_ref, gain_ref,
):
    total = mm_cols(cots_ref[:, :HEAD_DIM], query_ref[...])
    total += mm_cols(cots_ref[:, HEAD_DIM : 2 * HEAD_DIM], key_ref[...])
    total += mm_cols(cots_ref[:, 2 * HEAD_DIM : 3 * HEAD_DIM], value_ref[...])
    slots = cots_ref[:, 3 * HEAD_DIM : 3 * HEAD_DIM + SLOTS]
    spread = jnp.concatenate(
        [jnp.where(rank_ref[0] == head, slots, jnp.zeros_like(slots)) for head in range(4)],
        axis=1,
    )
    total += mm_cols(spread, slot_ref[...])
    for i, ref in enumerate((own_ref, near_ref, far_ref, farthest_ref)):
        ref[...] = total[i * ROWS_OWN : (i + 1) * ROWS_OWN].astype(BF16)
    gain_ref[...] = jnp.sum(total * normed_ref[...].astype(F32), axis=0, keepdims=True)


def unproject(rank, cots, normed, query_weight, key_weight, value_weight, slot_weight):
    weight = pl.BlockSpec((K_TILE, HEAD_DIM), lambda k, rank: (k, rank[0]))
    rows = pl.BlockSpec((ROWS_OWN, K_TILE), lambda k, rank: (0, k))
    return pl.pallas_call(
        unproject_kernel,
        grid_spec=pltpu.PrefetchScalarGridSpec(
            num_scalar_prefetch=1,
            grid=(WIDTH // K_TILE,),
            in_specs=[
                pl.BlockSpec((TOKENS, WIDE), lambda k, rank: (0, 0)),
                pl.BlockSpec((TOKENS, K_TILE), lambda k, rank: (0, k)),
                weight,
                weight,
                weight,
                pl.BlockSpec((K_TILE, ALL_SLOTS), lambda k, rank: (k, 0)),
            ],
            out_specs=[rows] * 4 + [pl.BlockSpec((1, K_TILE), lambda k, rank: (0, k))],
        ),
        out_shape=[jax.ShapeDtypeStruct((ROWS_OWN, WIDTH), BF16)] * 4
        + [jax.ShapeDtypeStruct((1, WIDTH), F32)],
        compiler_params=pltpu.CompilerParams(
            vmem_limit_bytes=48 * 1024 * 1024, dimension_semantics=("arbitrary",)
        ),
        cost_estimate=cost(7),
        name="unproject",
    )(rank, cots, normed, query_weight, key_weight, value_weight, slot_weight)


def fill(rows_ref, piece_refs):
    start = 0
    for ref in piece_refs:
        rows_ref[start : start + ref.shape[0]] = ref[...]
        start += ref.shape[0]


def ffn_kernel(count, *refs):
    pair_ref, down_ref, inner_ref, cots_ref, rows_ref, cot_ref = refs[2 * count :]

    @pl.when(pl.program_id(0) == 0)
    def _():
        fill(rows_ref, refs[:count])
        fill(cot_ref, refs[count : 2 * count])

    for half in range(2):
        rows = slice(half * TOKENS, (half + 1) * TOKENS)
        both = mm(rows_ref[rows], pair_ref[...])
        gate_pre, up_pre = both[:, :TILE], both[:, TILE:]
        inner_cot = mm(cot_ref[rows], down_ref[...])
        sigma = sigmoid(gate_pre)
        gate_act = gate_pre * sigma
        inner_ref[rows] = (gate_act * up_pre).astype(BF16)
        slope = sigma * (1.0 + gate_pre * (1.0 - sigma))
        cots_ref[rows, :TILE] = (inner_cot * up_pre * slope).astype(BF16)
        cots_ref[rows, TILE:] = (inner_cot * gate_act).astype(BF16)


def ffn(pieces, cot_pieces, weights):
    def fixed(rows):
        return pl.BlockSpec((rows, WIDTH), lambda n: (0, 0))

    both = 2 * TOKENS
    return pl.pallas_call(
        functools.partial(ffn_kernel, len(pieces)),
        grid=(TILES,),
        in_specs=[fixed(piece.shape[0]) for piece in pieces + cot_pieces]
        + [
            pl.BlockSpec((WIDTH, 2 * TILE), lambda n: (0, n)),
            pl.BlockSpec((WIDTH, TILE), lambda n: (0, 2 * TILES + n)),
        ],
        out_specs=[
            pl.BlockSpec((both, TILE), lambda n: (0, n)),
            pl.BlockSpec((both, 2 * TILE), lambda n: (0, n)),
        ],
        out_shape=[
            jax.ShapeDtypeStruct((both, HIDDEN), BF16),
            jax.ShapeDtypeStruct((both, 2 * HIDDEN), BF16),
        ],
        scratch_shapes=[pltpu.VMEM((both, WIDTH), BF16)] * 2,
        compiler_params=pltpu.CompilerParams(
            vmem_limit_bytes=56 * 1024 * 1024, dimension_semantics=("arbitrary",)
        ),
        cost_estimate=cost(16),
        name="ffn",
    )(*pieces, *cot_pieces, weights, weights)


PAIRED = 2 * HIDDEN
ALL_HIDDEN = 3 * HIDDEN
GRAD_ROWS = 256
COLUMNS = HEAD_DIM + WIDE
CHUNK = 64
BLOCK_ROWS = WIDTH // 4


def ffn_grads_kernel(count, *refs):
    cots_ref, inner_ref, out_ref = refs[2 * count :]
    rows = jnp.concatenate([ref[...] for ref in refs[:count]], axis=0)
    out_ref[:, :PAIRED] = mm_rows(rows, cots_ref[...]).astype(BF16)
    cot = jnp.concatenate([ref[...] for ref in refs[count : 2 * count]], axis=0)
    out_ref[:, PAIRED:] = mm_rows(cot, inner_ref[...]).astype(BF16)


def ffn_grads(pieces, cot_pieces, cots, inner):
    both = cots.shape[0]
    return pl.pallas_call(
        functools.partial(ffn_grads_kernel, len(pieces)),
        grid=(WIDTH // GRAD_ROWS,),
        in_specs=[
            pl.BlockSpec((piece.shape[0], GRAD_ROWS), lambda n: (0, n))
            for piece in pieces + cot_pieces
        ]
        + [
            pl.BlockSpec((both, PAIRED), lambda n: (0, 0)),
            pl.BlockSpec((both, HIDDEN), lambda n: (0, 0)),
        ],
        out_specs=pl.BlockSpec((GRAD_ROWS, ALL_HIDDEN), lambda n: (n, 0)),
        out_shape=jax.ShapeDtypeStruct((WIDTH, ALL_HIDDEN), BF16),
        compiler_params=pltpu.CompilerParams(
            vmem_limit_bytes=56 * 1024 * 1024, dimension_semantics=("arbitrary",)
        ),
        cost_estimate=cost(16),
        name="ffn_grads",
    )(*pieces, *cot_pieces, cots, inner)


def mixer_grads_kernel(*refs):
    _, normed_ref, cots_ref, *mixed_refs, branch_ref, out_ref, block_ref = refs
    block_ref[:, :WIDE] = mm_rows(normed_ref[...], cots_ref[...]).astype(BF16)
    mixed = jnp.concatenate([ref[...] for ref in mixed_refs], axis=0)
    block_ref[:, WIDE:] = mm_rows(mixed, branch_ref[...]).astype(BF16)
    for side in range(2):
        for z in range(4):
            source = (side * 4 + z) * CHUNK
            target = (z * 2 + side) * CHUNK
            out_ref[target : target + CHUNK] = block_ref[source : source + CHUNK]


def mixer_grads(place, normed, cots, mixed, branch):
    return pl.pallas_call(
        mixer_grads_kernel,
        grid_spec=pltpu.PrefetchScalarGridSpec(
            num_scalar_prefetch=1,
            grid=(4,),
            in_specs=[
                pl.BlockSpec((TOKENS, BLOCK_ROWS), lambda y, place: (0, y)),
                pl.BlockSpec((TOKENS, WIDE), lambda y, place: (0, 0)),
            ]
            + [pl.BlockSpec((ROWS_OWN, BLOCK_ROWS), lambda y, place: (0, y))] * 4
            + [pl.BlockSpec((TOKENS, HEAD_DIM), lambda y, place: (0, place[0]))],
            out_specs=pl.BlockSpec((BLOCK_ROWS, COLUMNS), lambda y, place: (y, 0)),
            scratch_shapes=[pltpu.VMEM((BLOCK_ROWS, COLUMNS), BF16)],
        ),
        out_shape=jax.ShapeDtypeStruct((WIDTH, COLUMNS), BF16),
        compiler_params=pltpu.CompilerParams(
            vmem_limit_bytes=56 * 1024 * 1024, dimension_semantics=("arbitrary",)
        ),
        cost_estimate=cost(12),
        name="mixer_grads",
    )(place, normed, cots, *mixed, branch)


def to_plane(value):
    parts = []
    for y in range(4):
        for z in range(4):
            for side in range(2):
                start = y * 8 * CHUNK + side * 4 * CHUNK + z * CHUNK
                parts.append(value[:, start : start + CHUNK])
    return jnp.concatenate(parts, axis=1)


def from_plane(value):
    parts = []
    for y in range(4):
        for side in range(2):
            for z in range(4):
                start = y * 8 * CHUNK + z * 2 * CHUNK + side * CHUNK
                parts.append(value[:, start : start + CHUNK])
    return jnp.concatenate(parts, axis=1)


def rms_parts(rows):
    root = lax.rsqrt(jnp.mean(rows * rows, axis=1, keepdims=True) + EPS)
    return rows * root, root


def rms_back(incoming, gain, unit, root):
    scaled = incoming * gain
    return root * (scaled - unit * jnp.mean(scaled * unit, axis=1, keepdims=True))


def mix_out_kernel(rank_ref, *refs):
    part_refs = refs[:4]
    weight_ref, input_ref, keep_ref, gain_ref, hidden_ref, ffn_in_ref, mixed_ref = refs[4:]
    step = pl.program_id(0)
    for k in range(4):

        @pl.when(step == k)
        def _():
            part = part_refs[k][...]
            place = pl.multiple_of((rank_ref[0] ^ k) * HEAD_DIM, HEAD_DIM)
            mixed_ref[:, pl.ds(place, HEAD_DIM)] = part
            product = mm(part, weight_ref[...])
            hidden_ref[...] = product if k == 0 else hidden_ref[...] + product

    @pl.when(step == 3)
    def _():
        hidden = input_ref[...].astype(F32) + keep_ref[...] * hidden_ref[...]
        hidden_ref[...] = hidden
        ffn_in_ref[...] = to_plane((rms_parts(hidden)[0] * gain_ref[...]).astype(BF16))


def mix_out(rank, parts, out_weight, block_input, keep, gain):
    def fixed(shape):
        return pl.BlockSpec(shape, lambda k, rank: (0, 0))

    own = (ROWS_OWN, WIDTH)
    return pl.pallas_call(
        mix_out_kernel,
        grid_spec=pltpu.PrefetchScalarGridSpec(
            num_scalar_prefetch=1,
            grid=(4,),
            in_specs=[fixed((ROWS_OWN, HEAD_DIM))] * 4
            + [
                pl.BlockSpec((HEAD_DIM, WIDTH), lambda k, rank: (rank[0] ^ k, 0)),
                fixed(own),
                fixed((ROWS_OWN, 1)),
                fixed((1, WIDTH)),
            ],
            out_specs=[fixed(own)] * 3,
        ),
        out_shape=[
            jax.ShapeDtypeStruct(own, F32),
            jax.ShapeDtypeStruct(own, BF16),
            jax.ShapeDtypeStruct(own, BF16),
        ],
        compiler_params=pltpu.CompilerParams(
            vmem_limit_bytes=48 * 1024 * 1024, dimension_semantics=("arbitrary",)
        ),
        cost_estimate=cost(6),
        name="mix_out",
    )(rank, *parts, out_weight, block_input, keep, gain)


def norm_back_kernel(
    own_ref, left_ref, right_ref, cot_ref, hidden_ref, keep_ref, gain_ref,
    hidden_cot_ref, branch_ref, gain_cot_ref,
):
    incoming = own_ref[...] + left_ref[...].astype(F32) + right_ref[...].astype(F32)
    incoming = from_plane(incoming)
    unit, root = rms_parts(hidden_ref[...])
    hidden_cot = cot_ref[...].astype(F32) + rms_back(incoming, gain_ref[...], unit, root)
    hidden_cot_ref[...] = hidden_cot
    branch_ref[...] = (keep_ref[...] * hidden_cot).astype(BF16)
    gain_cot_ref[...] = jnp.sum(incoming * unit, axis=0, keepdims=True)


def block_out_kernel(own_ref, left_ref, right_ref, hidden_ref, keep_ref, out_ref):
    down = own_ref[...] + left_ref[...].astype(F32) + right_ref[...].astype(F32)
    out_ref[...] = hidden_ref[...] + keep_ref[...] * from_plane(down)


def input_back_kernel(own_ref, near_ref, far_ref, input_ref, hidden_cot_ref, gain_ref, out_ref):
    incoming = own_ref[...].astype(F32) + near_ref[...].astype(F32) + far_ref[...].astype(F32)
    unit, root = rms_parts(input_ref[...].astype(F32))
    out_ref[...] = hidden_cot_ref[...] + rms_back(incoming, gain_ref[...], unit, root)


def own_rows(kernel, arrays, outs, name):
    def spec(shape):
        return pl.BlockSpec((min(shape[0], ROWS_OWN), shape[1]), lambda i: (0, 0))

    return pl.pallas_call(
        kernel,
        grid=(1,),
        in_specs=[spec(array.shape) for array in arrays],
        out_specs=[spec(shape) for shape, _ in outs],
        out_shape=[jax.ShapeDtypeStruct(shape, dtype) for shape, dtype in outs],
        compiler_params=pltpu.CompilerParams(vmem_limit_bytes=32 * 1024 * 1024),
        cost_estimate=cost(3),
        name=name,
    )(*arrays)


def norm_back(*arrays):
    own = (ROWS_OWN, WIDTH)
    return own_rows(
        norm_back_kernel, arrays, [(own, F32), (own, BF16), ((1, WIDTH), F32)], "norm_back"
    )


def block_out(*arrays):
    return own_rows(block_out_kernel, arrays, [((ROWS_OWN, WIDTH), F32)], "block_out")[0]


def input_back(*arrays):
    return own_rows(input_back_kernel, arrays, [((ROWS_OWN, WIDTH), F32)], "input_back")[0]


AXES = ("y", "xh", "z", "xl", "c")
DP = ("y", "xh", "z")
MP = ("xl", "c")
RING = ("xh", "xl")
PLANE = ("y", "z")
SWAP = ((0, 1), (1, 0))


def to_plane_order(rows):
    count, width = rows.shape
    return rows.reshape(count, 4, 2, 4, width // 32).transpose(0, 1, 3, 2, 4).reshape(count, width)


def after(value, *first):
    return lax.optimization_barrier((value,) + first)[0]


def other_core(value):
    return lax.ppermute(value, "c", SWAP)


def other_chip(value):
    return lax.ppermute(value, "xl", SWAP)


def along_ring(value, step):
    return lax.ppermute(value, RING, [(i, (i + step) % 4) for i in range(4)])


def gather_sides(own):
    return along_ring(own, 1), along_ring(own, -1), other_core(own)


def gather_opposite(left, right):
    half = left.shape[0] // 2
    return along_ring(left[:half], 1), along_ring(right[half:], -1)


def gathered(own, left, right, near, first, second):
    away = [near] + [other_core(value) for value in (left, right, first, second)]
    return [own, left, right, first, second] + away


def ring_fold(near, away):
    near = near.astype(F32) + other_core(away).astype(F32)
    own, left, right, opposite = jnp.split(near, 4, axis=0)
    return near, left, right, opposite.astype(BF16)


def ring_opposite(opposite):
    half = opposite.shape[0] // 2
    return along_ring(opposite[:half], 1), along_ring(opposite[half:], -1)


def ring_sides(left, right, from_left, from_right):
    half = left.shape[0] // 2
    right = jnp.concatenate([right[:half] + from_left.astype(F32), right[half:]], axis=0)
    left = jnp.concatenate([left[:half], left[half:] + from_right.astype(F32)], axis=0)
    return left.astype(BF16), right.astype(BF16)


def ring_send(left, right):
    return along_ring(right, 1), along_ring(left, -1)


def sum_all(value):
    for axis in ("c", "xl", "xh"):
        value = value + lax.ppermute(value, axis, SWAP)
    for axis in PLANE:
        for step in (1, 2):
            value = value + lax.ppermute(value, axis, [(i, i ^ step) for i in range(4)])
    return value


def add(left, right):
    return (left.astype(F32) + right.astype(F32)).astype(BF16)


def on_device(
    block_input,
    cotangent,
    pad_mask,
    seq_counts,
    gain_mix,
    query_weight,
    key_weight,
    value_weight,
    slot_weight,
    out_weight,
    gain_ffn,
    gate_weight,
    up_weight,
    down_weight,
):
    rows_own, width = block_input.shape
    rank = lax.axis_index(MP)
    side = lax.axis_index("xh")
    live = (jnp.arange(SEQS) < seq_counts[0]).astype(jnp.int32)
    keep_seq = (pad_mask[0] * live[:, None]).astype(F32)
    keep_own = lax.dynamic_slice_in_dim(keep_seq, rank * RUN, RUN, 1).reshape(rows_own, 1)

    rank_array = rank.reshape(1).astype(jnp.int32)

    hidden_part = gate_weight.shape[1] // 2
    owned = jnp.stack([gate_weight, up_weight, down_weight.T])
    kept = lax.dynamic_slice_in_dim(owned, side * hidden_part, hidden_part, 2)
    given = lax.dynamic_slice_in_dim(owned, (1 - side) * hidden_part, hidden_part, 2)
    got = lax.ppermute(given, "xh", SWAP)
    far, got = lax.optimization_barrier((other_chip(block_input), got))
    input_pieces = (block_input, other_core(block_input), far, other_core(far))
    paired = jnp.concatenate(
        [jnp.where(side == 0, kept, got), jnp.where(side == 0, got, kept)], axis=1
    )
    paired = jnp.pad(paired, ((0, 0), (0, 0), (0, HIDDEN - hidden_part)))
    paired = paired.reshape(3, 128, TILES, TILE)
    columns = [paired[i, :, n] for n in range(TILES) for i in range(2)]
    columns += [paired[2, :, n] for n in range(TILES)]
    weights = lax.all_gather(jnp.concatenate(columns, axis=1), PLANE, axis=0, tiled=True)

    cot_own = to_plane_order(cotangent)
    cot_start, input_pieces = lax.optimization_barrier(
        (cot_own * keep_own.astype(BF16), input_pieces)
    )
    cot_sides = gather_sides(cot_start)
    mixer_weights = (query_weight, key_weight, value_weight, slot_weight)
    pre, normed_four = project(rank_array, input_pieces, gain_mix[None], *mixer_weights)
    keep_column = keep_seq[:, :, None]
    pre, cot_sides = lax.optimization_barrier((pre, cot_sides))
    cot_ends = gather_opposite(*cot_sides[:2])
    mixed_four, mixing, probs, past = mixer_forward(rank_array, pre, keep_column)
    blocks = jnp.split(mixed_four, 4, axis=0)
    mixed_parts = (
        blocks[0],
        other_core(blocks[1]),
        other_chip(blocks[2]),
        lax.ppermute(blocks[3], MP, [(i, 3 - i) for i in range(4)]),
    )
    hidden, ffn_own, mixed_own = mix_out(
        rank_array, mixed_parts, out_weight, block_input, keep_own, gain_ffn[None]
    )
    hidden, cot_ends = lax.optimization_barrier((hidden, cot_ends))
    cot_pieces = gathered(cot_start, *cot_sides, *cot_ends)
    ffn_own = after(ffn_own, *cot_ends)
    sides = gather_sides(ffn_own)
    ends = gather_opposite(*sides[:2])
    pieces = gathered(ffn_own, *sides, *ends)
    mixed_far = other_chip(after(mixed_own, *ends))
    inner, cots = ffn(pieces, cot_pieces, weights)
    inner, cots, mixed_far = lax.optimization_barrier((inner, cots, mixed_far))
    grads = ffn_grads(pieces, cot_pieces, cots, inner)
    ffn_sums = lax.psum_scatter(grads, PLANE, scatter_dimension=0, tiled=True)
    cots = after(cots, grads)
    pair_weights = weights[:, :PAIRED]
    away = mm_cols(cots[TOKENS:], pair_weights).astype(BF16)
    near = mm_cols(after(cots, away)[:TOKENS], pair_weights).astype(BF16)
    own, left, right, opposite = ring_fold(near, away)
    late_down = mm_cols(after(inner, opposite), weights[:, PAIRED:]).astype(BF16)
    from_left, from_right, late_down = lax.optimization_barrier(
        ring_opposite(opposite) + (late_down,)
    )
    left, right = ring_sides(left, right, from_left, from_right)
    from_left, from_right = ring_send(left, right)
    hidden_cot, branch_cot, gain_ffn_part = norm_back(
        own, from_left, from_right, cotangent, hidden, keep_own, gain_ffn[None]
    )
    branch_far = other_chip(branch_cot)
    branch_four = jnp.concatenate(
        [branch_cot, other_core(branch_cot), branch_far, other_core(branch_far)], axis=0
    )
    out_rows = lax.dynamic_slice_in_dim(out_weight, rank * HEAD_DIM, HEAD_DIM, 0)
    mixed_cot = mm_cols(branch_four, out_rows).astype(BF16)
    head_cots = mixer_backward(rank_array, pre, keep_column, mixing, probs, past, mixed_cot)
    mixed_all = (mixed_own, other_core(mixed_own), mixed_far, other_core(mixed_far))
    mixer_sums = lax.psum_scatter(
        mixer_grads(rank_array, normed_four, head_cots, mixed_all, branch_four),
        PLANE,
        scatter_dimension=0,
        tiled=True,
    )

    own, near, far, farthest, gain_mix_part = unproject(
        rank_array, after(head_cots, mixed_all[3]), normed_four, *mixer_weights
    )
    near = other_core(near)
    far = other_chip(add(far, other_core(farthest)))
    input_grad = input_back(own, near, far, block_input, hidden_cot, gain_mix[None])
    late_down = after(late_down, far)
    late_own, late_left, late_right, late_ends = ring_fold(
        late_down[:TOKENS], late_down[TOKENS:]
    )
    late_sides = ring_send(*ring_sides(late_left, late_right, *ring_opposite(late_ends)))
    block_output = block_out(late_own, *late_sides, hidden, keep_own)
    gain_sums = sum_all(
        jnp.stack([gain_mix_part[0] / gain_mix, gain_ffn_part[0]]).reshape(32, 128)
    ).reshape(2, width)
    kept = lax.dynamic_slice_in_dim(ffn_sums, side * CHUNK, CHUNK, 0)
    given_back = lax.ppermute(
        lax.dynamic_slice_in_dim(ffn_sums, (1 - side) * CHUNK, CHUNK, 0), "xh", SWAP
    )
    mixer_sums, block_output, input_grad, gain_sums, given_back = lax.optimization_barrier(
        (mixer_sums, block_output, input_grad, gain_sums, given_back)
    )
    rows_out = rows_own // 8
    pieces = lax.all_to_all(
        mixer_sums.reshape(8, rows_out, COLUMNS), ("xh", "xl", "c"), 0, 0
    )
    pieces = pieces.astype(F32).reshape(2, 4, rows_out, COLUMNS).sum(0).transpose(1, 0, 2)

    def columns(start, count):
        return pieces[:, :, start : start + count].reshape(rows_out, 4 * count)

    def finish(tiles):
        mine, theirs = [
            jnp.concatenate([grads[:, n * TILE : (n + 1) * TILE] for n in tiles], axis=1)[
                :, :hidden_part
            ]
            for grads in (kept, given_back)
        ]
        return jnp.concatenate(
            [jnp.where(side == 0, mine, theirs), jnp.where(side == 0, theirs, mine)], axis=1
        ).astype(F32)

    return (
        block_output,
        input_grad,
        gain_sums[0],
        columns(0, HEAD_DIM),
        columns(HEAD_DIM, HEAD_DIM),
        columns(2 * HEAD_DIM, HEAD_DIM),
        columns(3 * HEAD_DIM, SLOTS),
        columns(WIDE, HEAD_DIM),
        gain_sums[1],
        finish((0, 2, 4)),
        finish((1, 3, 5)),
        finish((6, 7, 8)).T,
    )


def solution(mesh):
    fine = jax.sharding.Mesh(mesh.devices.reshape(4, 2, 4, 2, 2), AXES)
    rows = P(AXES, None)
    return jax.shard_map(
        on_device,
        mesh=fine,
        in_specs=(
            rows,
            rows,
            P(DP, None, None),
            P(DP),
            P(),
            P(),
            P(),
            P(),
            P(),
            P(),
            P(),
            P(DP, MP),
            P(DP, MP),
            P(MP, DP),
        ),
        out_specs=(
            rows,
            rows,
            P(),
            rows,
            rows,
            rows,
            rows,
            rows,
            P(),
            P(DP, MP),
            P(DP, MP),
            P(MP, DP),
        ),
        check_vma=False,
    )
```

```python
import functools

import jax
import jax.numpy as jnp
from jax import lax
from jax.experimental import pallas as pl
from jax.experimental.pallas import tpu as pltpu
from jax.sharding import PartitionSpec as P

HEAD_DIM = 512
SLOTS = 64
LENGTH = 256
RUN = 64
RUNS = 4
SEQS = 2
LEVELS = (128, 64, 32, 16, 8, 4, 2, 1)
SCALE = HEAD_DIM ** (-0.5)
GATE_SCALE = 0.125
F32 = jnp.float32
BF16 = jnp.bfloat16


def mm(left, right):
    return jnp.dot(left, right, preferred_element_type=F32)


def mm_cols(left, right):
    return lax.dot_general(left, right, (((1,), (1,)), ((), ())), preferred_element_type=F32)


def mm_rows(left, right):
    return lax.dot_general(left, right, (((0,), (0,)), ((), ())), preferred_element_type=F32)


def halves(value):
    high = value.astype(BF16)
    return high, (value - high.astype(F32)).astype(BF16)


def fine_product(left, right):
    left_high, left_low = halves(left)
    right_high, right_low = halves(right)
    rows, width = left.shape[0], right.shape[1]
    out = mm(
        jnp.concatenate([left_high, left_low], axis=0),
        jnp.concatenate([right_high, right_low], axis=1),
    )
    return out[:rows, :width] + out[:rows, width:] + out[rows:, :width]


def fine_cols_product(left, right):
    left_high, left_low = halves(left)
    right_high, right_low = halves(right)
    return mm_cols(
        jnp.concatenate([left_high, left_low, left_high], axis=1),
        jnp.concatenate([right_high, right_high, right_low], axis=1),
    )


def decay_tables(slot_pre, keep):
    log_gate = jnp.minimum(slot_pre, 0.0) - jnp.log1p(jnp.exp(-jnp.abs(slot_pre)))
    log_decay = keep * log_gate * GATE_SCALE
    half = jnp.tanh(-0.5 * log_decay)
    written = 2.0 * half / (1.0 + half)
    rows = lax.broadcasted_iota(jnp.int32, log_decay.shape, 0)
    running = log_decay
    shift = 1
    while shift < LENGTH:
        running = running + jnp.where(rows >= shift, pltpu.roll(running, shift, 0), 0.0)
        shift *= 2
    return log_decay, written, running


def later_sum(value):
    rows = lax.broadcasted_iota(jnp.int32, value.shape, 0)
    shift = 1
    while shift < LENGTH:
        value = value + jnp.where(rows < LENGTH - shift, pltpu.roll(value, LENGTH - shift, 0), 0.0)
        shift *= 2
    return value


def level_factors(running):
    rows = lax.broadcasted_iota(jnp.int32, running.shape, 0)
    last = running
    factors = {}
    size = 1
    while size < LENGTH:
        odd = (rows & size) != 0
        before = pltpu.roll(last, size, 0)
        factor = jnp.exp(jnp.where(odd, running - before, last - running))
        factors[size] = (jnp.where(odd, factor, 0.0), jnp.where(odd, 0.0, factor))
        last = jnp.where(odd, last, pltpu.roll(last, LENGTH - size, 0))
        size *= 2
    return factors


def level_map(flip):
    rows = lax.broadcasted_iota(jnp.int32, (LENGTH, LENGTH), 0)
    cols = lax.broadcasted_iota(jnp.int32, (LENGTH, LENGTH), 1)
    later = rows < cols if flip else rows > cols
    return jnp.where(later, rows ^ cols, 0), rows == cols


def at_level(where_map, size):
    return (where_map >= size) & (where_map < 2 * size)


def gather_rows(ref, rank, seq, start, width):
    parts = []
    for run in range(RUNS):
        first = pl.multiple_of(((rank ^ run) * SEQS + seq) * RUN, RUN)
        parts.append(ref[pl.ds(first, RUN), start : start + width])
    return jnp.concatenate(parts, axis=0)


def spread_rows(ref, rank, seq, start, width, value):
    for run in range(RUNS):
        first = pl.multiple_of(((rank ^ run) * SEQS + seq) * RUN, RUN)
        ref[pl.ds(first, RUN), start : start + width] = value[run * RUN : (run + 1) * RUN]


def sigmoid(value):
    return 1.0 / (1.0 + jnp.exp(-value))


def silu(value):
    return value * sigmoid(value)


def silu_slope(pre):
    sigma = sigmoid(pre)
    return sigma * (1.0 + pre * (1.0 - sigma))


def mix_forward(rank, seq, pre_ref, keep, mixed_ref, mixing_ref, probs_ref, past_ref):
    queries = silu(gather_rows(pre_ref, rank, seq, 0, HEAD_DIM)).astype(BF16)
    keys = silu(gather_rows(pre_ref, rank, seq, HEAD_DIM, HEAD_DIM)).astype(BF16)
    values = gather_rows(pre_ref, rank, seq, 2 * HEAD_DIM, HEAD_DIM).astype(BF16)
    slot_pre = gather_rows(pre_ref, rank, seq, 3 * HEAD_DIM, SLOTS)
    _, written, running = decay_tables(slot_pre, keep)
    factors = level_factors(running)
    where_map, own = level_map(False)
    pairs = mm_cols(queries, keys)
    own_pairs = jnp.sum(jnp.where(own, pairs, 0.0), axis=1, keepdims=True)
    past = jnp.zeros((LENGTH, SLOTS), F32)
    for size in LEVELS:
        after, before = factors[size]
        past = past + after * fine_product(
            jnp.where(at_level(where_map, size), pairs, 0.0), before * written
        )
    past = SCALE * past
    scores = past + SCALE * own_pairs * written
    grown = jnp.exp(scores - jnp.max(scores, axis=1, keepdims=True))
    probs = grown / jnp.sum(grown, axis=1, keepdims=True)
    mixing = jnp.where(own, jnp.sum(probs * written, axis=1, keepdims=True), 0.0)
    for size in LEVELS:
        after, before = factors[size]
        mixing = jnp.where(
            at_level(where_map, size),
            fine_cols_product(probs * after, before * written),
            mixing,
        )
    mixing = mixing.astype(BF16)
    mixed = mm(mixing, values).astype(BF16)
    spread_rows(mixed_ref, rank, seq, 0, HEAD_DIM, mixed)
    mixing_ref[seq] = mixing
    probs_ref[seq] = probs
    past_ref[seq] = past


def mixer_backward_kernel(
    rank_ref, pre_ref, keep_ref, mixing_ref, probs_ref, past_ref, weight_ref,
    own_ref, near_ref, far_ref, farthest_ref, out_ref, cot_ref,
):
    rank = rank_ref[0]
    seq = pl.program_id(0)

    @pl.when(seq == 0)
    def _():
        branch = [ref[...] for ref in (own_ref, near_ref, far_ref, farthest_ref)]
        cot_ref[...] = mm_cols(jnp.concatenate(branch, axis=0), weight_ref[...]).astype(BF16)

    query_pre = gather_rows(pre_ref, rank, seq, 0, HEAD_DIM)
    key_pre = gather_rows(pre_ref, rank, seq, HEAD_DIM, HEAD_DIM)
    queries = silu(query_pre).astype(BF16)
    keys = silu(key_pre).astype(BF16)
    values = gather_rows(pre_ref, rank, seq, 2 * HEAD_DIM, HEAD_DIM).astype(BF16)
    slot_pre = gather_rows(pre_ref, rank, seq, 3 * HEAD_DIM, SLOTS)
    cot = gather_rows(cot_ref, rank, seq, 0, HEAD_DIM)
    keep = keep_ref[0]
    log_decay, written, running = decay_tables(slot_pre, keep)
    factors = level_factors(running)
    where_map, own = level_map(False)
    where_flip, _ = level_map(True)
    probs = probs_ref[0]
    past = past_ref[0]
    mixing = mixing_ref[0]
    spread_rows(
        out_ref, rank, seq, 2 * HEAD_DIM, HEAD_DIM, mm_rows(mixing, cot).astype(BF16)
    )
    pairs_flip = mm_cols(keys, queries) * SCALE
    cot_flip = mm_cols(values, cot)
    mixing_cot = mm_cols(cot, values)
    own_cot = jnp.sum(jnp.where(own, mixing_cot, 0.0), axis=1, keepdims=True)
    own_pairs = jnp.sum(jnp.where(own, pairs_flip, 0.0), axis=1, keepdims=True)
    past_cot = jnp.zeros((LENGTH, SLOTS), F32)
    for size in LEVELS:
        after, before = factors[size]
        past_cot = past_cot + after * fine_product(
            jnp.where(at_level(where_map, size), mixing_cot, 0.0), before * written
        )
    probs_cot = past_cot + own_cot * written
    scores_cot = probs * (probs_cot - jnp.sum(probs * probs_cot, axis=1, keepdims=True))
    row_flow = probs * past_cot + scores_cot * past
    pairs_cot = jnp.where(own, jnp.sum(scores_cot * written, axis=1, keepdims=True), 0.0)
    ahead = jnp.zeros((LENGTH, SLOTS), F32)
    both_flip = jnp.concatenate([cot_flip, pairs_flip], axis=1)
    where_both = jnp.concatenate([where_flip, where_flip], axis=1)
    for size in LEVELS:
        after, before = factors[size]
        pairs_cot = jnp.where(
            at_level(where_map, size),
            fine_cols_product(scores_cot * after, before * written),
            pairs_cot,
        )
        ahead = ahead + before * fine_product(
            jnp.where(at_level(where_both, size), both_flip, 0.0),
            jnp.concatenate([probs * after, scores_cot * after], axis=0),
        )
    pairs_low = (SCALE * pairs_cot).astype(BF16)
    query_cot = (mm(pairs_low, keys) * silu_slope(query_pre)).astype(BF16)
    spread_rows(out_ref, rank, seq, 0, HEAD_DIM, query_cot)
    key_cot = (mm_rows(pairs_low, queries) * silu_slope(key_pre)).astype(BF16)
    spread_rows(out_ref, rank, seq, HEAD_DIM, HEAD_DIM, key_cot)
    running_cot = row_flow - written * ahead
    written_cot = ahead + own_cot * probs + scores_cot * own_pairs
    decay_cot = later_sum(running_cot) - written_cot * jnp.exp(log_decay)
    slot_cot = decay_cot * keep * GATE_SCALE * sigmoid(-slot_pre)
    padded = jnp.concatenate([slot_cot, jnp.zeros((LENGTH, SLOTS), F32)], axis=1).astype(BF16)
    spread_rows(out_ref, rank, seq, 3 * HEAD_DIM, 2 * SLOTS, padded)


def cost(microseconds):
    return pl.CostEstimate(
        flops=int(microseconds * 1.1e9), bytes_accessed=1 << 20, transcendentals=0
    )


def whole(shape):
    zeros = (0,) * len(shape)
    return pl.BlockSpec(shape, lambda seq, rank: zeros)


def one_seq(shape):
    return pl.BlockSpec((1,) + shape, lambda seq, rank: (seq, 0, 0))


TOKENS = RUNS * SEQS * RUN
WIDE = 3 * HEAD_DIM + 2 * SLOTS
WIDTH = 2048
ROWS_OWN = SEQS * RUN
RANK_SPEC = pl.BlockSpec(memory_space=pltpu.SMEM)


def mixer_backward(rank, pre, keep, mixing, probs, past, out_weight, branch):
    return pl.pallas_call(
        mixer_backward_kernel,
        grid_spec=pltpu.PrefetchScalarGridSpec(
            num_scalar_prefetch=1,
            grid=(SEQS,),
            in_specs=[
                whole((TOKENS, WIDE)),
                one_seq((LENGTH, 1)),
                one_seq((LENGTH, LENGTH)),
                one_seq((LENGTH, SLOTS)),
                one_seq((LENGTH, SLOTS)),
                pl.BlockSpec((HEAD_DIM, WIDTH), lambda seq, rank: (rank[0], 0)),
            ]
            + [whole((ROWS_OWN, WIDTH))] * 4,
            out_specs=whole((TOKENS, WIDE)),
            scratch_shapes=[pltpu.VMEM((TOKENS, HEAD_DIM), BF16)],
        ),
        out_shape=jax.ShapeDtypeStruct((TOKENS, WIDE), BF16),
        compiler_params=pltpu.CompilerParams(
            vmem_limit_bytes=48 * 1024 * 1024, dimension_semantics=("arbitrary",)
        ),
        cost_estimate=cost(13),
        name="mixer_backward",
    )(rank, pre, keep, mixing, probs, past, out_weight, *branch)


EPS = 1e-05
K_TILE = 512
ALL_SLOTS = 4 * SLOTS
TILE = 256
TILES = 3
HIDDEN = TILE * TILES


def project_step(step, rank, row_refs, gain, weight_refs, slot_ref, pre_ref, normed_ref, slots_ref, first):
    last = first + 2 * ROWS_OWN

    @pl.when(step == 0)
    def _():
        for i, ref in enumerate(row_refs):
            rows = ref[...].astype(F32)
            root = lax.rsqrt(jnp.mean(rows * rows, axis=1, keepdims=True) + EPS)
            start = first + i * ROWS_OWN
            normed_ref[start : start + ROWS_OWN] = (rows * root * gain).astype(BF16)
        pre_ref[first:last] = jnp.zeros((2 * ROWS_OWN, WIDE), F32)
        slots_ref[...] = jnp.zeros_like(slots_ref)

    left = normed_ref[first:last, pl.ds(pl.multiple_of(step * K_TILE, K_TILE), K_TILE)]
    for i, ref in enumerate(weight_refs):
        pre_ref[first:last, i * HEAD_DIM : (i + 1) * HEAD_DIM] += mm(left, ref[...])
    slots_ref[...] += mm(left, slot_ref[...])

    @pl.when(step == WIDTH // K_TILE - 1)
    def _():
        mine = jnp.zeros((2 * ROWS_OWN, SLOTS), F32)
        for head in range(4):
            mine = jnp.where(rank == head, slots_ref[:, head * SLOTS : (head + 1) * SLOTS], mine)
        pre_ref[first:last, 3 * HEAD_DIM :] = jnp.concatenate([mine, jnp.zeros_like(mine)], axis=1)


def project_near_kernel(
    rank_ref, own_ref, near_ref, gain_ref, query_ref, key_ref, value_ref, slot_ref,
    pre_ref, normed_ref, done_ref, slots_ref,
):
    step = pl.program_id(0)
    project_step(
        step, rank_ref[0], (own_ref, near_ref), gain_ref[...], (query_ref, key_ref, value_ref),
        slot_ref, pre_ref, normed_ref, slots_ref, 0,
    )
    done_ref[...] = jnp.zeros_like(done_ref)


def project_mix_kernel(
    rank_ref, far_ref, farthest_ref, gain_ref, query_ref, key_ref, value_ref, slot_ref,
    near_pre_ref, near_normed_ref, keep_ref,
    pre_ref, normed_ref, first_ref, second_ref, third_ref, fourth_ref,
    mixing_ref, probs_ref, past_ref, slots_ref, mixed_ref,
):
    step = pl.program_id(0)
    half = 2 * ROWS_OWN

    @pl.when(step == 0)
    def _():
        pre_ref[:half] = near_pre_ref[...]
        normed_ref[:half] = near_normed_ref[...]

    project_step(
        step, rank_ref[0], (far_ref, farthest_ref), gain_ref[...], (query_ref, key_ref, value_ref),
        slot_ref, pre_ref, normed_ref, slots_ref, half,
    )

    @pl.when(step == WIDTH // K_TILE - 1)
    def _():
        for seq in range(SEQS):
            mix_forward(
                rank_ref[0], seq, pre_ref, keep_ref[seq], mixed_ref, mixing_ref, probs_ref, past_ref
            )
        for i, ref in enumerate((first_ref, second_ref, third_ref, fourth_ref)):
            ref[...] = mixed_ref[i * ROWS_OWN : (i + 1) * ROWS_OWN]


def project(kernel, rank, pieces, gain, weights, extra, outs, scratch, micros, name):
    def fixed(shape):
        zeros = (0,) * len(shape)
        return pl.BlockSpec(shape, lambda k, rank: zeros)

    weight = pl.BlockSpec((K_TILE, HEAD_DIM), lambda k, rank: (k, rank[0]))
    return pl.pallas_call(
        kernel,
        grid_spec=pltpu.PrefetchScalarGridSpec(
            num_scalar_prefetch=1,
            grid=(WIDTH // K_TILE,),
            in_specs=[fixed(piece.shape) for piece in pieces]
            + [fixed((1, WIDTH)), weight, weight, weight]
            + [pl.BlockSpec((K_TILE, ALL_SLOTS), lambda k, rank: (k, 0))]
            + [fixed(array.shape) for array in extra],
            out_specs=[fixed(shape) for shape, _ in outs],
            scratch_shapes=[pltpu.VMEM((2 * ROWS_OWN, ALL_SLOTS), F32)] + scratch,
        ),
        out_shape=[jax.ShapeDtypeStruct(shape, dtype) for shape, dtype in outs],
        compiler_params=pltpu.CompilerParams(
            vmem_limit_bytes=48 * 1024 * 1024, dimension_semantics=("arbitrary",)
        ),
        cost_estimate=cost(micros),
        name=name,
    )(rank, *pieces, gain, *weights, *extra)


def project_near(rank, pieces, gain, weights):
    half = 2 * ROWS_OWN
    outs = [((half, WIDE), F32), ((half, WIDTH), BF16), ((8, 128), F32)]
    return project(
        project_near_kernel, rank, pieces, gain, weights, (), outs, [], 7, "project_near"
    )


def project_mix(rank, pieces, gain, weights, near_pre, near_normed, keep):
    outs = [((TOKENS, WIDE), F32), ((TOKENS, WIDTH), BF16)]
    outs += [((ROWS_OWN, HEAD_DIM), BF16)] * 4 + [((SEQS, LENGTH, LENGTH), BF16)]
    outs += [((SEQS, LENGTH, SLOTS), F32)] * 2
    return project(
        project_mix_kernel, rank, pieces, gain, weights, (near_pre, near_normed, keep), outs,
        [pltpu.VMEM((TOKENS, HEAD_DIM), BF16)], 13, "project_mix",
    )


def unproject_kernel(
    rank_ref, cots_ref, normed_ref, query_ref, key_ref, value_ref, slot_ref,
    own_ref, near_ref, far_ref, farthest_ref, gain_ref,
):
    total = mm_cols(cots_ref[:, :HEAD_DIM], query_ref[...])
    total += mm_cols(cots_ref[:, HEAD_DIM : 2 * HEAD_DIM], key_ref[...])
    total += mm_cols(cots_ref[:, 2 * HEAD_DIM : 3 * HEAD_DIM], value_ref[...])
    slots = cots_ref[:, 3 * HEAD_DIM : 3 * HEAD_DIM + SLOTS]
    spread = jnp.concatenate(
        [jnp.where(rank_ref[0] == head, slots, jnp.zeros_like(slots)) for head in range(4)],
        axis=1,
    )
    total += mm_cols(spread, slot_ref[...])
    for i, ref in enumerate((own_ref, near_ref, far_ref, farthest_ref)):
        ref[...] = total[i * ROWS_OWN : (i + 1) * ROWS_OWN].astype(BF16)
    gain_ref[...] = jnp.sum(total * normed_ref[...].astype(F32), axis=0, keepdims=True)


def unproject(rank, cots, normed, query_weight, key_weight, value_weight, slot_weight):
    weight = pl.BlockSpec((K_TILE, HEAD_DIM), lambda k, rank: (k, rank[0]))
    rows = pl.BlockSpec((ROWS_OWN, K_TILE), lambda k, rank: (0, k))
    return pl.pallas_call(
        unproject_kernel,
        grid_spec=pltpu.PrefetchScalarGridSpec(
            num_scalar_prefetch=1,
            grid=(WIDTH // K_TILE,),
            in_specs=[
                pl.BlockSpec((TOKENS, WIDE), lambda k, rank: (0, 0)),
                pl.BlockSpec((TOKENS, K_TILE), lambda k, rank: (0, k)),
                weight,
                weight,
                weight,
                pl.BlockSpec((K_TILE, ALL_SLOTS), lambda k, rank: (k, 0)),
            ],
            out_specs=[rows] * 4 + [pl.BlockSpec((1, K_TILE), lambda k, rank: (0, k))],
        ),
        out_shape=[jax.ShapeDtypeStruct((ROWS_OWN, WIDTH), BF16)] * 4
        + [jax.ShapeDtypeStruct((1, WIDTH), F32)],
        compiler_params=pltpu.CompilerParams(
            vmem_limit_bytes=48 * 1024 * 1024, dimension_semantics=("arbitrary",)
        ),
        cost_estimate=cost(7),
        name="unproject",
    )(rank, cots, normed, query_weight, key_weight, value_weight, slot_weight)


ALL_HIDDEN = 3 * HIDDEN
COLUMNS = HEAD_DIM + WIDE
CHUNK = 64
BLOCK_ROWS = WIDTH // 4


def mixer_grads_kernel(*refs):
    normed_ref, cots_ref, out_ref, block_ref = refs[1], refs[2], refs[-2], refs[-1]
    block_ref[:, :WIDE] = mm_rows(normed_ref[...], cots_ref[...]).astype(BF16)
    mixed = jnp.concatenate([ref[...] for ref in refs[3:7]], axis=0)
    branch = jnp.concatenate([ref[...] for ref in refs[7:11]], axis=0)
    block_ref[:, WIDE:] = mm_rows(mixed, branch).astype(BF16)
    for side in range(2):
        for z in range(4):
            source = (side * 4 + z) * CHUNK
            target = (z * 2 + side) * CHUNK
            out_ref[target : target + CHUNK] = block_ref[source : source + CHUNK]


def mixer_grads(rank, normed, cots, mixed, branch):
    return pl.pallas_call(
        mixer_grads_kernel,
        grid_spec=pltpu.PrefetchScalarGridSpec(
            num_scalar_prefetch=1,
            grid=(4,),
            in_specs=[
                pl.BlockSpec((TOKENS, BLOCK_ROWS), lambda y, rank: (0, y)),
                pl.BlockSpec((TOKENS, WIDE), lambda y, rank: (0, 0)),
            ]
            + [pl.BlockSpec((ROWS_OWN, BLOCK_ROWS), lambda y, rank: (0, y))] * 4
            + [pl.BlockSpec((ROWS_OWN, HEAD_DIM), lambda y, rank: (0, rank[0]))] * 4,
            out_specs=pl.BlockSpec((BLOCK_ROWS, COLUMNS), lambda y, rank: (y, 0)),
            scratch_shapes=[pltpu.VMEM((BLOCK_ROWS, COLUMNS), BF16)],
        ),
        out_shape=jax.ShapeDtypeStruct((WIDTH, COLUMNS), BF16),
        compiler_params=pltpu.CompilerParams(
            vmem_limit_bytes=56 * 1024 * 1024, dimension_semantics=("arbitrary",)
        ),
        cost_estimate=cost(10),
        name="mixer_grads",
    )(rank, normed, cots, *mixed, *branch)


def ffn_kernel(count, *refs):
    piece_refs = refs[: 2 * count]
    weight_ref, inner_ref, cots_ref, grads_ref, rows_ref, sems = refs[2 * count : 2 * count + 6]
    step = pl.program_id(0)

    def copies(side):
        start = 0
        made = []
        for i, ref in enumerate(piece_refs[side * count : (side + 1) * count]):
            place = rows_ref.at[side, pl.ds(start, ref.shape[0])]
            made.append(pltpu.make_async_copy(ref, place, sems.at[side * count + i]))
            start += ref.shape[0]
        return made

    @pl.when(step == 0)
    def _():
        for copy in copies(0) + copies(1):
            copy.start()
        for copy in copies(0):
            copy.wait()

    def halves_of(side, columns):
        return [
            mm(rows_ref[side, half * TOKENS : (half + 1) * TOKENS], weight_ref[:, columns])
            for half in range(2)
        ]

    both = halves_of(0, slice(0, 2 * TILE))

    @pl.when(step == 0)
    def _():
        for copy in copies(1):
            copy.wait()

    inner_cots = halves_of(1, slice(2 * TILE, 3 * TILE))
    for half in range(2):
        rows = slice(half * TOKENS, (half + 1) * TOKENS)
        gate_pre, up_pre = both[half][:, :TILE], both[half][:, TILE:]
        inner_cot = inner_cots[half]
        sigma = sigmoid(gate_pre)
        gate_act = gate_pre * sigma
        inner_ref[rows] = (gate_act * up_pre).astype(BF16)
        slope = sigma * (1.0 + gate_pre * (1.0 - sigma))
        cots_ref[rows, :TILE] = (inner_cot * up_pre * slope).astype(BF16)
        cots_ref[rows, TILE:] = (inner_cot * gate_act).astype(BF16)
    for m in range(4):
        cut = slice(m * BLOCK_ROWS, (m + 1) * BLOCK_ROWS)
        grads_ref[cut, : 2 * TILE] = mm_rows(rows_ref[0, :, cut], cots_ref[...]).astype(BF16)
        grads_ref[cut, 2 * TILE :] = mm_rows(rows_ref[1, :, cut], inner_ref[...]).astype(BF16)


def ffn(pieces, cot_pieces, weights):
    both = 2 * TOKENS
    count = len(pieces)
    return pl.pallas_call(
        functools.partial(ffn_kernel, count),
        grid=(TILES,),
        in_specs=[pl.BlockSpec(memory_space=pl.ANY)] * (2 * count)
        + [pl.BlockSpec((WIDTH, 3 * TILE), lambda n: (0, n))],
        out_specs=[
            pl.BlockSpec((both, TILE), lambda n: (0, n)),
            pl.BlockSpec((both, 2 * TILE), lambda n: (0, n)),
            pl.BlockSpec((WIDTH, 3 * TILE), lambda n: (0, n)),
        ],
        out_shape=[
            jax.ShapeDtypeStruct((both, HIDDEN), BF16),
            jax.ShapeDtypeStruct((both, 2 * HIDDEN), BF16),
            jax.ShapeDtypeStruct((WIDTH, ALL_HIDDEN), BF16),
        ],
        scratch_shapes=[
            pltpu.VMEM((2, both, WIDTH), BF16),
            pltpu.SemaphoreType.DMA((2 * count,)),
        ],
        compiler_params=pltpu.CompilerParams(
            vmem_limit_bytes=56 * 1024 * 1024, dimension_semantics=("arbitrary",)
        ),
        cost_estimate=cost(24),
        name="ffn",
    )(*pieces, *cot_pieces, weights)


def back_product(cots_ref, weight_refs):
    total = None
    width = cots_ref.shape[1] // TILES
    for n, ref in enumerate(weight_refs):
        term = mm_cols(cots_ref[:, n * width : (n + 1) * width], ref[...])
        total = term if total is None else total + term
    return total


def away_kernel(cots_ref, *refs):
    refs[-1][...] = back_product(cots_ref, refs[:TILES]).astype(BF16)


def near_kernel(cots_ref, *refs):
    total = back_product(cots_ref, refs[:TILES]) + refs[TILES][...].astype(F32)
    for i, ref in enumerate(refs[-4:]):
        ref[...] = total[i * ROWS_OWN : (i + 1) * ROWS_OWN].astype(ref.dtype)


def pair_block(n):
    return pl.BlockSpec(
        (pl.Element(BLOCK_ROWS), pl.Element(2 * TILE)),
        lambda m: (m * BLOCK_ROWS, n * 3 * TILE),
    )


def down_block(n):
    return pl.BlockSpec((BLOCK_ROWS, TILE), lambda m: (m, 3 * n + 2))


def ffn_back(cots, weights, block, half, got=None, done=()):
    kernel = away_kernel if got is None else near_kernel
    own = jax.ShapeDtypeStruct((ROWS_OWN, WIDTH), F32)
    ends = jax.ShapeDtypeStruct((ROWS_OWN, WIDTH), BF16)
    away = jax.ShapeDtypeStruct((TOKENS, WIDTH), BF16)
    outs = [away] if got is None else [own, own, own, ends]
    extra = [] if got is None else [got]
    return pl.pallas_call(
        kernel,
        grid=(4,),
        in_specs=[pl.BlockSpec((TOKENS, cots.shape[1]), lambda m: (half, 0))]
        + [block(n) for n in range(TILES)]
        + [pl.BlockSpec((TOKENS, BLOCK_ROWS), lambda m: (0, m)) for _ in extra]
        + [pl.BlockSpec(memory_space=pl.ANY) for _ in done],
        out_specs=[pl.BlockSpec((out.shape[0], BLOCK_ROWS), lambda m: (0, m)) for out in outs],
        out_shape=outs,
        compiler_params=pltpu.CompilerParams(vmem_limit_bytes=48 * 1024 * 1024),
        cost_estimate=cost(5),
        name="ffn_back",
    )(cots, *[weights] * TILES, *extra, *done)


def mixer_out_kernel(pieces_ref, query_ref, key_ref, value_ref, slot_ref, out_ref):
    slots = []
    for head in range(4):
        block = pieces_ref[head].astype(F32) + pieces_ref[4 + head].astype(F32)
        columns = slice(head * HEAD_DIM, (head + 1) * HEAD_DIM)
        for i, ref in enumerate((query_ref, key_ref, value_ref)):
            ref[:, columns] = block[:, i * HEAD_DIM : (i + 1) * HEAD_DIM]
        slots.append(block[:, 3 * HEAD_DIM : 3 * HEAD_DIM + SLOTS])
        out_ref[:, columns] = block[:, WIDE:]
    slot_ref[...] = jnp.concatenate(slots, axis=1)


def mixer_out(pieces):
    rows = pieces.shape[1]
    widths = (WIDTH, WIDTH, WIDTH, ALL_SLOTS, WIDTH)
    return pl.pallas_call(
        mixer_out_kernel,
        in_specs=[pl.BlockSpec(memory_space=pltpu.VMEM)],
        out_specs=[pl.BlockSpec(memory_space=pltpu.VMEM)] * 5,
        out_shape=[jax.ShapeDtypeStruct((rows, width), F32) for width in widths],
        cost_estimate=cost(2),
        name="mixer_out",
    )(pieces)


def to_plane(value):
    parts = []
    for y in range(4):
        for z in range(4):
            for side in range(2):
                start = y * 8 * CHUNK + side * 4 * CHUNK + z * CHUNK
                parts.append(value[:, start : start + CHUNK])
    return jnp.concatenate(parts, axis=1)


def from_plane(value):
    parts = []
    for y in range(4):
        for side in range(2):
            for z in range(4):
                start = y * 8 * CHUNK + z * 2 * CHUNK + side * CHUNK
                parts.append(value[:, start : start + CHUNK])
    return jnp.concatenate(parts, axis=1)


def rms_parts(rows):
    root = lax.rsqrt(jnp.mean(rows * rows, axis=1, keepdims=True) + EPS)
    return rows * root, root


def rms_back(incoming, gain, unit, root):
    scaled = incoming * gain
    return root * (scaled - unit * jnp.mean(scaled * unit, axis=1, keepdims=True))


def mix_out_kernel(rank_ref, *refs):
    part_refs = refs[:4]
    weight_ref, input_ref, keep_ref, gain_ref, hidden_ref, ffn_in_ref, mixed_ref = refs[4:]
    step = pl.program_id(0)
    for k in range(4):

        @pl.when(step == k)
        def _():
            part = part_refs[k][...]
            place = pl.multiple_of((rank_ref[0] ^ k) * HEAD_DIM, HEAD_DIM)
            mixed_ref[:, pl.ds(place, HEAD_DIM)] = part
            product = mm(part, weight_ref[...])
            hidden_ref[...] = product if k == 0 else hidden_ref[...] + product

    @pl.when(step == 3)
    def _():
        hidden = input_ref[...].astype(F32) + keep_ref[...] * hidden_ref[...]
        hidden_ref[...] = hidden
        ffn_in_ref[...] = to_plane((rms_parts(hidden)[0] * gain_ref[...]).astype(BF16))


def mix_out(rank, parts, out_weight, block_input, keep, gain):
    def fixed(shape):
        return pl.BlockSpec(shape, lambda k, rank: (0, 0))

    own = (ROWS_OWN, WIDTH)
    return pl.pallas_call(
        mix_out_kernel,
        grid_spec=pltpu.PrefetchScalarGridSpec(
            num_scalar_prefetch=1,
            grid=(4,),
            in_specs=[fixed((ROWS_OWN, HEAD_DIM))] * 4
            + [
                pl.BlockSpec((HEAD_DIM, WIDTH), lambda k, rank: (rank[0] ^ k, 0)),
                fixed(own),
                fixed((ROWS_OWN, 1)),
                fixed((1, WIDTH)),
            ],
            out_specs=[fixed(own)] * 3,
        ),
        out_shape=[
            jax.ShapeDtypeStruct(own, F32),
            jax.ShapeDtypeStruct(own, BF16),
            jax.ShapeDtypeStruct(own, BF16),
        ],
        compiler_params=pltpu.CompilerParams(
            vmem_limit_bytes=48 * 1024 * 1024, dimension_semantics=("arbitrary",)
        ),
        cost_estimate=cost(6),
        name="mix_out",
    )(rank, *parts, out_weight, block_input, keep, gain)


def norm_back_kernel(
    own_ref, left_ref, right_ref, cot_ref, hidden_ref, keep_ref, gain_ref,
    hidden_cot_ref, branch_ref, gain_cot_ref,
):
    incoming = own_ref[...] + left_ref[...].astype(F32) + right_ref[...].astype(F32)
    incoming = from_plane(incoming)
    unit, root = rms_parts(hidden_ref[...])
    hidden_cot = cot_ref[...].astype(F32) + rms_back(incoming, gain_ref[...], unit, root)
    hidden_cot_ref[...] = hidden_cot
    branch_ref[...] = (keep_ref[...] * hidden_cot).astype(BF16)
    gain_cot_ref[...] = jnp.sum(incoming * unit, axis=0, keepdims=True)


def block_out_kernel(own_ref, left_ref, right_ref, hidden_ref, keep_ref, out_ref):
    down = own_ref[...] + left_ref[...].astype(F32) + right_ref[...].astype(F32)
    out_ref[...] = hidden_ref[...] + keep_ref[...] * from_plane(down)


def input_back_kernel(own_ref, near_ref, far_ref, input_ref, hidden_cot_ref, gain_ref, out_ref):
    incoming = own_ref[...].astype(F32) + near_ref[...].astype(F32) + far_ref[...].astype(F32)
    unit, root = rms_parts(input_ref[...].astype(F32))
    out_ref[...] = hidden_cot_ref[...] + rms_back(incoming, gain_ref[...], unit, root)


def own_rows(kernel, arrays, outs, name):
    def spec(shape):
        return pl.BlockSpec((min(shape[0], ROWS_OWN), shape[1]), lambda i: (0, 0))

    return pl.pallas_call(
        kernel,
        grid=(1,),
        in_specs=[spec(array.shape) for array in arrays],
        out_specs=[spec(shape) for shape, _ in outs],
        out_shape=[jax.ShapeDtypeStruct(shape, dtype) for shape, dtype in outs],
        compiler_params=pltpu.CompilerParams(vmem_limit_bytes=32 * 1024 * 1024),
        cost_estimate=cost(3),
        name=name,
    )(*arrays)


def norm_back(*arrays):
    own = (ROWS_OWN, WIDTH)
    return own_rows(
        norm_back_kernel, arrays, [(own, F32), (own, BF16), ((1, WIDTH), F32)], "norm_back"
    )


def block_out(*arrays):
    return own_rows(block_out_kernel, arrays, [((ROWS_OWN, WIDTH), F32)], "block_out")[0]


def input_back(*arrays):
    return own_rows(input_back_kernel, arrays, [((ROWS_OWN, WIDTH), F32)], "input_back")[0]


def halves_kernel(side_ref, gate_ref, up_ref, down_ref, keep_ref, give_ref):
    rows = gate_ref.shape[0]
    part = gate_ref.shape[1] // 2
    padding = jnp.zeros((rows, HIDDEN - part), BF16)
    down = down_ref[...]
    for half in range(2):
        cut = slice(half * part, (half + 1) * part)
        gate, up, turned = [
            jnp.concatenate([value, padding], axis=1)
            for value in (gate_ref[:, cut], up_ref[:, cut], down[:, cut])
        ]
        tiles = []
        for n in range(TILES):
            tiles += [value[:, n * TILE : (n + 1) * TILE] for value in (gate, up, turned)]
        packed = jnp.concatenate(tiles, axis=1)

        @pl.when(side_ref[0] == half)
        def _():
            keep_ref[...] = packed

        @pl.when(side_ref[0] != half)
        def _():
            give_ref[...] = packed


def weight_halves(side, gate_weight, up_weight, down_weight):
    shape = jax.ShapeDtypeStruct((gate_weight.shape[0], 3 * HIDDEN), BF16)
    return pl.pallas_call(
        halves_kernel,
        in_specs=[RANK_SPEC] + [pl.BlockSpec(memory_space=pltpu.VMEM)] * 3,
        out_specs=[pl.BlockSpec(memory_space=pltpu.VMEM)] * 2,
        out_shape=[shape, shape],
        cost_estimate=cost(2),
        name="weight_halves",
    )(side, gate_weight, up_weight, down_weight)


def turn_kernel(rows_ref, keep_ref, out_ref):
    kept = rows_ref[...].astype(F32) * keep_ref[...]
    out_ref[...] = to_plane(kept.astype(BF16))


def turn_rows(rows, keep):
    return own_rows(turn_kernel, [rows, keep], [(rows.shape, BF16)], "turn_rows")[0]


AXES = ("y", "xh", "z", "xl", "c")
DP = ("y", "xh", "z")
MP = ("xl", "c")
RING = ("xh", "xl")
PLANE = ("y", "z")
SWAP = ((0, 1), (1, 0))


def tied(value, token):
    return value + (0.0 * token[0, 0]).astype(value.dtype)


def after(value, *first):
    return lax.optimization_barrier((value,) + first)[0]


def other_core(value):
    return lax.ppermute(value, "c", SWAP)


def other_chip(value):
    return lax.ppermute(value, "xl", SWAP)


def along_ring(value, step):
    return lax.ppermute(value, RING, [(i, (i + step) % 4) for i in range(4)])


def gather_sides(own):
    return along_ring(own, 1), along_ring(own, -1), other_core(own)


def gather_opposite(left, right):
    half = left.shape[0] // 2
    return along_ring(left[:half], 1), along_ring(right[half:], -1)


def gathered(own, left, right, near, first, second):
    away = [near] + [other_core(value) for value in (left, right, first, second)]
    return [own, left, right, first, second] + away


def ring_opposite(opposite):
    half = opposite.shape[0] // 2
    return along_ring(opposite[:half], 1), along_ring(opposite[half:], -1)


def ring_sides(left, right, from_left, from_right):
    half = left.shape[0] // 2
    right = jnp.concatenate([right[:half] + from_left.astype(F32), right[half:]], axis=0)
    left = jnp.concatenate([left[:half], left[half:] + from_right.astype(F32)], axis=0)
    return left.astype(BF16), right.astype(BF16)


def ring_send(left, right):
    return along_ring(right, 1), along_ring(left, -1)


def add(left, right):
    return (left.astype(F32) + right.astype(F32)).astype(BF16)


def on_device(
    block_input,
    cotangent,
    pad_mask,
    seq_counts,
    gain_mix,
    query_weight,
    key_weight,
    value_weight,
    slot_weight,
    out_weight,
    gain_ffn,
    gate_weight,
    up_weight,
    down_weight,
):
    rows_own, width = block_input.shape
    rank = lax.axis_index(MP)
    side = lax.axis_index("xh")
    live = (jnp.arange(SEQS) < seq_counts[0]).astype(jnp.int32)
    keep_seq = (pad_mask[0] * live[:, None]).astype(F32)
    keep_own = lax.dynamic_slice_in_dim(keep_seq, rank * RUN, RUN, 1).reshape(rows_own, 1)

    rank_array = rank.reshape(1).astype(jnp.int32)

    hidden_part = gate_weight.shape[1] // 2
    kept, given = weight_halves(
        side.reshape(1).astype(jnp.int32), gate_weight, up_weight, down_weight.T
    )
    got = lax.ppermute(given, "xh", SWAP)
    paired = jnp.concatenate(
        [jnp.where(side == 0, kept, got), jnp.where(side == 0, got, kept)], axis=0
    )
    weights = lax.all_gather(paired, PLANE, axis=0, tiled=True)

    far = other_chip(after(block_input, got))
    cot_start = turn_rows(cotangent, keep_own)
    mixer_weights = (query_weight, key_weight, value_weight, slot_weight)
    near_input = other_core(block_input)
    keep_column = keep_seq[:, :, None]
    near_pre, near_normed, done = project_near(
        rank_array, (block_input, near_input), gain_mix[None], mixer_weights
    )
    far = tied(far, done)
    cot_sides = gather_sides(tied(cot_start, done))
    pre, normed_four, *blocks, mixing, probs, past = project_mix(
        rank_array, (far, other_core(far)), gain_mix[None], mixer_weights,
        near_pre, near_normed, keep_column,
    )
    cot_ends = gather_opposite(*cot_sides[:2])
    mixed_parts = (
        blocks[0],
        other_core(blocks[1]),
        other_chip(blocks[2]),
        lax.ppermute(blocks[3], MP, [(i, 3 - i) for i in range(4)]),
    )
    hidden, ffn_own, mixed_own = mix_out(
        rank_array, mixed_parts, out_weight, block_input, keep_own, gain_ffn[None]
    )
    hidden, cot_ends = lax.optimization_barrier((hidden, cot_ends))
    cot_pieces = gathered(cot_start, *cot_sides, *cot_ends)
    ffn_own = after(ffn_own, *cot_ends)
    sides = gather_sides(ffn_own)
    ends = gather_opposite(*sides[:2])
    pieces = gathered(ffn_own, *sides, *ends)
    inner, cots, grads = ffn(pieces, cot_pieces, weights)
    ffn_sums = lax.psum_scatter(grads, PLANE, scatter_dimension=0, tiled=True)
    (away,) = ffn_back(cots, weights, pair_block, 1)
    (late_away,) = ffn_back(after(inner, away), weights, down_block, 1)
    got = other_core(away)
    own, left, right, ends = ffn_back(cots, weights, pair_block, 0, after(got, late_away))
    mixed_far = other_chip(tied(mixed_own, away))
    (late_near,) = ffn_back(
        after(inner, ends), weights, down_block, 0, done=(mixed_far, ends)
    )
    from_left, from_right, late_near = lax.optimization_barrier(
        ring_opposite(ends) + (late_near,)
    )
    left, right = ring_sides(left, right, from_left, from_right)
    from_left, from_right = ring_send(left, right)
    hidden_cot, branch_cot, gain_ffn_part = norm_back(
        own, from_left, from_right, cotangent, hidden, keep_own, gain_ffn[None]
    )
    branch_near = other_core(branch_cot)
    branch_far = other_chip(branch_cot)
    branch = (branch_cot, branch_near, branch_far, other_core(branch_far))
    head_cots = mixer_backward(
        rank_array, pre, keep_column, mixing, probs, past, out_weight, branch
    )
    mixed_all = (mixed_own, other_core(mixed_own), mixed_far, other_core(mixed_far))
    mixer_sums = lax.psum_scatter(
        mixer_grads(rank_array, normed_four, head_cots, mixed_all, branch),
        PLANE,
        scatter_dimension=0,
        tiled=True,
    )

    own, near, far, farthest, gain_mix_part = unproject(
        rank_array, after(head_cots, mixed_all[3]), normed_four, *mixer_weights
    )
    near = other_core(near)
    far = add(far, other_core(farthest))
    late_got = other_core(tied(late_away, gain_mix_part))
    gain_sums = jnp.stack([gain_mix_part[0] / gain_mix, gain_ffn_part[0]]).reshape(32, 128)
    for axis in ("c", "xl", "xh"):
        gain_sums = gain_sums + lax.ppermute(gain_sums, axis, SWAP)
    far = other_chip(tied(far, gain_sums))
    late_near = late_near.astype(F32) + late_got.astype(F32)
    late_own, late_left, late_right, late_ends = jnp.split(late_near, 4, axis=0)
    late_ends = ring_opposite(late_ends.astype(BF16))
    for axis in PLANE:
        for step in (1, 2):
            gain_sums = gain_sums + lax.ppermute(
                gain_sums, axis, [(i, i ^ step) for i in range(4)]
            )
    late_sides = ring_send(*ring_sides(late_left, late_right, *late_ends))
    gain_sums = gain_sums.reshape(2, width)
    input_grad = input_back(own, near, far, block_input, hidden_cot, gain_mix[None])
    block_output = block_out(late_own, *late_sides, hidden, keep_own)
    kept = lax.dynamic_slice_in_dim(ffn_sums, side * CHUNK, CHUNK, 0)
    given_back = lax.ppermute(
        lax.dynamic_slice_in_dim(ffn_sums, (1 - side) * CHUNK, CHUNK, 0), "xh", SWAP
    )
    mixer_sums, block_output, input_grad, gain_sums, given_back = lax.optimization_barrier(
        (mixer_sums, block_output, input_grad, gain_sums, given_back)
    )
    rows_out = rows_own // 8
    pieces = lax.all_to_all(
        mixer_sums.reshape(8, rows_out, COLUMNS), ("xh", "xl", "c"), 0, 0
    )
    query_grad, key_grad, value_grad, slot_grad, out_grad = mixer_out(pieces)

    def finish(tiles):
        mine, theirs = [
            jnp.concatenate([grads[:, n * TILE : (n + 1) * TILE] for n in tiles], axis=1)[
                :, :hidden_part
            ]
            for grads in (kept, given_back)
        ]
        return jnp.concatenate(
            [jnp.where(side == 0, mine, theirs), jnp.where(side == 0, theirs, mine)], axis=1
        ).astype(F32)

    return (
        block_output,
        input_grad,
        gain_sums[0],
        query_grad,
        key_grad,
        value_grad,
        slot_grad,
        out_grad,
        gain_sums[1],
        finish((0, 3, 6)),
        finish((1, 4, 7)),
        finish((2, 5, 8)).T,
    )


def solution(mesh):
    fine = jax.sharding.Mesh(mesh.devices.reshape(4, 2, 4, 2, 2), AXES)
    rows = P(AXES, None)
    return jax.shard_map(
        on_device,
        mesh=fine,
        in_specs=(
            rows,
            rows,
            P(DP, None, None),
            P(DP),
            P(),
            P(),
            P(),
            P(),
            P(),
            P(),
            P(),
            P(DP, MP),
            P(DP, MP),
            P(MP, DP),
        ),
        out_specs=(
            rows,
            rows,
            P(),
            rows,
            rows,
            rows,
            rows,
            rows,
            P(),
            P(DP, MP),
            P(DP, MP),
            P(MP, DP),
        ),
        check_vma=False,
    )
```

```python
import functools

import jax
import jax.numpy as jnp
from jax import lax
from jax.experimental import pallas as pl
from jax.experimental.pallas import tpu as pltpu
from jax.sharding import PartitionSpec as P

HEAD_DIM = 512
SLOTS = 64
LENGTH = 256
RUN = 64
RUNS = 4
SEQS = 2
LEVELS = (128, 64, 32, 16, 8, 4, 2, 1)
SCALE = HEAD_DIM ** (-0.5)
GATE_SCALE = 0.125
F32 = jnp.float32
BF16 = jnp.bfloat16


def mm(left, right):
    return jnp.dot(left, right, preferred_element_type=F32)


def mm_cols(left, right):
    return lax.dot_general(left, right, (((1,), (1,)), ((), ())), preferred_element_type=F32)


def mm_rows(left, right):
    return lax.dot_general(left, right, (((0,), (0,)), ((), ())), preferred_element_type=F32)


def halves(value):
    high = value.astype(BF16)
    return high, (value - high.astype(F32)).astype(BF16)


def fine_product(left, right):
    left_high, left_low = halves(left)
    right_high, right_low = halves(right)
    rows, width = left.shape[0], right.shape[1]
    out = mm(
        jnp.concatenate([left_high, left_low], axis=0),
        jnp.concatenate([right_high, right_low], axis=1),
    )
    return out[:rows, :width] + out[:rows, width:] + out[rows:, :width]


def fine_cols_product(left, right):
    left_high, left_low = halves(left)
    right_high, right_low = halves(right)
    return mm_cols(
        jnp.concatenate([left_high, left_low, left_high], axis=1),
        jnp.concatenate([right_high, right_high, right_low], axis=1),
    )


def decay_tables(slot_pre, keep):
    log_gate = jnp.minimum(slot_pre, 0.0) - jnp.log1p(jnp.exp(-jnp.abs(slot_pre)))
    log_decay = keep * log_gate * GATE_SCALE
    half = jnp.tanh(-0.5 * log_decay)
    written = 2.0 * half / (1.0 + half)
    rows = lax.broadcasted_iota(jnp.int32, log_decay.shape, 0)
    running = log_decay
    shift = 1
    while shift < LENGTH:
        running = running + jnp.where(rows >= shift, pltpu.roll(running, shift, 0), 0.0)
        shift *= 2
    return log_decay, written, running


def later_sum(value):
    rows = lax.broadcasted_iota(jnp.int32, value.shape, 0)
    shift = 1
    while shift < LENGTH:
        value = value + jnp.where(rows < LENGTH - shift, pltpu.roll(value, LENGTH - shift, 0), 0.0)
        shift *= 2
    return value


def level_factors(running):
    rows = lax.broadcasted_iota(jnp.int32, running.shape, 0)
    last = running
    factors = {}
    size = 1
    while size < LENGTH:
        odd = (rows & size) != 0
        before = pltpu.roll(last, size, 0)
        factor = jnp.exp(jnp.where(odd, running - before, last - running))
        factors[size] = (jnp.where(odd, factor, 0.0), jnp.where(odd, 0.0, factor))
        last = jnp.where(odd, last, pltpu.roll(last, LENGTH - size, 0))
        size *= 2
    return factors


def level_map(flip):
    rows = lax.broadcasted_iota(jnp.int32, (LENGTH, LENGTH), 0)
    cols = lax.broadcasted_iota(jnp.int32, (LENGTH, LENGTH), 1)
    later = rows < cols if flip else rows > cols
    return jnp.where(later, rows ^ cols, 0), rows == cols


def at_level(where_map, size):
    return (where_map >= size) & (where_map < 2 * size)


def gather_rows(ref, rank, seq, start, width):
    parts = []
    for run in range(RUNS):
        first = pl.multiple_of(((rank ^ run) * SEQS + seq) * RUN, RUN)
        parts.append(ref[pl.ds(first, RUN), start : start + width])
    return jnp.concatenate(parts, axis=0)


def spread_rows(ref, rank, seq, start, width, value):
    for run in range(RUNS):
        first = pl.multiple_of(((rank ^ run) * SEQS + seq) * RUN, RUN)
        ref[pl.ds(first, RUN), start : start + width] = value[run * RUN : (run + 1) * RUN]


def sigmoid(value):
    return 1.0 / (1.0 + jnp.exp(-value))


def silu(value):
    return value * sigmoid(value)


def silu_slope(pre):
    sigma = sigmoid(pre)
    return sigma * (1.0 + pre * (1.0 - sigma))


def mix_forward(rank, seq, pre_ref, keep, mixed_ref, mixing_ref, probs_ref, past_ref):
    queries = silu(gather_rows(pre_ref, rank, seq, 0, HEAD_DIM)).astype(BF16)
    keys = silu(gather_rows(pre_ref, rank, seq, HEAD_DIM, HEAD_DIM)).astype(BF16)
    values = gather_rows(pre_ref, rank, seq, 2 * HEAD_DIM, HEAD_DIM).astype(BF16)
    slot_pre = gather_rows(pre_ref, rank, seq, 3 * HEAD_DIM, SLOTS)
    _, written, running = decay_tables(slot_pre, keep)
    factors = level_factors(running)
    where_map, own = level_map(False)
    pairs = mm_cols(queries, keys)
    own_pairs = jnp.sum(jnp.where(own, pairs, 0.0), axis=1, keepdims=True)
    past = jnp.zeros((LENGTH, SLOTS), F32)
    for size in LEVELS:
        after, before = factors[size]
        past = past + after * fine_product(
            jnp.where(at_level(where_map, size), pairs, 0.0), before * written
        )
    past = SCALE * past
    scores = past + SCALE * own_pairs * written
    grown = jnp.exp(scores - jnp.max(scores, axis=1, keepdims=True))
    probs = grown / jnp.sum(grown, axis=1, keepdims=True)
    mixing = jnp.where(own, jnp.sum(probs * written, axis=1, keepdims=True), 0.0)
    for size in LEVELS:
        after, before = factors[size]
        mixing = jnp.where(
            at_level(where_map, size),
            fine_cols_product(probs * after, before * written),
            mixing,
        )
    mixing = mixing.astype(BF16)
    mixed = mm(mixing, values).astype(BF16)
    spread_rows(mixed_ref, rank, seq, 0, HEAD_DIM, mixed)
    mixing_ref[seq] = mixing
    probs_ref[seq] = probs
    past_ref[seq] = past


def mixer_backward_kernel(
    rank_ref, pre_ref, keep_ref, mixing_ref, probs_ref, past_ref, weight_ref,
    own_ref, near_ref, far_ref, farthest_ref, out_ref, cot_ref,
):
    rank = rank_ref[0]
    seq = pl.program_id(0)

    @pl.when(seq == 0)
    def _():
        branch = [ref[...] for ref in (own_ref, near_ref, far_ref, farthest_ref)]
        cot_ref[...] = mm_cols(jnp.concatenate(branch, axis=0), weight_ref[...]).astype(BF16)

    query_pre = gather_rows(pre_ref, rank, seq, 0, HEAD_DIM)
    key_pre = gather_rows(pre_ref, rank, seq, HEAD_DIM, HEAD_DIM)
    queries = silu(query_pre).astype(BF16)
    keys = silu(key_pre).astype(BF16)
    values = gather_rows(pre_ref, rank, seq, 2 * HEAD_DIM, HEAD_DIM).astype(BF16)
    slot_pre = gather_rows(pre_ref, rank, seq, 3 * HEAD_DIM, SLOTS)
    cot = gather_rows(cot_ref, rank, seq, 0, HEAD_DIM)
    keep = keep_ref[0]
    log_decay, written, running = decay_tables(slot_pre, keep)
    factors = level_factors(running)
    where_map, own = level_map(False)
    where_flip, _ = level_map(True)
    probs = probs_ref[0]
    past = past_ref[0]
    mixing = mixing_ref[0]
    spread_rows(
        out_ref, rank, seq, 2 * HEAD_DIM, HEAD_DIM, mm_rows(mixing, cot).astype(BF16)
    )
    pairs_flip = mm_cols(keys, queries) * SCALE
    cot_flip = mm_cols(values, cot)
    mixing_cot = mm_cols(cot, values)
    own_cot = jnp.sum(jnp.where(own, mixing_cot, 0.0), axis=1, keepdims=True)
    own_pairs = jnp.sum(jnp.where(own, pairs_flip, 0.0), axis=1, keepdims=True)
    past_cot = jnp.zeros((LENGTH, SLOTS), F32)
    for size in LEVELS:
        after, before = factors[size]
        past_cot = past_cot + after * fine_product(
            jnp.where(at_level(where_map, size), mixing_cot, 0.0), before * written
        )
    probs_cot = past_cot + own_cot * written
    scores_cot = probs * (probs_cot - jnp.sum(probs * probs_cot, axis=1, keepdims=True))
    row_flow = probs * past_cot + scores_cot * past
    pairs_cot = jnp.where(own, jnp.sum(scores_cot * written, axis=1, keepdims=True), 0.0)
    ahead = jnp.zeros((LENGTH, SLOTS), F32)
    both_flip = jnp.concatenate([cot_flip, pairs_flip], axis=1)
    where_both = jnp.concatenate([where_flip, where_flip], axis=1)
    for size in LEVELS:
        after, before = factors[size]
        pairs_cot = jnp.where(
            at_level(where_map, size),
            fine_cols_product(scores_cot * after, before * written),
            pairs_cot,
        )
        ahead = ahead + before * fine_product(
            jnp.where(at_level(where_both, size), both_flip, 0.0),
            jnp.concatenate([probs * after, scores_cot * after], axis=0),
        )
    pairs_low = (SCALE * pairs_cot).astype(BF16)
    query_cot = (mm(pairs_low, keys) * silu_slope(query_pre)).astype(BF16)
    spread_rows(out_ref, rank, seq, 0, HEAD_DIM, query_cot)
    key_cot = (mm_rows(pairs_low, queries) * silu_slope(key_pre)).astype(BF16)
    spread_rows(out_ref, rank, seq, HEAD_DIM, HEAD_DIM, key_cot)
    running_cot = row_flow - written * ahead
    written_cot = ahead + own_cot * probs + scores_cot * own_pairs
    decay_cot = later_sum(running_cot) - written_cot * jnp.exp(log_decay)
    slot_cot = decay_cot * keep * GATE_SCALE * sigmoid(-slot_pre)
    padded = jnp.concatenate([slot_cot, jnp.zeros((LENGTH, SLOTS), F32)], axis=1).astype(BF16)
    spread_rows(out_ref, rank, seq, 3 * HEAD_DIM, 2 * SLOTS, padded)


def cost(microseconds):
    return pl.CostEstimate(
        flops=int(microseconds * 1.1e9), bytes_accessed=1 << 20, transcendentals=0
    )


def whole(shape):
    zeros = (0,) * len(shape)
    return pl.BlockSpec(shape, lambda seq, rank: zeros)


def one_seq(shape):
    return pl.BlockSpec((1,) + shape, lambda seq, rank: (seq, 0, 0))


TOKENS = RUNS * SEQS * RUN
WIDE = 3 * HEAD_DIM + 2 * SLOTS
WIDTH = 2048
ROWS_OWN = SEQS * RUN
RANK_SPEC = pl.BlockSpec(memory_space=pltpu.SMEM)


def mixer_backward(rank, pre, keep, mixing, probs, past, out_weight, branch):
    return pl.pallas_call(
        mixer_backward_kernel,
        grid_spec=pltpu.PrefetchScalarGridSpec(
            num_scalar_prefetch=1,
            grid=(SEQS,),
            in_specs=[
                whole((TOKENS, WIDE)),
                one_seq((LENGTH, 1)),
                one_seq((LENGTH, LENGTH)),
                one_seq((LENGTH, SLOTS)),
                one_seq((LENGTH, SLOTS)),
                pl.BlockSpec((HEAD_DIM, WIDTH), lambda seq, rank: (rank[0], 0)),
            ]
            + [whole((ROWS_OWN, WIDTH))] * 4,
            out_specs=whole((TOKENS, WIDE)),
            scratch_shapes=[pltpu.VMEM((TOKENS, HEAD_DIM), BF16)],
        ),
        out_shape=jax.ShapeDtypeStruct((TOKENS, WIDE), BF16),
        compiler_params=pltpu.CompilerParams(
            vmem_limit_bytes=48 * 1024 * 1024, dimension_semantics=("arbitrary",)
        ),
        cost_estimate=cost(13),
        name="mixer_backward",
    )(rank, pre, keep, mixing, probs, past, out_weight, *branch)


EPS = 1e-05
K_TILE = 512
ALL_SLOTS = 4 * SLOTS
TILE = 256
TILES = 3
HIDDEN = TILE * TILES


def project_step(step, rank, row_refs, gain, weight_refs, slot_ref, pre_ref, normed_ref, slots_ref, first):
    last = first + 2 * ROWS_OWN

    @pl.when(step == 0)
    def _():
        for i, ref in enumerate(row_refs):
            rows = ref[...].astype(F32)
            root = lax.rsqrt(jnp.mean(rows * rows, axis=1, keepdims=True) + EPS)
            start = first + i * ROWS_OWN
            normed_ref[start : start + ROWS_OWN] = (rows * root * gain).astype(BF16)
        pre_ref[first:last] = jnp.zeros((2 * ROWS_OWN, WIDE), F32)
        slots_ref[...] = jnp.zeros_like(slots_ref)

    left = normed_ref[first:last, pl.ds(pl.multiple_of(step * K_TILE, K_TILE), K_TILE)]
    for i, ref in enumerate(weight_refs):
        pre_ref[first:last, i * HEAD_DIM : (i + 1) * HEAD_DIM] += mm(left, ref[...])
    slots_ref[...] += mm(left, slot_ref[...])

    @pl.when(step == WIDTH // K_TILE - 1)
    def _():
        mine = jnp.zeros((2 * ROWS_OWN, SLOTS), F32)
        for head in range(4):
            mine = jnp.where(rank == head, slots_ref[:, head * SLOTS : (head + 1) * SLOTS], mine)
        pre_ref[first:last, 3 * HEAD_DIM :] = jnp.concatenate([mine, jnp.zeros_like(mine)], axis=1)


def project_near_kernel(
    rank_ref, own_ref, near_ref, gain_ref, query_ref, key_ref, value_ref, slot_ref,
    pre_ref, normed_ref, done_ref, slots_ref,
):
    step = pl.program_id(0)
    project_step(
        step, rank_ref[0], (own_ref, near_ref), gain_ref[...], (query_ref, key_ref, value_ref),
        slot_ref, pre_ref, normed_ref, slots_ref, 0,
    )
    done_ref[...] = jnp.zeros_like(done_ref)


def project_mix_kernel(
    rank_ref, far_ref, farthest_ref, gain_ref, query_ref, key_ref, value_ref, slot_ref,
    near_pre_ref, near_normed_ref, keep_ref,
    pre_ref, normed_ref, first_ref, second_ref, third_ref, fourth_ref,
    mixing_ref, probs_ref, past_ref, slots_ref, mixed_ref,
):
    step = pl.program_id(0)
    half = 2 * ROWS_OWN

    @pl.when(step == 0)
    def _():
        pre_ref[:half] = near_pre_ref[...]
        normed_ref[:half] = near_normed_ref[...]

    project_step(
        step, rank_ref[0], (far_ref, farthest_ref), gain_ref[...], (query_ref, key_ref, value_ref),
        slot_ref, pre_ref, normed_ref, slots_ref, half,
    )

    @pl.when(step == WIDTH // K_TILE - 1)
    def _():
        for seq in range(SEQS):
            mix_forward(
                rank_ref[0], seq, pre_ref, keep_ref[seq], mixed_ref, mixing_ref, probs_ref, past_ref
            )
        for i, ref in enumerate((first_ref, second_ref, third_ref, fourth_ref)):
            ref[...] = mixed_ref[i * ROWS_OWN : (i + 1) * ROWS_OWN]


def project(kernel, rank, pieces, gain, weights, extra, outs, scratch, micros, name):
    def fixed(shape):
        zeros = (0,) * len(shape)
        return pl.BlockSpec(shape, lambda k, rank: zeros)

    weight = pl.BlockSpec((K_TILE, HEAD_DIM), lambda k, rank: (k, rank[0]))
    return pl.pallas_call(
        kernel,
        grid_spec=pltpu.PrefetchScalarGridSpec(
            num_scalar_prefetch=1,
            grid=(WIDTH // K_TILE,),
            in_specs=[fixed(piece.shape) for piece in pieces]
            + [fixed((1, WIDTH)), weight, weight, weight]
            + [pl.BlockSpec((K_TILE, ALL_SLOTS), lambda k, rank: (k, 0))]
            + [fixed(array.shape) for array in extra],
            out_specs=[fixed(shape) for shape, _ in outs],
            scratch_shapes=[pltpu.VMEM((2 * ROWS_OWN, ALL_SLOTS), F32)] + scratch,
        ),
        out_shape=[jax.ShapeDtypeStruct(shape, dtype) for shape, dtype in outs],
        compiler_params=pltpu.CompilerParams(
            vmem_limit_bytes=48 * 1024 * 1024, dimension_semantics=("arbitrary",)
        ),
        cost_estimate=cost(micros),
        name=name,
    )(rank, *pieces, gain, *weights, *extra)


def project_near(rank, pieces, gain, weights):
    half = 2 * ROWS_OWN
    outs = [((half, WIDE), F32), ((half, WIDTH), BF16), ((8, 128), F32)]
    return project(
        project_near_kernel, rank, pieces, gain, weights, (), outs, [], 7, "project_near"
    )


def project_mix(rank, pieces, gain, weights, near_pre, near_normed, keep):
    outs = [((TOKENS, WIDE), F32), ((TOKENS, WIDTH), BF16)]
    outs += [((ROWS_OWN, HEAD_DIM), BF16)] * 4 + [((SEQS, LENGTH, LENGTH), BF16)]
    outs += [((SEQS, LENGTH, SLOTS), F32)] * 2
    return project(
        project_mix_kernel, rank, pieces, gain, weights, (near_pre, near_normed, keep), outs,
        [pltpu.VMEM((TOKENS, HEAD_DIM), BF16)], 13, "project_mix",
    )


def unproject_kernel(
    rank_ref, cots_ref, normed_ref, query_ref, key_ref, value_ref, slot_ref,
    own_ref, near_ref, far_ref, farthest_ref, gain_ref,
):
    total = mm_cols(cots_ref[:, :HEAD_DIM], query_ref[...])
    total += mm_cols(cots_ref[:, HEAD_DIM : 2 * HEAD_DIM], key_ref[...])
    total += mm_cols(cots_ref[:, 2 * HEAD_DIM : 3 * HEAD_DIM], value_ref[...])
    slots = cots_ref[:, 3 * HEAD_DIM : 3 * HEAD_DIM + SLOTS]
    spread = jnp.concatenate(
        [jnp.where(rank_ref[0] == head, slots, jnp.zeros_like(slots)) for head in range(4)],
        axis=1,
    )
    total += mm_cols(spread, slot_ref[...])
    for i, ref in enumerate((own_ref, near_ref, far_ref, farthest_ref)):
        ref[...] = total[i * ROWS_OWN : (i + 1) * ROWS_OWN].astype(BF16)
    gain_ref[...] = jnp.sum(total * normed_ref[...].astype(F32), axis=0, keepdims=True)


def unproject(rank, cots, normed, query_weight, key_weight, value_weight, slot_weight):
    weight = pl.BlockSpec((K_TILE, HEAD_DIM), lambda k, rank: (k, rank[0]))
    rows = pl.BlockSpec((ROWS_OWN, K_TILE), lambda k, rank: (0, k))
    return pl.pallas_call(
        unproject_kernel,
        grid_spec=pltpu.PrefetchScalarGridSpec(
            num_scalar_prefetch=1,
            grid=(WIDTH // K_TILE,),
            in_specs=[
                pl.BlockSpec((TOKENS, WIDE), lambda k, rank: (0, 0)),
                pl.BlockSpec((TOKENS, K_TILE), lambda k, rank: (0, k)),
                weight,
                weight,
                weight,
                pl.BlockSpec((K_TILE, ALL_SLOTS), lambda k, rank: (k, 0)),
            ],
            out_specs=[rows] * 4 + [pl.BlockSpec((1, K_TILE), lambda k, rank: (0, k))],
        ),
        out_shape=[jax.ShapeDtypeStruct((ROWS_OWN, WIDTH), BF16)] * 4
        + [jax.ShapeDtypeStruct((1, WIDTH), F32)],
        compiler_params=pltpu.CompilerParams(
            vmem_limit_bytes=48 * 1024 * 1024, dimension_semantics=("arbitrary",)
        ),
        cost_estimate=cost(7),
        name="unproject",
    )(rank, cots, normed, query_weight, key_weight, value_weight, slot_weight)


ALL_HIDDEN = 3 * HIDDEN
COLUMNS = HEAD_DIM + WIDE
CHUNK = 64
BLOCK_ROWS = WIDTH // 4


def mixer_grads_kernel(*refs):
    normed_ref, cots_ref, out_ref, block_ref = refs[1], refs[2], refs[-2], refs[-1]
    block_ref[:, :WIDE] = mm_rows(normed_ref[...], cots_ref[...]).astype(BF16)
    mixed = jnp.concatenate([ref[...] for ref in refs[3:7]], axis=0)
    branch = jnp.concatenate([ref[...] for ref in refs[7:11]], axis=0)
    block_ref[:, WIDE:] = mm_rows(mixed, branch).astype(BF16)
    for side in range(2):
        for z in range(4):
            source = (side * 4 + z) * CHUNK
            target = (z * 2 + side) * CHUNK
            out_ref[target : target + CHUNK] = block_ref[source : source + CHUNK]


def mixer_grads(rank, normed, cots, mixed, branch):
    return pl.pallas_call(
        mixer_grads_kernel,
        grid_spec=pltpu.PrefetchScalarGridSpec(
            num_scalar_prefetch=1,
            grid=(4,),
            in_specs=[
                pl.BlockSpec((TOKENS, BLOCK_ROWS), lambda y, rank: (0, y)),
                pl.BlockSpec((TOKENS, WIDE), lambda y, rank: (0, 0)),
            ]
            + [pl.BlockSpec((ROWS_OWN, BLOCK_ROWS), lambda y, rank: (0, y))] * 4
            + [pl.BlockSpec((ROWS_OWN, HEAD_DIM), lambda y, rank: (0, rank[0]))] * 4,
            out_specs=pl.BlockSpec((BLOCK_ROWS, COLUMNS), lambda y, rank: (y, 0)),
            scratch_shapes=[pltpu.VMEM((BLOCK_ROWS, COLUMNS), BF16)],
        ),
        out_shape=jax.ShapeDtypeStruct((WIDTH, COLUMNS), BF16),
        compiler_params=pltpu.CompilerParams(
            vmem_limit_bytes=56 * 1024 * 1024, dimension_semantics=("arbitrary",)
        ),
        cost_estimate=cost(10),
        name="mixer_grads",
    )(rank, normed, cots, *mixed, *branch)


def ffn_kernel(plan, *refs):
    weight_ref, inner_ref, cots_ref, grads_ref, rows_ref, sems = refs[-6:]
    step = pl.program_id(0)

    def copies(side):
        start = 0
        made = []
        for i, (at, first, rows) in enumerate(plan[side]):
            source = refs[at].at[pl.ds(first, rows)]
            place = rows_ref.at[side, pl.ds(start, rows)]
            made.append(pltpu.make_async_copy(source, place, sems.at[side, i]))
            start += rows
        return made

    @pl.when(step == 0)
    def _():
        for copy in copies(0) + copies(1):
            copy.start()
        for copy in copies(0):
            copy.wait()

    def halves_of(side, columns):
        return [
            mm(rows_ref[side, half * TOKENS : (half + 1) * TOKENS], weight_ref[:, columns])
            for half in range(2)
        ]

    both = halves_of(0, slice(0, 2 * TILE))

    @pl.when(step == 0)
    def _():
        for copy in copies(1):
            copy.wait()

    inner_cots = halves_of(1, slice(2 * TILE, 3 * TILE))
    for half in range(2):
        rows = slice(half * TOKENS, (half + 1) * TOKENS)
        gate_pre, up_pre = both[half][:, :TILE], both[half][:, TILE:]
        inner_cot = inner_cots[half]
        sigma = sigmoid(gate_pre)
        gate_act = gate_pre * sigma
        inner_ref[rows] = (gate_act * up_pre).astype(BF16)
        slope = sigma * (1.0 + gate_pre * (1.0 - sigma))
        cots_ref[rows, :TILE] = (inner_cot * up_pre * slope).astype(BF16)
        cots_ref[rows, TILE:] = (inner_cot * gate_act).astype(BF16)
    for m in range(4):
        cut = slice(m * BLOCK_ROWS, (m + 1) * BLOCK_ROWS)
        grads_ref[cut, : 2 * TILE] = mm_rows(rows_ref[0, :, cut], cots_ref[...]).astype(BF16)
        grads_ref[cut, 2 * TILE :] = mm_rows(rows_ref[1, :, cut], inner_ref[...]).astype(BF16)


def ffn(arrays, plan, weights):
    both = 2 * TOKENS
    return pl.pallas_call(
        functools.partial(ffn_kernel, plan),
        grid=(TILES,),
        in_specs=[pl.BlockSpec(memory_space=pl.ANY)] * len(arrays)
        + [pl.BlockSpec((WIDTH, 3 * TILE), lambda n: (0, n))],
        out_specs=[
            pl.BlockSpec((both, TILE), lambda n: (0, n)),
            pl.BlockSpec((both, 2 * TILE), lambda n: (0, n)),
            pl.BlockSpec((WIDTH, 3 * TILE), lambda n: (0, n)),
        ],
        out_shape=[
            jax.ShapeDtypeStruct((both, HIDDEN), BF16),
            jax.ShapeDtypeStruct((both, 2 * HIDDEN), BF16),
            jax.ShapeDtypeStruct((WIDTH, ALL_HIDDEN), BF16),
        ],
        scratch_shapes=[
            pltpu.VMEM((2, both, WIDTH), BF16),
            pltpu.SemaphoreType.DMA((2, len(plan[0]))),
        ],
        compiler_params=pltpu.CompilerParams(
            vmem_limit_bytes=56 * 1024 * 1024, dimension_semantics=("arbitrary",)
        ),
        cost_estimate=cost(24),
        name="ffn",
    )(*arrays, weights)


def back_product(cots_ref, weight_refs):
    total = None
    width = cots_ref.shape[1] // TILES
    for n, ref in enumerate(weight_refs):
        term = mm_cols(cots_ref[:, n * width : (n + 1) * width], ref[...])
        total = term if total is None else total + term
    return total


def away_kernel(cots_ref, *refs):
    refs[-1][...] = back_product(cots_ref, refs[:TILES]).astype(BF16)


def near_kernel(cots_ref, *refs):
    total = back_product(cots_ref, refs[:TILES]) + refs[TILES][...].astype(F32)
    for i, ref in enumerate(refs[-4:]):
        ref[...] = total[i * ROWS_OWN : (i + 1) * ROWS_OWN].astype(ref.dtype)


def pair_block(n):
    return pl.BlockSpec(
        (pl.Element(BLOCK_ROWS), pl.Element(2 * TILE)),
        lambda m: (m * BLOCK_ROWS, n * 3 * TILE),
    )


def down_block(n):
    return pl.BlockSpec((BLOCK_ROWS, TILE), lambda m: (m, 3 * n + 2))


def ffn_back(cots, weights, block, half, got=None, done=()):
    kernel = away_kernel if got is None else near_kernel
    own = jax.ShapeDtypeStruct((ROWS_OWN, WIDTH), F32)
    ends = jax.ShapeDtypeStruct((ROWS_OWN, WIDTH), BF16)
    away = jax.ShapeDtypeStruct((TOKENS, WIDTH), BF16)
    outs = [away] if got is None else [own, own, own, ends]
    extra = [] if got is None else [got]
    return pl.pallas_call(
        kernel,
        grid=(4,),
        in_specs=[pl.BlockSpec((TOKENS, cots.shape[1]), lambda m: (half, 0))]
        + [block(n) for n in range(TILES)]
        + [pl.BlockSpec((TOKENS, BLOCK_ROWS), lambda m: (0, m)) for _ in extra]
        + [pl.BlockSpec(memory_space=pl.ANY) for _ in done],
        out_specs=[pl.BlockSpec((out.shape[0], BLOCK_ROWS), lambda m: (0, m)) for out in outs],
        out_shape=outs,
        compiler_params=pltpu.CompilerParams(vmem_limit_bytes=48 * 1024 * 1024),
        cost_estimate=cost(5),
        name="ffn_back",
    )(cots, *[weights] * TILES, *extra, *done)


def mixer_out_kernel(pieces_ref, query_ref, key_ref, value_ref, slot_ref, out_ref):
    slots = []
    for head in range(4):
        block = pieces_ref[head].astype(F32) + pieces_ref[4 + head].astype(F32)
        columns = slice(head * HEAD_DIM, (head + 1) * HEAD_DIM)
        for i, ref in enumerate((query_ref, key_ref, value_ref)):
            ref[:, columns] = block[:, i * HEAD_DIM : (i + 1) * HEAD_DIM]
        slots.append(block[:, 3 * HEAD_DIM : 3 * HEAD_DIM + SLOTS])
        out_ref[:, columns] = block[:, WIDE:]
    slot_ref[...] = jnp.concatenate(slots, axis=1)


def mixer_out(pieces):
    rows = pieces.shape[1]
    widths = (WIDTH, WIDTH, WIDTH, ALL_SLOTS, WIDTH)
    return pl.pallas_call(
        mixer_out_kernel,
        in_specs=[pl.BlockSpec(memory_space=pltpu.VMEM)],
        out_specs=[pl.BlockSpec(memory_space=pltpu.VMEM)] * 5,
        out_shape=[jax.ShapeDtypeStruct((rows, width), F32) for width in widths],
        cost_estimate=cost(2),
        name="mixer_out",
    )(pieces)


def to_plane(value):
    parts = []
    for y in range(4):
        for z in range(4):
            for side in range(2):
                start = y * 8 * CHUNK + side * 4 * CHUNK + z * CHUNK
                parts.append(value[:, start : start + CHUNK])
    return jnp.concatenate(parts, axis=1)


def from_plane(value):
    parts = []
    for y in range(4):
        for side in range(2):
            for z in range(4):
                start = y * 8 * CHUNK + z * 2 * CHUNK + side * CHUNK
                parts.append(value[:, start : start + CHUNK])
    return jnp.concatenate(parts, axis=1)


def rms_parts(rows):
    root = lax.rsqrt(jnp.mean(rows * rows, axis=1, keepdims=True) + EPS)
    return rows * root, root


def rms_back(incoming, gain, unit, root):
    scaled = incoming * gain
    return root * (scaled - unit * jnp.mean(scaled * unit, axis=1, keepdims=True))


def mix_out_kernel(rank_ref, *refs):
    part_refs = refs[:4]
    weight_ref, input_ref, keep_ref, gain_ref, hidden_ref, ffn_in_ref, mixed_ref = refs[4:]
    step = pl.program_id(0)
    for k in range(4):

        @pl.when(step == k)
        def _():
            part = part_refs[k][...]
            place = pl.multiple_of((rank_ref[0] ^ k) * HEAD_DIM, HEAD_DIM)
            mixed_ref[:, pl.ds(place, HEAD_DIM)] = part
            product = mm(part, weight_ref[...])
            hidden_ref[...] = product if k == 0 else hidden_ref[...] + product

    @pl.when(step == 3)
    def _():
        hidden = input_ref[...].astype(F32) + keep_ref[...] * hidden_ref[...]
        hidden_ref[...] = hidden
        ffn_in_ref[...] = to_plane((rms_parts(hidden)[0] * gain_ref[...]).astype(BF16))


def mix_out(rank, parts, out_weight, block_input, keep, gain):
    def fixed(shape):
        return pl.BlockSpec(shape, lambda k, rank: (0, 0))

    own = (ROWS_OWN, WIDTH)
    return pl.pallas_call(
        mix_out_kernel,
        grid_spec=pltpu.PrefetchScalarGridSpec(
            num_scalar_prefetch=1,
            grid=(4,),
            in_specs=[fixed((ROWS_OWN, HEAD_DIM))] * 4
            + [
                pl.BlockSpec((HEAD_DIM, WIDTH), lambda k, rank: (rank[0] ^ k, 0)),
                fixed(own),
                fixed((ROWS_OWN, 1)),
                fixed((1, WIDTH)),
            ],
            out_specs=[fixed(own)] * 3,
        ),
        out_shape=[
            jax.ShapeDtypeStruct(own, F32),
            jax.ShapeDtypeStruct(own, BF16),
            jax.ShapeDtypeStruct(own, BF16),
        ],
        compiler_params=pltpu.CompilerParams(
            vmem_limit_bytes=48 * 1024 * 1024, dimension_semantics=("arbitrary",)
        ),
        cost_estimate=cost(6),
        name="mix_out",
    )(rank, *parts, out_weight, block_input, keep, gain)


def norm_back_kernel(
    own_ref, left_ref, right_ref, cot_ref, hidden_ref, keep_ref, gain_ref,
    hidden_cot_ref, branch_ref, gain_cot_ref,
):
    incoming = own_ref[...] + left_ref[...].astype(F32) + right_ref[...].astype(F32)
    incoming = from_plane(incoming)
    unit, root = rms_parts(hidden_ref[...])
    hidden_cot = cot_ref[...].astype(F32) + rms_back(incoming, gain_ref[...], unit, root)
    hidden_cot_ref[...] = hidden_cot
    branch_ref[...] = (keep_ref[...] * hidden_cot).astype(BF16)
    gain_cot_ref[...] = jnp.sum(incoming * unit, axis=0, keepdims=True)


def block_out_kernel(own_ref, left_ref, right_ref, hidden_ref, keep_ref, out_ref):
    down = own_ref[...] + left_ref[...].astype(F32) + right_ref[...].astype(F32)
    out_ref[...] = hidden_ref[...] + keep_ref[...] * from_plane(down)


def input_back_kernel(own_ref, near_ref, far_ref, input_ref, hidden_cot_ref, gain_ref, out_ref):
    incoming = own_ref[...].astype(F32) + near_ref[...].astype(F32) + far_ref[...].astype(F32)
    unit, root = rms_parts(input_ref[...].astype(F32))
    out_ref[...] = hidden_cot_ref[...] + rms_back(incoming, gain_ref[...], unit, root)


def own_rows(kernel, arrays, outs, name):
    def spec(shape):
        return pl.BlockSpec((min(shape[0], ROWS_OWN), shape[1]), lambda i: (0, 0))

    return pl.pallas_call(
        kernel,
        grid=(1,),
        in_specs=[spec(array.shape) for array in arrays],
        out_specs=[spec(shape) for shape, _ in outs],
        out_shape=[jax.ShapeDtypeStruct(shape, dtype) for shape, dtype in outs],
        compiler_params=pltpu.CompilerParams(vmem_limit_bytes=32 * 1024 * 1024),
        cost_estimate=cost(3),
        name=name,
    )(*arrays)


def norm_back(*arrays):
    own = (ROWS_OWN, WIDTH)
    return own_rows(
        norm_back_kernel, arrays, [(own, F32), (own, BF16), ((1, WIDTH), F32)], "norm_back"
    )


def block_out(*arrays):
    return own_rows(block_out_kernel, arrays, [((ROWS_OWN, WIDTH), F32)], "block_out")[0]


def input_back(*arrays):
    return own_rows(input_back_kernel, arrays, [((ROWS_OWN, WIDTH), F32)], "input_back")[0]


def halves_kernel(side_ref, gate_ref, up_ref, down_ref, keep_ref, give_ref):
    rows = gate_ref.shape[0]
    part = gate_ref.shape[1] // 2
    padding = jnp.zeros((rows, HIDDEN - part), BF16)
    down = down_ref[...]
    for half in range(2):
        cut = slice(half * part, (half + 1) * part)
        gate, up, turned = [
            jnp.concatenate([value, padding], axis=1)
            for value in (gate_ref[:, cut], up_ref[:, cut], down[:, cut])
        ]
        tiles = []
        for n in range(TILES):
            tiles += [value[:, n * TILE : (n + 1) * TILE] for value in (gate, up, turned)]
        packed = jnp.concatenate(tiles, axis=1)

        @pl.when(side_ref[0] == half)
        def _():
            keep_ref[...] = packed

        @pl.when(side_ref[0] != half)
        def _():
            give_ref[...] = packed


def weight_halves(side, gate_weight, up_weight, down_weight):
    shape = jax.ShapeDtypeStruct((gate_weight.shape[0], 3 * HIDDEN), BF16)
    return pl.pallas_call(
        halves_kernel,
        in_specs=[RANK_SPEC] + [pl.BlockSpec(memory_space=pltpu.VMEM)] * 3,
        out_specs=[pl.BlockSpec(memory_space=pltpu.VMEM)] * 2,
        out_shape=[shape, shape],
        cost_estimate=cost(2),
        name="weight_halves",
    )(side, gate_weight, up_weight, down_weight)


def turn_kernel(rows_ref, keep_ref, out_ref):
    kept = rows_ref[...].astype(F32) * keep_ref[...]
    out_ref[...] = to_plane(kept.astype(BF16))


def turn_rows(rows, keep):
    return own_rows(turn_kernel, [rows, keep], [(rows.shape, BF16)], "turn_rows")[0]


AXES = ("y", "xh", "z", "xl", "c")
DP = ("y", "xh", "z")
MP = ("xl", "c")
RING = ("xh", "xl")
PLANE = ("y", "z")
SWAP = ((0, 1), (1, 0))


def tied(value, token):
    return value + (0.0 * token[0, 0]).astype(value.dtype)


def after(value, *first):
    return lax.optimization_barrier((value,) + first)[0]


def other_core(value):
    return lax.ppermute(value, "c", SWAP)


def other_chip(value):
    return lax.ppermute(value, "xl", SWAP)


def along_ring(value, step):
    return lax.ppermute(value, RING, [(i, (i + step) % 4) for i in range(4)])


def gather_sides(own):
    return along_ring(own, 1), along_ring(own, -1), other_core(own)


def ring_opposite(opposite):
    half = opposite.shape[0] // 2
    return along_ring(opposite[:half], 1), along_ring(opposite[half:], -1)


def ring_sides(left, right, from_left, from_right):
    half = left.shape[0] // 2
    right = jnp.concatenate([right[:half] + from_left.astype(F32), right[half:]], axis=0)
    left = jnp.concatenate([left[:half], left[half:] + from_right.astype(F32)], axis=0)
    return left.astype(BF16), right.astype(BF16)


def ring_send(left, right):
    return along_ring(right, 1), along_ring(left, -1)


def add(left, right):
    return (left.astype(F32) + right.astype(F32)).astype(BF16)


def on_device(
    block_input,
    cotangent,
    pad_mask,
    seq_counts,
    gain_mix,
    query_weight,
    key_weight,
    value_weight,
    slot_weight,
    out_weight,
    gain_ffn,
    gate_weight,
    up_weight,
    down_weight,
):
    rows_own, width = block_input.shape
    rank = lax.axis_index(MP)
    side = lax.axis_index("xh")
    live = (jnp.arange(SEQS) < seq_counts[0]).astype(jnp.int32)
    keep_seq = (pad_mask[0] * live[:, None]).astype(F32)
    keep_own = lax.dynamic_slice_in_dim(keep_seq, rank * RUN, RUN, 1).reshape(rows_own, 1)

    rank_array = rank.reshape(1).astype(jnp.int32)

    hidden_part = gate_weight.shape[1] // 2
    kept, given = weight_halves(
        side.reshape(1).astype(jnp.int32), gate_weight, up_weight, down_weight.T
    )
    got = lax.ppermute(given, "xh", SWAP)
    paired = jnp.concatenate(
        [jnp.where(side == 0, kept, got), jnp.where(side == 0, got, kept)], axis=0
    )
    weights = lax.all_gather(paired, PLANE, axis=0, tiled=True)

    far = other_chip(after(block_input, got))
    cot_start = turn_rows(cotangent, keep_own)
    mixer_weights = (query_weight, key_weight, value_weight, slot_weight)
    near_input = other_core(block_input)
    keep_column = keep_seq[:, :, None]
    near_pre, near_normed, done = project_near(
        rank_array, (block_input, near_input), gain_mix[None], mixer_weights
    )
    far = tied(far, done)
    cot_sides = gather_sides(tied(cot_start, done))
    pre, normed_four, *blocks, mixing, probs, past = project_mix(
        rank_array, (far, other_core(far)), gain_mix[None], mixer_weights,
        near_pre, near_normed, keep_column,
    )
    mixed_parts = (
        blocks[0],
        other_core(blocks[1]),
        other_chip(blocks[2]),
        lax.ppermute(blocks[3], MP, [(i, 3 - i) for i in range(4)]),
    )
    hidden, ffn_own, mixed_own = mix_out(
        rank_array, mixed_parts, out_weight, block_input, keep_own, gain_ffn[None]
    )
    sides = gather_sides(ffn_own)
    half = rows_own // 2
    from_left = along_ring(jnp.concatenate([sides[0][:half], cot_sides[0][:half]], axis=0), 1)
    from_right = along_ring(jnp.concatenate([sides[1][half:], cot_sides[1][half:]], axis=0), -1)
    arrays = [ffn_own, *sides[:2], cot_start, *cot_sides[:2], from_left, from_right]
    arrays += [sides[2], *map(other_core, sides[:2])]
    arrays += [cot_sides[2], *map(other_core, cot_sides[:2])]
    arrays += [other_core(from_left), other_core(from_right)]
    plan = [
        [
            (core + at, first, count)
            for core in (0, 8)
            for at, first, count in (
                (3 * kind, 0, rows_own),
                (3 * kind + 1, 0, rows_own),
                (3 * kind + 2, 0, rows_own),
                (6, kind * half, half),
                (7, kind * half, half),
            )
        ]
        for kind in range(2)
    ]
    inner, cots, grads = ffn(arrays, plan, weights)
    ffn_sums = lax.psum_scatter(grads, PLANE, scatter_dimension=0, tiled=True)
    (away,) = ffn_back(cots, weights, pair_block, 1)
    (late_away,) = ffn_back(after(inner, away), weights, down_block, 1)
    got = other_core(away)
    own, left, right, ends = ffn_back(cots, weights, pair_block, 0, after(got, late_away))
    mixed_far = other_chip(tied(mixed_own, away))
    (late_near,) = ffn_back(
        after(inner, ends), weights, down_block, 0, done=(mixed_far, ends)
    )
    from_left, from_right, late_near = lax.optimization_barrier(
        ring_opposite(ends) + (late_near,)
    )
    left, right = ring_sides(left, right, from_left, from_right)
    from_left, from_right = ring_send(left, right)
    hidden_cot, branch_cot, gain_ffn_part = norm_back(
        own, from_left, from_right, cotangent, hidden, keep_own, gain_ffn[None]
    )
    branch_near = other_core(branch_cot)
    branch_far = other_chip(branch_cot)
    branch = (branch_cot, branch_near, branch_far, other_core(branch_far))
    head_cots = mixer_backward(
        rank_array, pre, keep_column, mixing, probs, past, out_weight, branch
    )
    mixed_all = (mixed_own, other_core(mixed_own), mixed_far, other_core(mixed_far))
    mixer_sums = lax.psum_scatter(
        mixer_grads(rank_array, normed_four, head_cots, mixed_all, branch),
        PLANE,
        scatter_dimension=0,
        tiled=True,
    )

    own, near, far, farthest, gain_mix_part = unproject(
        rank_array, after(head_cots, mixed_all[3]), normed_four, *mixer_weights
    )
    near = other_core(near)
    far = add(far, other_core(farthest))
    late_got = other_core(tied(late_away, gain_mix_part))
    gain_sums = jnp.stack([gain_mix_part[0] / gain_mix, gain_ffn_part[0]]).reshape(32, 128)
    for axis in ("c", "xl", "xh"):
        gain_sums = gain_sums + lax.ppermute(gain_sums, axis, SWAP)
    far = other_chip(tied(far, gain_sums))
    late_near = late_near.astype(F32) + late_got.astype(F32)
    late_own, late_left, late_right, late_ends = jnp.split(late_near, 4, axis=0)
    late_ends = ring_opposite(late_ends.astype(BF16))
    for axis in PLANE:
        for step in (1, 2):
            gain_sums = gain_sums + lax.ppermute(
                gain_sums, axis, [(i, i ^ step) for i in range(4)]
            )
    late_sides = ring_send(*ring_sides(late_left, late_right, *late_ends))
    gain_sums = gain_sums.reshape(2, width)
    input_grad = input_back(own, near, far, block_input, hidden_cot, gain_mix[None])
    block_output = block_out(late_own, *late_sides, hidden, keep_own)
    kept = lax.dynamic_slice_in_dim(ffn_sums, side * CHUNK, CHUNK, 0)
    given_back = lax.ppermute(
        lax.dynamic_slice_in_dim(ffn_sums, (1 - side) * CHUNK, CHUNK, 0), "xh", SWAP
    )
    mixer_sums, block_output, input_grad, gain_sums, given_back = lax.optimization_barrier(
        (mixer_sums, block_output, input_grad, gain_sums, given_back)
    )
    rows_out = rows_own // 8
    pieces = lax.all_to_all(
        mixer_sums.reshape(8, rows_out, COLUMNS), ("xh", "xl", "c"), 0, 0
    )
    query_grad, key_grad, value_grad, slot_grad, out_grad = mixer_out(pieces)

    def finish(tiles):
        mine, theirs = [
            jnp.concatenate([grads[:, n * TILE : (n + 1) * TILE] for n in tiles], axis=1)[
                :, :hidden_part
            ]
            for grads in (kept, given_back)
        ]
        return jnp.concatenate(
            [jnp.where(side == 0, mine, theirs), jnp.where(side == 0, theirs, mine)], axis=1
        ).astype(F32)

    return (
        block_output,
        input_grad,
        gain_sums[0],
        query_grad,
        key_grad,
        value_grad,
        slot_grad,
        out_grad,
        gain_sums[1],
        finish((0, 3, 6)),
        finish((1, 4, 7)),
        finish((2, 5, 8)).T,
    )


def solution(mesh):
    fine = jax.sharding.Mesh(mesh.devices.reshape(4, 2, 4, 2, 2), AXES)
    rows = P(AXES, None)
    return jax.shard_map(
        on_device,
        mesh=fine,
        in_specs=(
            rows,
            rows,
            P(DP, None, None),
            P(DP),
            P(),
            P(),
            P(),
            P(),
            P(),
            P(),
            P(),
            P(DP, MP),
            P(DP, MP),
            P(MP, DP),
        ),
        out_specs=(
            rows,
            rows,
            P(),
            rows,
            rows,
            rows,
            rows,
            rows,
            P(),
            P(DP, MP),
            P(DP, MP),
            P(MP, DP),
        ),
        check_vma=False,
    )
```

```python
import functools

import jax
import jax.numpy as jnp
from jax import lax
from jax.experimental import pallas as pl
from jax.experimental.pallas import tpu as pltpu
from jax.sharding import PartitionSpec as P

HEAD_DIM = 512
SLOTS = 64
LENGTH = 256
RUN = 64
RUNS = 4
SEQS = 2
LEVELS = (128, 64, 32, 16, 8, 4, 2, 1)
SCALE = HEAD_DIM ** (-0.5)
GATE_SCALE = 0.125
F32 = jnp.float32
BF16 = jnp.bfloat16


def mm(left, right):
    return jnp.dot(left, right, preferred_element_type=F32)


def mm_cols(left, right):
    return lax.dot_general(left, right, (((1,), (1,)), ((), ())), preferred_element_type=F32)


def mm_rows(left, right):
    return lax.dot_general(left, right, (((0,), (0,)), ((), ())), preferred_element_type=F32)


def halves(value):
    high = value.astype(BF16)
    return high, (value - high.astype(F32)).astype(BF16)


def fine_product(left, right):
    left_high, left_low = halves(left)
    right_high, right_low = halves(right)
    rows, width = left.shape[0], right.shape[1]
    out = mm(
        jnp.concatenate([left_high, left_low], axis=0),
        jnp.concatenate([right_high, right_low], axis=1),
    )
    return out[:rows, :width] + out[:rows, width:] + out[rows:, :width]


def fine_cols_product(left, right):
    left_high, left_low = halves(left)
    right_high, right_low = halves(right)
    return mm_cols(
        jnp.concatenate([left_high, left_low, left_high], axis=1),
        jnp.concatenate([right_high, right_high, right_low], axis=1),
    )


def decay_tables(slot_pre, keep):
    log_gate = jnp.minimum(slot_pre, 0.0) - jnp.log1p(jnp.exp(-jnp.abs(slot_pre)))
    log_decay = keep * log_gate * GATE_SCALE
    half = jnp.tanh(-0.5 * log_decay)
    written = 2.0 * half / (1.0 + half)
    rows = lax.broadcasted_iota(jnp.int32, log_decay.shape, 0)
    running = log_decay
    shift = 1
    while shift < LENGTH:
        running = running + jnp.where(rows >= shift, pltpu.roll(running, shift, 0), 0.0)
        shift *= 2
    return log_decay, written, running


def later_sum(value):
    rows = lax.broadcasted_iota(jnp.int32, value.shape, 0)
    shift = 1
    while shift < LENGTH:
        value = value + jnp.where(rows < LENGTH - shift, pltpu.roll(value, LENGTH - shift, 0), 0.0)
        shift *= 2
    return value


def level_factors(running):
    rows = lax.broadcasted_iota(jnp.int32, running.shape, 0)
    last = running
    factors = {}
    size = 1
    while size < LENGTH:
        odd = (rows & size) != 0
        before = pltpu.roll(last, size, 0)
        factor = jnp.exp(jnp.where(odd, running - before, last - running))
        factors[size] = (jnp.where(odd, factor, 0.0), jnp.where(odd, 0.0, factor))
        last = jnp.where(odd, last, pltpu.roll(last, LENGTH - size, 0))
        size *= 2
    return factors


def level_map(flip):
    rows = lax.broadcasted_iota(jnp.int32, (LENGTH, LENGTH), 0)
    cols = lax.broadcasted_iota(jnp.int32, (LENGTH, LENGTH), 1)
    later = rows < cols if flip else rows > cols
    return jnp.where(later, rows ^ cols, 0), rows == cols


def at_level(where_map, size):
    return (where_map >= size) & (where_map < 2 * size)


def gather_rows(ref, rank, seq, start, width):
    parts = []
    for run in range(RUNS):
        first = pl.multiple_of(((rank ^ run) * SEQS + seq) * RUN, RUN)
        parts.append(ref[pl.ds(first, RUN), start : start + width])
    return jnp.concatenate(parts, axis=0)


def spread_rows(ref, rank, seq, start, width, value):
    for run in range(RUNS):
        first = pl.multiple_of(((rank ^ run) * SEQS + seq) * RUN, RUN)
        ref[pl.ds(first, RUN), start : start + width] = value[run * RUN : (run + 1) * RUN]


def sigmoid(value):
    return 1.0 / (1.0 + jnp.exp(-value))


def silu(value):
    return value * sigmoid(value)


def silu_slope(pre):
    sigma = sigmoid(pre)
    return sigma * (1.0 + pre * (1.0 - sigma))


def mix_forward(rank, seq, pre_ref, keep, mixed_ref, mixing_ref, probs_ref, past_ref):
    queries = silu(gather_rows(pre_ref, rank, seq, 0, HEAD_DIM)).astype(BF16)
    keys = silu(gather_rows(pre_ref, rank, seq, HEAD_DIM, HEAD_DIM)).astype(BF16)
    values = gather_rows(pre_ref, rank, seq, 2 * HEAD_DIM, HEAD_DIM).astype(BF16)
    slot_pre = gather_rows(pre_ref, rank, seq, 3 * HEAD_DIM, SLOTS)
    _, written, running = decay_tables(slot_pre, keep)
    factors = level_factors(running)
    where_map, own = level_map(False)
    pairs = mm_cols(queries, keys)
    own_pairs = jnp.sum(jnp.where(own, pairs, 0.0), axis=1, keepdims=True)
    past = jnp.zeros((LENGTH, SLOTS), F32)
    for size in LEVELS:
        after, before = factors[size]
        past = past + after * fine_product(
            jnp.where(at_level(where_map, size), pairs, 0.0), before * written
        )
    past = SCALE * past
    scores = past + SCALE * own_pairs * written
    grown = jnp.exp(scores - jnp.max(scores, axis=1, keepdims=True))
    probs = grown / jnp.sum(grown, axis=1, keepdims=True)
    mixing = jnp.where(own, jnp.sum(probs * written, axis=1, keepdims=True), 0.0)
    for size in LEVELS:
        after, before = factors[size]
        mixing = jnp.where(
            at_level(where_map, size),
            fine_cols_product(probs * after, before * written),
            mixing,
        )
    mixing = mixing.astype(BF16)
    mixed = mm(mixing, values).astype(BF16)
    spread_rows(mixed_ref, rank, seq, 0, HEAD_DIM, mixed)
    mixing_ref[seq] = mixing
    probs_ref[seq] = probs
    past_ref[seq] = past


def mixer_backward_kernel(
    rank_ref, pre_ref, keep_ref, mixing_ref, probs_ref, past_ref, weight_ref,
    own_ref, near_ref, far_ref, farthest_ref, out_ref, cot_ref,
):
    rank = rank_ref[0]
    seq = pl.program_id(0)

    @pl.when(seq == 0)
    def _():
        branch = [ref[...] for ref in (own_ref, near_ref, far_ref, farthest_ref)]
        cot_ref[...] = mm_cols(jnp.concatenate(branch, axis=0), weight_ref[...]).astype(BF16)

    query_pre = gather_rows(pre_ref, rank, seq, 0, HEAD_DIM)
    key_pre = gather_rows(pre_ref, rank, seq, HEAD_DIM, HEAD_DIM)
    queries = silu(query_pre).astype(BF16)
    keys = silu(key_pre).astype(BF16)
    values = gather_rows(pre_ref, rank, seq, 2 * HEAD_DIM, HEAD_DIM).astype(BF16)
    slot_pre = gather_rows(pre_ref, rank, seq, 3 * HEAD_DIM, SLOTS)
    cot = gather_rows(cot_ref, rank, seq, 0, HEAD_DIM)
    keep = keep_ref[0]
    log_decay, written, running = decay_tables(slot_pre, keep)
    factors = level_factors(running)
    where_map, own = level_map(False)
    where_flip, _ = level_map(True)
    probs = probs_ref[0]
    past = past_ref[0]
    mixing = mixing_ref[0]
    spread_rows(
        out_ref, rank, seq, 2 * HEAD_DIM, HEAD_DIM, mm_rows(mixing, cot).astype(BF16)
    )
    pairs_flip = mm_cols(keys, queries) * SCALE
    cot_flip = mm_cols(values, cot)
    mixing_cot = mm_cols(cot, values)
    own_cot = jnp.sum(jnp.where(own, mixing_cot, 0.0), axis=1, keepdims=True)
    own_pairs = jnp.sum(jnp.where(own, pairs_flip, 0.0), axis=1, keepdims=True)
    past_cot = jnp.zeros((LENGTH, SLOTS), F32)
    for size in LEVELS:
        after, before = factors[size]
        past_cot = past_cot + after * fine_product(
            jnp.where(at_level(where_map, size), mixing_cot, 0.0), before * written
        )
    probs_cot = past_cot + own_cot * written
    scores_cot = probs * (probs_cot - jnp.sum(probs * probs_cot, axis=1, keepdims=True))
    row_flow = probs * past_cot + scores_cot * past
    pairs_cot = jnp.where(own, jnp.sum(scores_cot * written, axis=1, keepdims=True), 0.0)
    ahead = jnp.zeros((LENGTH, SLOTS), F32)
    both_flip = jnp.concatenate([cot_flip, pairs_flip], axis=1)
    where_both = jnp.concatenate([where_flip, where_flip], axis=1)
    for size in LEVELS:
        after, before = factors[size]
        pairs_cot = jnp.where(
            at_level(where_map, size),
            fine_cols_product(scores_cot * after, before * written),
            pairs_cot,
        )
        ahead = ahead + before * fine_product(
            jnp.where(at_level(where_both, size), both_flip, 0.0),
            jnp.concatenate([probs * after, scores_cot * after], axis=0),
        )
    pairs_low = (SCALE * pairs_cot).astype(BF16)
    query_cot = (mm(pairs_low, keys) * silu_slope(query_pre)).astype(BF16)
    spread_rows(out_ref, rank, seq, 0, HEAD_DIM, query_cot)
    key_cot = (mm_rows(pairs_low, queries) * silu_slope(key_pre)).astype(BF16)
    spread_rows(out_ref, rank, seq, HEAD_DIM, HEAD_DIM, key_cot)
    running_cot = row_flow - written * ahead
    written_cot = ahead + own_cot * probs + scores_cot * own_pairs
    decay_cot = later_sum(running_cot) - written_cot * jnp.exp(log_decay)
    slot_cot = decay_cot * keep * GATE_SCALE * sigmoid(-slot_pre)
    padded = jnp.concatenate([slot_cot, jnp.zeros((LENGTH, SLOTS), F32)], axis=1).astype(BF16)
    spread_rows(out_ref, rank, seq, 3 * HEAD_DIM, 2 * SLOTS, padded)


def cost(microseconds):
    return pl.CostEstimate(
        flops=int(microseconds * 1.1e9), bytes_accessed=1 << 20, transcendentals=0
    )


def whole(shape):
    zeros = (0,) * len(shape)
    return pl.BlockSpec(shape, lambda seq, rank: zeros)


def one_seq(shape):
    return pl.BlockSpec((1,) + shape, lambda seq, rank: (seq, 0, 0))


TOKENS = RUNS * SEQS * RUN
WIDE = 3 * HEAD_DIM + 2 * SLOTS
WIDTH = 2048
ROWS_OWN = SEQS * RUN
RANK_SPEC = pl.BlockSpec(memory_space=pltpu.SMEM)


def mixer_backward(rank, pre, keep, mixing, probs, past, out_weight, branch):
    return pl.pallas_call(
        mixer_backward_kernel,
        grid_spec=pltpu.PrefetchScalarGridSpec(
            num_scalar_prefetch=1,
            grid=(SEQS,),
            in_specs=[
                whole((TOKENS, WIDE)),
                one_seq((LENGTH, 1)),
                one_seq((LENGTH, LENGTH)),
                one_seq((LENGTH, SLOTS)),
                one_seq((LENGTH, SLOTS)),
                pl.BlockSpec((HEAD_DIM, WIDTH), lambda seq, rank: (rank[0], 0)),
            ]
            + [whole((ROWS_OWN, WIDTH))] * 4,
            out_specs=whole((TOKENS, WIDE)),
            scratch_shapes=[pltpu.VMEM((TOKENS, HEAD_DIM), BF16)],
        ),
        out_shape=jax.ShapeDtypeStruct((TOKENS, WIDE), BF16),
        compiler_params=pltpu.CompilerParams(
            vmem_limit_bytes=48 * 1024 * 1024, dimension_semantics=("arbitrary",)
        ),
        cost_estimate=cost(13),
        name="mixer_backward",
    )(rank, pre, keep, mixing, probs, past, out_weight, *branch)


EPS = 1e-05
K_TILE = 512
ALL_SLOTS = 4 * SLOTS
TILE = 256
TILES = 3
HIDDEN = TILE * TILES


def project_step(step, rank, row_refs, gain, weight_refs, slot_ref, pre_ref, normed_ref, slots_ref, first):
    last = first + 2 * ROWS_OWN

    @pl.when(step == 0)
    def _():
        for i, ref in enumerate(row_refs):
            rows = ref[...].astype(F32)
            root = lax.rsqrt(jnp.mean(rows * rows, axis=1, keepdims=True) + EPS)
            start = first + i * ROWS_OWN
            normed_ref[start : start + ROWS_OWN] = (rows * root * gain).astype(BF16)
        pre_ref[first:last] = jnp.zeros((2 * ROWS_OWN, WIDE), F32)
        slots_ref[...] = jnp.zeros_like(slots_ref)

    left = normed_ref[first:last, pl.ds(pl.multiple_of(step * K_TILE, K_TILE), K_TILE)]
    for i, ref in enumerate(weight_refs):
        pre_ref[first:last, i * HEAD_DIM : (i + 1) * HEAD_DIM] += mm(left, ref[...])
    slots_ref[...] += mm(left, slot_ref[...])

    @pl.when(step == WIDTH // K_TILE - 1)
    def _():
        mine = jnp.zeros((2 * ROWS_OWN, SLOTS), F32)
        for head in range(4):
            mine = jnp.where(rank == head, slots_ref[:, head * SLOTS : (head + 1) * SLOTS], mine)
        pre_ref[first:last, 3 * HEAD_DIM :] = jnp.concatenate([mine, jnp.zeros_like(mine)], axis=1)


def project_near_kernel(
    rank_ref, own_ref, near_ref, gain_ref, query_ref, key_ref, value_ref, slot_ref,
    pre_ref, normed_ref, done_ref, slots_ref,
):
    step = pl.program_id(0)
    project_step(
        step, rank_ref[0], (own_ref, near_ref), gain_ref[...], (query_ref, key_ref, value_ref),
        slot_ref, pre_ref, normed_ref, slots_ref, 0,
    )
    done_ref[...] = jnp.zeros_like(done_ref)


def project_mix_kernel(
    rank_ref, far_ref, farthest_ref, gain_ref, query_ref, key_ref, value_ref, slot_ref,
    near_pre_ref, near_normed_ref, keep_ref,
    pre_ref, normed_ref, first_ref, second_ref, third_ref, fourth_ref,
    mixing_ref, probs_ref, past_ref, slots_ref, mixed_ref,
):
    step = pl.program_id(0)
    half = 2 * ROWS_OWN

    @pl.when(step == 0)
    def _():
        pre_ref[:half] = near_pre_ref[...]
        normed_ref[:half] = near_normed_ref[...]

    project_step(
        step, rank_ref[0], (far_ref, farthest_ref), gain_ref[...], (query_ref, key_ref, value_ref),
        slot_ref, pre_ref, normed_ref, slots_ref, half,
    )

    @pl.when(step == WIDTH // K_TILE - 1)
    def _():
        for seq in range(SEQS):
            mix_forward(
                rank_ref[0], seq, pre_ref, keep_ref[seq], mixed_ref, mixing_ref, probs_ref, past_ref
            )
        for i, ref in enumerate((first_ref, second_ref, third_ref, fourth_ref)):
            ref[...] = mixed_ref[i * ROWS_OWN : (i + 1) * ROWS_OWN]


def project(kernel, rank, pieces, gain, weights, extra, outs, scratch, micros, name):
    def fixed(shape):
        zeros = (0,) * len(shape)
        return pl.BlockSpec(shape, lambda k, rank: zeros)

    weight = pl.BlockSpec((K_TILE, HEAD_DIM), lambda k, rank: (k, rank[0]))
    return pl.pallas_call(
        kernel,
        grid_spec=pltpu.PrefetchScalarGridSpec(
            num_scalar_prefetch=1,
            grid=(WIDTH // K_TILE,),
            in_specs=[fixed(piece.shape) for piece in pieces]
            + [fixed((1, WIDTH)), weight, weight, weight]
            + [pl.BlockSpec((K_TILE, ALL_SLOTS), lambda k, rank: (k, 0))]
            + [fixed(array.shape) for array in extra],
            out_specs=[fixed(shape) for shape, _ in outs],
            scratch_shapes=[pltpu.VMEM((2 * ROWS_OWN, ALL_SLOTS), F32)] + scratch,
        ),
        out_shape=[jax.ShapeDtypeStruct(shape, dtype) for shape, dtype in outs],
        compiler_params=pltpu.CompilerParams(
            vmem_limit_bytes=48 * 1024 * 1024, dimension_semantics=("arbitrary",)
        ),
        cost_estimate=cost(micros),
        name=name,
    )(rank, *pieces, gain, *weights, *extra)


def project_near(rank, pieces, gain, weights):
    half = 2 * ROWS_OWN
    outs = [((half, WIDE), F32), ((half, WIDTH), BF16), ((8, 128), F32)]
    return project(
        project_near_kernel, rank, pieces, gain, weights, (), outs, [], 1, "project_near"
    )


def project_mix(rank, pieces, gain, weights, near_pre, near_normed, keep):
    outs = [((TOKENS, WIDE), F32), ((TOKENS, WIDTH), BF16)]
    outs += [((ROWS_OWN, HEAD_DIM), BF16)] * 4 + [((SEQS, LENGTH, LENGTH), BF16)]
    outs += [((SEQS, LENGTH, SLOTS), F32)] * 2
    return project(
        project_mix_kernel, rank, pieces, gain, weights, (near_pre, near_normed, keep), outs,
        [pltpu.VMEM((TOKENS, HEAD_DIM), BF16)], 13, "project_mix",
    )


def unproject_kernel(
    rank_ref, cots_ref, normed_ref, query_ref, key_ref, value_ref, slot_ref,
    own_ref, near_ref, far_ref, farthest_ref, gain_ref,
):
    total = mm_cols(cots_ref[:, :HEAD_DIM], query_ref[...])
    total += mm_cols(cots_ref[:, HEAD_DIM : 2 * HEAD_DIM], key_ref[...])
    total += mm_cols(cots_ref[:, 2 * HEAD_DIM : 3 * HEAD_DIM], value_ref[...])
    slots = cots_ref[:, 3 * HEAD_DIM : 3 * HEAD_DIM + SLOTS]
    spread = jnp.concatenate(
        [jnp.where(rank_ref[0] == head, slots, jnp.zeros_like(slots)) for head in range(4)],
        axis=1,
    )
    total += mm_cols(spread, slot_ref[...])
    for i, ref in enumerate((own_ref, near_ref, far_ref, farthest_ref)):
        ref[...] = total[i * ROWS_OWN : (i + 1) * ROWS_OWN].astype(BF16)
    gain_ref[...] = jnp.sum(total * normed_ref[...].astype(F32), axis=0, keepdims=True)


def unproject(rank, cots, normed, query_weight, key_weight, value_weight, slot_weight):
    weight = pl.BlockSpec((K_TILE, HEAD_DIM), lambda k, rank: (k, rank[0]))
    rows = pl.BlockSpec((ROWS_OWN, K_TILE), lambda k, rank: (0, k))
    return pl.pallas_call(
        unproject_kernel,
        grid_spec=pltpu.PrefetchScalarGridSpec(
            num_scalar_prefetch=1,
            grid=(WIDTH // K_TILE,),
            in_specs=[
                pl.BlockSpec((TOKENS, WIDE), lambda k, rank: (0, 0)),
                pl.BlockSpec((TOKENS, K_TILE), lambda k, rank: (0, k)),
                weight,
                weight,
                weight,
                pl.BlockSpec((K_TILE, ALL_SLOTS), lambda k, rank: (k, 0)),
            ],
            out_specs=[rows] * 4 + [pl.BlockSpec((1, K_TILE), lambda k, rank: (0, k))],
        ),
        out_shape=[jax.ShapeDtypeStruct((ROWS_OWN, WIDTH), BF16)] * 4
        + [jax.ShapeDtypeStruct((1, WIDTH), F32)],
        compiler_params=pltpu.CompilerParams(
            vmem_limit_bytes=48 * 1024 * 1024, dimension_semantics=("arbitrary",)
        ),
        cost_estimate=cost(7),
        name="unproject",
    )(rank, cots, normed, query_weight, key_weight, value_weight, slot_weight)


ALL_HIDDEN = 3 * HIDDEN
COLUMNS = HEAD_DIM + WIDE
CHUNK = 64
BLOCK_ROWS = WIDTH // 4


def mixer_grads_kernel(*refs):
    normed_ref, cots_ref, out_ref, block_ref = refs[1], refs[2], refs[-2], refs[-1]
    block_ref[:, :WIDE] = mm_rows(normed_ref[...], cots_ref[...]).astype(BF16)
    mixed = jnp.concatenate([ref[...] for ref in refs[3:7]], axis=0)
    branch = jnp.concatenate([ref[...] for ref in refs[7:11]], axis=0)
    block_ref[:, WIDE:] = mm_rows(mixed, branch).astype(BF16)
    for side in range(2):
        for z in range(4):
            source = (side * 4 + z) * CHUNK
            target = (z * 2 + side) * CHUNK
            out_ref[target : target + CHUNK] = block_ref[source : source + CHUNK]


def mixer_grads(rank, normed, cots, mixed, branch):
    return pl.pallas_call(
        mixer_grads_kernel,
        grid_spec=pltpu.PrefetchScalarGridSpec(
            num_scalar_prefetch=1,
            grid=(4,),
            in_specs=[
                pl.BlockSpec((TOKENS, BLOCK_ROWS), lambda y, rank: (0, y)),
                pl.BlockSpec((TOKENS, WIDE), lambda y, rank: (0, 0)),
            ]
            + [pl.BlockSpec((ROWS_OWN, BLOCK_ROWS), lambda y, rank: (0, y))] * 4
            + [pl.BlockSpec((ROWS_OWN, HEAD_DIM), lambda y, rank: (0, rank[0]))] * 4,
            out_specs=pl.BlockSpec((BLOCK_ROWS, COLUMNS), lambda y, rank: (y, 0)),
            scratch_shapes=[pltpu.VMEM((BLOCK_ROWS, COLUMNS), BF16)],
        ),
        out_shape=jax.ShapeDtypeStruct((WIDTH, COLUMNS), BF16),
        compiler_params=pltpu.CompilerParams(
            vmem_limit_bytes=56 * 1024 * 1024, dimension_semantics=("arbitrary",)
        ),
        cost_estimate=cost(10),
        name="mixer_grads",
    )(rank, normed, cots, *mixed, *branch)


def ffn_kernel(plan, *refs):
    weight_ref, inner_ref, cots_ref, grads_ref, rows_ref, sems = refs[-6:]
    step = pl.program_id(0)

    def copies(side):
        start = 0
        made = []
        for i, (at, first, rows) in enumerate(plan[side]):
            source = refs[at].at[pl.ds(first, rows)]
            place = rows_ref.at[side, pl.ds(start, rows)]
            made.append(pltpu.make_async_copy(source, place, sems.at[side, i]))
            start += rows
        return made

    @pl.when(step == 0)
    def _():
        for copy in copies(0) + copies(1):
            copy.start()
        for copy in copies(0):
            copy.wait()

    def halves_of(side, columns):
        return [
            mm(rows_ref[side, half * TOKENS : (half + 1) * TOKENS], weight_ref[:, columns])
            for half in range(2)
        ]

    both = halves_of(0, slice(0, 2 * TILE))

    @pl.when(step == 0)
    def _():
        for copy in copies(1):
            copy.wait()

    inner_cots = halves_of(1, slice(2 * TILE, 3 * TILE))
    for half in range(2):
        rows = slice(half * TOKENS, (half + 1) * TOKENS)
        gate_pre, up_pre = both[half][:, :TILE], both[half][:, TILE:]
        inner_cot = inner_cots[half]
        sigma = sigmoid(gate_pre)
        gate_act = gate_pre * sigma
        inner_ref[rows] = (gate_act * up_pre).astype(BF16)
        slope = sigma * (1.0 + gate_pre * (1.0 - sigma))
        cots_ref[rows, :TILE] = (inner_cot * up_pre * slope).astype(BF16)
        cots_ref[rows, TILE:] = (inner_cot * gate_act).astype(BF16)
    for m in range(4):
        cut = slice(m * BLOCK_ROWS, (m + 1) * BLOCK_ROWS)
        grads_ref[cut, : 2 * TILE] = mm_rows(rows_ref[0, :, cut], cots_ref[...]).astype(BF16)
        grads_ref[cut, 2 * TILE :] = mm_rows(rows_ref[1, :, cut], inner_ref[...]).astype(BF16)


def ffn(arrays, plan, weights):
    both = 2 * TOKENS
    return pl.pallas_call(
        functools.partial(ffn_kernel, plan),
        grid=(TILES,),
        in_specs=[pl.BlockSpec(memory_space=pl.ANY)] * len(arrays)
        + [pl.BlockSpec((WIDTH, 3 * TILE), lambda n: (0, n))],
        out_specs=[
            pl.BlockSpec((both, TILE), lambda n: (0, n)),
            pl.BlockSpec((both, 2 * TILE), lambda n: (0, n)),
            pl.BlockSpec((WIDTH, 3 * TILE), lambda n: (0, n)),
        ],
        out_shape=[
            jax.ShapeDtypeStruct((both, HIDDEN), BF16),
            jax.ShapeDtypeStruct((both, 2 * HIDDEN), BF16),
            jax.ShapeDtypeStruct((WIDTH, ALL_HIDDEN), BF16),
        ],
        scratch_shapes=[
            pltpu.VMEM((2, both, WIDTH), BF16),
            pltpu.SemaphoreType.DMA((2, len(plan[0]))),
        ],
        compiler_params=pltpu.CompilerParams(
            vmem_limit_bytes=56 * 1024 * 1024, dimension_semantics=("arbitrary",)
        ),
        cost_estimate=cost(24),
        name="ffn",
    )(*arrays, weights)


def back_product(cots_ref, weight_refs):
    total = None
    width = cots_ref.shape[1] // TILES
    for n, ref in enumerate(weight_refs):
        term = mm_cols(cots_ref[:, n * width : (n + 1) * width], ref[...])
        total = term if total is None else total + term
    return total


def away_kernel(cots_ref, *refs):
    refs[-1][...] = back_product(cots_ref, refs[:TILES]).astype(BF16)


def near_kernel(cots_ref, *refs):
    total = back_product(cots_ref, refs[:TILES]) + refs[TILES][...].astype(F32)
    for i, ref in enumerate(refs[-4:]):
        ref[...] = total[i * ROWS_OWN : (i + 1) * ROWS_OWN].astype(ref.dtype)


def pair_block(n):
    return pl.BlockSpec(
        (pl.Element(BLOCK_ROWS), pl.Element(2 * TILE)),
        lambda m: (m * BLOCK_ROWS, n * 3 * TILE),
    )


def down_block(n):
    return pl.BlockSpec((BLOCK_ROWS, TILE), lambda m: (m, 3 * n + 2))


def ffn_back(cots, weights, block, half, got=None, done=()):
    kernel = away_kernel if got is None else near_kernel
    own = jax.ShapeDtypeStruct((ROWS_OWN, WIDTH), F32)
    ends = jax.ShapeDtypeStruct((ROWS_OWN, WIDTH), BF16)
    away = jax.ShapeDtypeStruct((TOKENS, WIDTH), BF16)
    outs = [away] if got is None else [own, own, own, ends]
    extra = [] if got is None else [got]
    return pl.pallas_call(
        kernel,
        grid=(4,),
        in_specs=[pl.BlockSpec((TOKENS, cots.shape[1]), lambda m: (half, 0))]
        + [block(n) for n in range(TILES)]
        + [pl.BlockSpec((TOKENS, BLOCK_ROWS), lambda m: (0, m)) for _ in extra]
        + [pl.BlockSpec(memory_space=pl.ANY) for _ in done],
        out_specs=[pl.BlockSpec((out.shape[0], BLOCK_ROWS), lambda m: (0, m)) for out in outs],
        out_shape=outs,
        compiler_params=pltpu.CompilerParams(vmem_limit_bytes=48 * 1024 * 1024),
        cost_estimate=cost(5),
        name="ffn_back",
    )(cots, *[weights] * TILES, *extra, *done)


def mixer_out_kernel(pieces_ref, query_ref, key_ref, value_ref, slot_ref, out_ref):
    slots = []
    for head in range(4):
        block = pieces_ref[head].astype(F32) + pieces_ref[4 + head].astype(F32)
        columns = slice(head * HEAD_DIM, (head + 1) * HEAD_DIM)
        for i, ref in enumerate((query_ref, key_ref, value_ref)):
            ref[:, columns] = block[:, i * HEAD_DIM : (i + 1) * HEAD_DIM]
        slots.append(block[:, 3 * HEAD_DIM : 3 * HEAD_DIM + SLOTS])
        out_ref[:, columns] = block[:, WIDE:]
    slot_ref[...] = jnp.concatenate(slots, axis=1)


def mixer_out(pieces):
    rows = pieces.shape[1]
    widths = (WIDTH, WIDTH, WIDTH, ALL_SLOTS, WIDTH)
    return pl.pallas_call(
        mixer_out_kernel,
        in_specs=[pl.BlockSpec(memory_space=pltpu.VMEM)],
        out_specs=[pl.BlockSpec(memory_space=pltpu.VMEM)] * 5,
        out_shape=[jax.ShapeDtypeStruct((rows, width), F32) for width in widths],
        cost_estimate=cost(2),
        name="mixer_out",
    )(pieces)


def to_plane(value):
    parts = []
    for y in range(4):
        for z in range(4):
            for side in range(2):
                start = y * 8 * CHUNK + side * 4 * CHUNK + z * CHUNK
                parts.append(value[:, start : start + CHUNK])
    return jnp.concatenate(parts, axis=1)


def from_plane(value):
    parts = []
    for y in range(4):
        for side in range(2):
            for z in range(4):
                start = y * 8 * CHUNK + z * 2 * CHUNK + side * CHUNK
                parts.append(value[:, start : start + CHUNK])
    return jnp.concatenate(parts, axis=1)


def rms_parts(rows):
    root = lax.rsqrt(jnp.mean(rows * rows, axis=1, keepdims=True) + EPS)
    return rows * root, root


def rms_back(incoming, gain, unit, root):
    scaled = incoming * gain
    return root * (scaled - unit * jnp.mean(scaled * unit, axis=1, keepdims=True))


def mix_out_kernel(rank_ref, *refs):
    part_refs = refs[:4]
    weight_ref, input_ref, keep_ref, gain_ref, hidden_ref, ffn_in_ref, mixed_ref = refs[4:]
    step = pl.program_id(0)
    for k in range(4):

        @pl.when(step == k)
        def _():
            part = part_refs[k][...]
            place = pl.multiple_of((rank_ref[0] ^ k) * HEAD_DIM, HEAD_DIM)
            mixed_ref[:, pl.ds(place, HEAD_DIM)] = part
            product = mm(part, weight_ref[...])
            hidden_ref[...] = product if k == 0 else hidden_ref[...] + product

    @pl.when(step == 3)
    def _():
        hidden = input_ref[...].astype(F32) + keep_ref[...] * hidden_ref[...]
        hidden_ref[...] = hidden
        ffn_in_ref[...] = to_plane((rms_parts(hidden)[0] * gain_ref[...]).astype(BF16))


def mix_out(rank, parts, out_weight, block_input, keep, gain):
    def fixed(shape):
        return pl.BlockSpec(shape, lambda k, rank: (0, 0))

    own = (ROWS_OWN, WIDTH)
    return pl.pallas_call(
        mix_out_kernel,
        grid_spec=pltpu.PrefetchScalarGridSpec(
            num_scalar_prefetch=1,
            grid=(4,),
            in_specs=[fixed((ROWS_OWN, HEAD_DIM))] * 4
            + [
                pl.BlockSpec((HEAD_DIM, WIDTH), lambda k, rank: (rank[0] ^ k, 0)),
                fixed(own),
                fixed((ROWS_OWN, 1)),
                fixed((1, WIDTH)),
            ],
            out_specs=[fixed(own)] * 3,
        ),
        out_shape=[
            jax.ShapeDtypeStruct(own, F32),
            jax.ShapeDtypeStruct(own, BF16),
            jax.ShapeDtypeStruct(own, BF16),
        ],
        compiler_params=pltpu.CompilerParams(
            vmem_limit_bytes=48 * 1024 * 1024, dimension_semantics=("arbitrary",)
        ),
        cost_estimate=cost(6),
        name="mix_out",
    )(rank, *parts, out_weight, block_input, keep, gain)


def norm_back_kernel(
    own_ref, left_ref, right_ref, cot_ref, hidden_ref, keep_ref, gain_ref,
    hidden_cot_ref, branch_ref, gain_cot_ref,
):
    incoming = own_ref[...] + left_ref[...].astype(F32) + right_ref[...].astype(F32)
    incoming = from_plane(incoming)
    unit, root = rms_parts(hidden_ref[...])
    hidden_cot = cot_ref[...].astype(F32) + rms_back(incoming, gain_ref[...], unit, root)
    hidden_cot_ref[...] = hidden_cot
    branch_ref[...] = (keep_ref[...] * hidden_cot).astype(BF16)
    gain_cot_ref[...] = jnp.sum(incoming * unit, axis=0, keepdims=True)


def block_out_kernel(own_ref, left_ref, right_ref, hidden_ref, keep_ref, out_ref):
    down = own_ref[...] + left_ref[...].astype(F32) + right_ref[...].astype(F32)
    out_ref[...] = hidden_ref[...] + keep_ref[...] * from_plane(down)


def input_back_kernel(own_ref, near_ref, far_ref, input_ref, hidden_cot_ref, gain_ref, out_ref):
    incoming = own_ref[...].astype(F32) + near_ref[...].astype(F32) + far_ref[...].astype(F32)
    unit, root = rms_parts(input_ref[...].astype(F32))
    out_ref[...] = hidden_cot_ref[...] + rms_back(incoming, gain_ref[...], unit, root)


def own_rows(kernel, arrays, outs, name):
    def spec(shape):
        return pl.BlockSpec((min(shape[0], ROWS_OWN), shape[1]), lambda i: (0, 0))

    return pl.pallas_call(
        kernel,
        grid=(1,),
        in_specs=[spec(array.shape) for array in arrays],
        out_specs=[spec(shape) for shape, _ in outs],
        out_shape=[jax.ShapeDtypeStruct(shape, dtype) for shape, dtype in outs],
        compiler_params=pltpu.CompilerParams(vmem_limit_bytes=32 * 1024 * 1024),
        cost_estimate=cost(3),
        name=name,
    )(*arrays)


def norm_back(*arrays):
    own = (ROWS_OWN, WIDTH)
    return own_rows(
        norm_back_kernel, arrays, [(own, F32), (own, BF16), ((1, WIDTH), F32)], "norm_back"
    )


def block_out(*arrays):
    return own_rows(block_out_kernel, arrays, [((ROWS_OWN, WIDTH), F32)], "block_out")[0]


def input_back(*arrays):
    return own_rows(input_back_kernel, arrays, [((ROWS_OWN, WIDTH), F32)], "input_back")[0]


def halves_kernel(side_ref, gate_ref, up_ref, down_ref, keep_ref, give_ref):
    rows = gate_ref.shape[0]
    part = gate_ref.shape[1] // 2
    padding = jnp.zeros((rows, HIDDEN - part), BF16)
    down = down_ref[...]
    for half in range(2):
        cut = slice(half * part, (half + 1) * part)
        gate, up, turned = [
            jnp.concatenate([value, padding], axis=1)
            for value in (gate_ref[:, cut], up_ref[:, cut], down[:, cut])
        ]
        tiles = []
        for n in range(TILES):
            tiles += [value[:, n * TILE : (n + 1) * TILE] for value in (gate, up, turned)]
        packed = jnp.concatenate(tiles, axis=1)

        @pl.when(side_ref[0] == half)
        def _():
            keep_ref[...] = packed

        @pl.when(side_ref[0] != half)
        def _():
            give_ref[...] = packed


def weight_halves(side, gate_weight, up_weight, down_weight):
    shape = jax.ShapeDtypeStruct((gate_weight.shape[0], 3 * HIDDEN), BF16)
    return pl.pallas_call(
        halves_kernel,
        in_specs=[RANK_SPEC] + [pl.BlockSpec(memory_space=pltpu.VMEM)] * 3,
        out_specs=[pl.BlockSpec(memory_space=pltpu.VMEM)] * 2,
        out_shape=[shape, shape],
        cost_estimate=cost(2),
        name="weight_halves",
    )(side, gate_weight, up_weight, down_weight)


def turn_kernel(rows_ref, keep_ref, out_ref):
    kept = rows_ref[...].astype(F32) * keep_ref[...]
    out_ref[...] = to_plane(kept.astype(BF16))


def turn_rows(rows, keep):
    return own_rows(turn_kernel, [rows, keep], [(rows.shape, BF16)], "turn_rows")[0]


AXES = ("y", "xh", "z", "xl", "c")
DP = ("y", "xh", "z")
MP = ("xl", "c")
RING = ("xh", "xl")
PLANE = ("y", "z")
SWAP = ((0, 1), (1, 0))


def tied(value, token):
    return value + (0.0 * token[0, 0]).astype(value.dtype)


def after(value, *first):
    return lax.optimization_barrier((value,) + first)[0]


def other_core(value):
    return lax.ppermute(value, "c", SWAP)


def other_chip(value):
    return lax.ppermute(value, "xl", SWAP)


def along_ring(value, step):
    return lax.ppermute(value, RING, [(i, (i + step) % 4) for i in range(4)])


def gather_sides(own):
    return along_ring(own, 1), along_ring(own, -1), other_core(own)


def gather_ends(left, right):
    half = left.shape[0] // 2
    return along_ring(left[:half], 1), along_ring(right[half:], -1)


def ring_opposite(opposite):
    half = opposite.shape[0] // 2
    return along_ring(opposite[:half], 1), along_ring(opposite[half:], -1)


def ring_sides(left, right, from_left, from_right):
    half = left.shape[0] // 2
    right = jnp.concatenate([right[:half] + from_left.astype(F32), right[half:]], axis=0)
    left = jnp.concatenate([left[:half], left[half:] + from_right.astype(F32)], axis=0)
    return left.astype(BF16), right.astype(BF16)


def ring_send(left, right):
    return along_ring(right, 1), along_ring(left, -1)


def add(left, right):
    return (left.astype(F32) + right.astype(F32)).astype(BF16)


def on_device(
    block_input,
    cotangent,
    pad_mask,
    seq_counts,
    gain_mix,
    query_weight,
    key_weight,
    value_weight,
    slot_weight,
    out_weight,
    gain_ffn,
    gate_weight,
    up_weight,
    down_weight,
):
    rows_own, width = block_input.shape
    rank = lax.axis_index(MP)
    side = lax.axis_index("xh")
    live = (jnp.arange(SEQS) < seq_counts[0]).astype(jnp.int32)
    keep_seq = (pad_mask[0] * live[:, None]).astype(F32)
    keep_own = lax.dynamic_slice_in_dim(keep_seq, rank * RUN, RUN, 1).reshape(rows_own, 1)

    rank_array = rank.reshape(1).astype(jnp.int32)

    hidden_part = gate_weight.shape[1] // 2
    kept, given = weight_halves(
        side.reshape(1).astype(jnp.int32), gate_weight, up_weight, down_weight.T
    )
    got = lax.ppermute(given, "xh", SWAP)
    paired = jnp.concatenate(
        [jnp.where(side == 0, kept, got), jnp.where(side == 0, got, kept)], axis=0
    )
    weights = lax.all_gather(paired, PLANE, axis=0, tiled=True)

    far = other_chip(after(block_input, got))
    cot_start = turn_rows(cotangent, keep_own)
    mixer_weights = (query_weight, key_weight, value_weight, slot_weight)
    near_input = other_core(block_input)
    keep_column = keep_seq[:, :, None]
    near_pre, near_normed, done = project_near(
        rank_array, (block_input, near_input), gain_mix[None], mixer_weights
    )
    farthest = other_core(tied(far, done))
    cot_sides = gather_sides(tied(cot_start, done))
    pre, normed_four, *blocks, mixing, probs, past = project_mix(
        rank_array, (far, farthest), gain_mix[None], mixer_weights,
        near_pre, near_normed, keep_column,
    )
    corner = cot_sides[0][:8, :128] + cot_sides[1][:8, :128] + blocks[0][:8, :128]
    mixed_parts = (
        blocks[0],
        other_core(blocks[1]),
        other_chip(tied(blocks[2], corner)),
        lax.ppermute(blocks[3], MP, [(i, 3 - i) for i in range(4)]),
    )
    corner = mixed_parts[2][:8, :128] + mixed_parts[3][:8, :128]
    cot_ends = gather_ends(tied(cot_sides[0], corner), tied(cot_sides[1], corner))
    hidden, ffn_own, mixed_own = mix_out(
        rank_array, mixed_parts, out_weight, block_input, keep_own, gain_ffn[None]
    )
    sides = gather_sides(ffn_own)
    ends = gather_ends(*sides[:2])
    arrays = [ffn_own, *sides[:2], *ends, cot_start, *cot_sides[:2], *cot_ends]
    arrays += [sides[2], *map(other_core, sides[:2]), *map(other_core, ends)]
    arrays += [cot_sides[2], *map(other_core, cot_sides[:2]), *map(other_core, cot_ends)]
    plan = [
        [(core + 5 * kind + i, 0, arrays[i].shape[0]) for core in (0, 10) for i in range(5)]
        for kind in range(2)
    ]
    inner, cots, grads = ffn(arrays, plan, weights)
    ffn_sums = lax.psum_scatter(grads, PLANE, scatter_dimension=0, tiled=True)
    (away,) = ffn_back(cots, weights, pair_block, 1)
    (late_away,) = ffn_back(after(inner, away), weights, down_block, 1)
    got = other_core(away)
    own, left, right, ends = ffn_back(cots, weights, pair_block, 0, after(got, late_away))
    mixed_far = other_chip(tied(mixed_own, away))
    (late_near,) = ffn_back(
        after(inner, ends), weights, down_block, 0, done=(mixed_far, ends)
    )
    from_left, from_right, late_near = lax.optimization_barrier(
        ring_opposite(ends) + (late_near,)
    )
    left, right = ring_sides(left, right, from_left, from_right)
    from_left, from_right = ring_send(left, right)
    hidden_cot, branch_cot, gain_ffn_part = norm_back(
        own, from_left, from_right, cotangent, hidden, keep_own, gain_ffn[None]
    )
    branch_near = other_core(branch_cot)
    branch_far = other_chip(branch_cot)
    branch = (branch_cot, branch_near, branch_far, other_core(branch_far))
    head_cots = mixer_backward(
        rank_array, pre, keep_column, mixing, probs, past, out_weight, branch
    )
    mixed_all = (mixed_own, other_core(mixed_own), mixed_far, other_core(mixed_far))
    mixer_sums = lax.psum_scatter(
        mixer_grads(rank_array, normed_four, head_cots, mixed_all, branch),
        PLANE,
        scatter_dimension=0,
        tiled=True,
    )

    own, near, far, farthest, gain_mix_part = unproject(
        rank_array, after(head_cots, mixed_all[3]), normed_four, *mixer_weights
    )
    near = other_core(near)
    far = add(far, other_core(farthest))
    late_got = other_core(tied(late_away, gain_mix_part))
    gain_sums = jnp.stack([gain_mix_part[0] / gain_mix, gain_ffn_part[0]]).reshape(32, 128)
    for axis in ("c", "xl", "xh"):
        gain_sums = gain_sums + lax.ppermute(gain_sums, axis, SWAP)
    far = other_chip(tied(far, gain_sums))
    late_near = late_near.astype(F32) + late_got.astype(F32)
    late_own, late_left, late_right, late_ends = jnp.split(late_near, 4, axis=0)
    late_ends = ring_opposite(late_ends.astype(BF16))
    for axis in PLANE:
        for step in (1, 2):
            gain_sums = gain_sums + lax.ppermute(
                gain_sums, axis, [(i, i ^ step) for i in range(4)]
            )
    late_sides = ring_send(*ring_sides(late_left, late_right, *late_ends))
    gain_sums = gain_sums.reshape(2, width)
    input_grad = input_back(own, near, far, block_input, hidden_cot, gain_mix[None])
    block_output = block_out(late_own, *late_sides, hidden, keep_own)
    kept = lax.dynamic_slice_in_dim(ffn_sums, side * CHUNK, CHUNK, 0)
    given_back = lax.ppermute(
        lax.dynamic_slice_in_dim(ffn_sums, (1 - side) * CHUNK, CHUNK, 0), "xh", SWAP
    )
    mixer_sums, block_output, input_grad, gain_sums, given_back = lax.optimization_barrier(
        (mixer_sums, block_output, input_grad, gain_sums, given_back)
    )
    rows_out = rows_own // 8
    pieces = lax.all_to_all(
        mixer_sums.reshape(8, rows_out, COLUMNS), ("xh", "xl", "c"), 0, 0
    )
    query_grad, key_grad, value_grad, slot_grad, out_grad = mixer_out(pieces)

    def finish(tiles):
        mine, theirs = [
            jnp.concatenate([grads[:, n * TILE : (n + 1) * TILE] for n in tiles], axis=1)[
                :, :hidden_part
            ]
            for grads in (kept, given_back)
        ]
        return jnp.concatenate(
            [jnp.where(side == 0, mine, theirs), jnp.where(side == 0, theirs, mine)], axis=1
        ).astype(F32)

    return (
        block_output,
        input_grad,
        gain_sums[0],
        query_grad,
        key_grad,
        value_grad,
        slot_grad,
        out_grad,
        gain_sums[1],
        finish((0, 3, 6)),
        finish((1, 4, 7)),
        finish((2, 5, 8)).T,
    )


def solution(mesh):
    fine = jax.sharding.Mesh(mesh.devices.reshape(4, 2, 4, 2, 2), AXES)
    rows = P(AXES, None)
    return jax.shard_map(
        on_device,
        mesh=fine,
        in_specs=(
            rows,
            rows,
            P(DP, None, None),
            P(DP),
            P(),
            P(),
            P(),
            P(),
            P(),
            P(),
            P(),
            P(DP, MP),
            P(DP, MP),
            P(MP, DP),
        ),
        out_specs=(
            rows,
            rows,
            P(),
            rows,
            rows,
            rows,
            rows,
            rows,
            P(),
            P(DP, MP),
            P(DP, MP),
            P(MP, DP),
        ),
        check_vma=False,
    )
```

```python
import functools

import jax
import jax.numpy as jnp
from jax import lax
from jax.experimental import pallas as pl
from jax.experimental.pallas import tpu as pltpu
from jax.sharding import PartitionSpec as P

HEAD_DIM = 512
SLOTS = 64
LENGTH = 256
RUN = 64
RUNS = 4
SEQS = 2
LEVELS = (128, 64, 32, 16, 8, 4, 2, 1)
SCALE = HEAD_DIM ** (-0.5)
GATE_SCALE = 0.125
F32 = jnp.float32
BF16 = jnp.bfloat16


def mm(left, right):
    return jnp.dot(left, right, preferred_element_type=F32)


def mm_cols(left, right):
    return lax.dot_general(left, right, (((1,), (1,)), ((), ())), preferred_element_type=F32)


def mm_rows(left, right):
    return lax.dot_general(left, right, (((0,), (0,)), ((), ())), preferred_element_type=F32)


def halves(value):
    high = value.astype(BF16)
    return high, (value - high.astype(F32)).astype(BF16)


def fine_product(left, right):
    left_high, left_low = halves(left)
    right_high, right_low = halves(right)
    rows, width = left.shape[0], right.shape[1]
    out = mm(
        jnp.concatenate([left_high, left_low], axis=0),
        jnp.concatenate([right_high, right_low], axis=1),
    )
    return out[:rows, :width] + out[:rows, width:] + out[rows:, :width]


def fine_cols_product(left, right):
    left_high, left_low = halves(left)
    right_high, right_low = halves(right)
    return mm_cols(
        jnp.concatenate([left_high, left_low, left_high], axis=1),
        jnp.concatenate([right_high, right_high, right_low], axis=1),
    )


def decay_tables(slot_pre, keep):
    log_gate = jnp.minimum(slot_pre, 0.0) - jnp.log1p(jnp.exp(-jnp.abs(slot_pre)))
    log_decay = keep * log_gate * GATE_SCALE
    half = jnp.tanh(-0.5 * log_decay)
    written = 2.0 * half / (1.0 + half)
    rows = lax.broadcasted_iota(jnp.int32, log_decay.shape, 0)
    running = log_decay
    shift = 1
    while shift < LENGTH:
        running = running + jnp.where(rows >= shift, pltpu.roll(running, shift, 0), 0.0)
        shift *= 2
    return log_decay, written, running


def later_sum(value):
    rows = lax.broadcasted_iota(jnp.int32, value.shape, 0)
    shift = 1
    while shift < LENGTH:
        value = value + jnp.where(rows < LENGTH - shift, pltpu.roll(value, LENGTH - shift, 0), 0.0)
        shift *= 2
    return value


def level_factors(running):
    rows = lax.broadcasted_iota(jnp.int32, running.shape, 0)
    last = running
    factors = {}
    size = 1
    while size < LENGTH:
        odd = (rows & size) != 0
        before = pltpu.roll(last, size, 0)
        factor = jnp.exp(jnp.where(odd, running - before, last - running))
        factors[size] = (jnp.where(odd, factor, 0.0), jnp.where(odd, 0.0, factor))
        last = jnp.where(odd, last, pltpu.roll(last, LENGTH - size, 0))
        size *= 2
    return factors


def level_map(flip):
    rows = lax.broadcasted_iota(jnp.int32, (LENGTH, LENGTH), 0)
    cols = lax.broadcasted_iota(jnp.int32, (LENGTH, LENGTH), 1)
    later = rows < cols if flip else rows > cols
    return jnp.where(later, rows ^ cols, 0), rows == cols


def at_level(where_map, size):
    return (where_map >= size) & (where_map < 2 * size)


def gather_rows(ref, rank, seq, start, width):
    parts = []
    for run in range(RUNS):
        first = pl.multiple_of(((rank ^ run) * SEQS + seq) * RUN, RUN)
        parts.append(ref[pl.ds(first, RUN), start : start + width])
    return jnp.concatenate(parts, axis=0)


def spread_rows(ref, rank, seq, start, width, value):
    for run in range(RUNS):
        first = pl.multiple_of(((rank ^ run) * SEQS + seq) * RUN, RUN)
        ref[pl.ds(first, RUN), start : start + width] = value[run * RUN : (run + 1) * RUN]


def sigmoid(value):
    return 1.0 / (1.0 + jnp.exp(-value))


def silu(value):
    return value * sigmoid(value)


def silu_slope(pre):
    sigma = sigmoid(pre)
    return sigma * (1.0 + pre * (1.0 - sigma))


def mix_forward(rank, seq, pre_ref, keep, mixed_ref, mixing_ref, probs_ref, past_ref):
    queries = silu(gather_rows(pre_ref, rank, seq, 0, HEAD_DIM)).astype(BF16)
    keys = silu(gather_rows(pre_ref, rank, seq, HEAD_DIM, HEAD_DIM)).astype(BF16)
    values = gather_rows(pre_ref, rank, seq, 2 * HEAD_DIM, HEAD_DIM).astype(BF16)
    slot_pre = gather_rows(pre_ref, rank, seq, 3 * HEAD_DIM, SLOTS)
    _, written, running = decay_tables(slot_pre, keep)
    factors = level_factors(running)
    where_map, own = level_map(False)
    pairs = mm_cols(queries, keys)
    own_pairs = jnp.sum(jnp.where(own, pairs, 0.0), axis=1, keepdims=True)
    past = jnp.zeros((LENGTH, SLOTS), F32)
    for size in LEVELS:
        after, before = factors[size]
        past = past + after * fine_product(
            jnp.where(at_level(where_map, size), pairs, 0.0), before * written
        )
    past = SCALE * past
    scores = past + SCALE * own_pairs * written
    grown = jnp.exp(scores - jnp.max(scores, axis=1, keepdims=True))
    probs = grown / jnp.sum(grown, axis=1, keepdims=True)
    mixing = jnp.where(own, jnp.sum(probs * written, axis=1, keepdims=True), 0.0)
    for size in LEVELS:
        after, before = factors[size]
        mixing = jnp.where(
            at_level(where_map, size),
            fine_cols_product(probs * after, before * written),
            mixing,
        )
    mixing = mixing.astype(BF16)
    mixed = mm(mixing, values).astype(BF16)
    spread_rows(mixed_ref, rank, seq, 0, HEAD_DIM, mixed)
    mixing_ref[seq] = mixing
    probs_ref[seq] = probs
    past_ref[seq] = past


def mixer_backward_kernel(
    rank_ref, pre_ref, keep_ref, mixing_ref, probs_ref, past_ref, weight_ref,
    own_ref, near_ref, far_ref, farthest_ref, out_ref, cot_ref,
):
    rank = rank_ref[0]
    seq = pl.program_id(0)

    @pl.when(seq == 0)
    def _():
        branch = [ref[...] for ref in (own_ref, near_ref, far_ref, farthest_ref)]
        cot_ref[...] = mm_cols(jnp.concatenate(branch, axis=0), weight_ref[...]).astype(BF16)

    query_pre = gather_rows(pre_ref, rank, seq, 0, HEAD_DIM)
    key_pre = gather_rows(pre_ref, rank, seq, HEAD_DIM, HEAD_DIM)
    queries = silu(query_pre).astype(BF16)
    keys = silu(key_pre).astype(BF16)
    values = gather_rows(pre_ref, rank, seq, 2 * HEAD_DIM, HEAD_DIM).astype(BF16)
    slot_pre = gather_rows(pre_ref, rank, seq, 3 * HEAD_DIM, SLOTS)
    cot = gather_rows(cot_ref, rank, seq, 0, HEAD_DIM)
    keep = keep_ref[0]
    log_decay, written, running = decay_tables(slot_pre, keep)
    factors = level_factors(running)
    where_map, own = level_map(False)
    where_flip, _ = level_map(True)
    probs = probs_ref[0]
    past = past_ref[0]
    mixing = mixing_ref[0]
    spread_rows(
        out_ref, rank, seq, 2 * HEAD_DIM, HEAD_DIM, mm_rows(mixing, cot).astype(BF16)
    )
    pairs_flip = mm_cols(keys, queries) * SCALE
    cot_flip = mm_cols(values, cot)
    mixing_cot = mm_cols(cot, values)
    own_cot = jnp.sum(jnp.where(own, mixing_cot, 0.0), axis=1, keepdims=True)
    own_pairs = jnp.sum(jnp.where(own, pairs_flip, 0.0), axis=1, keepdims=True)
    past_cot = jnp.zeros((LENGTH, SLOTS), F32)
    for size in LEVELS:
        after, before = factors[size]
        past_cot = past_cot + after * fine_product(
            jnp.where(at_level(where_map, size), mixing_cot, 0.0), before * written
        )
    probs_cot = past_cot + own_cot * written
    scores_cot = probs * (probs_cot - jnp.sum(probs * probs_cot, axis=1, keepdims=True))
    row_flow = probs * past_cot + scores_cot * past
    pairs_cot = jnp.where(own, jnp.sum(scores_cot * written, axis=1, keepdims=True), 0.0)
    ahead = jnp.zeros((LENGTH, SLOTS), F32)
    both_flip = jnp.concatenate([cot_flip, pairs_flip], axis=1)
    where_both = jnp.concatenate([where_flip, where_flip], axis=1)
    for size in LEVELS:
        after, before = factors[size]
        pairs_cot = jnp.where(
            at_level(where_map, size),
            fine_cols_product(scores_cot * after, before * written),
            pairs_cot,
        )
        ahead = ahead + before * fine_product(
            jnp.where(at_level(where_both, size), both_flip, 0.0),
            jnp.concatenate([probs * after, scores_cot * after], axis=0),
        )
    pairs_low = (SCALE * pairs_cot).astype(BF16)
    query_cot = (mm(pairs_low, keys) * silu_slope(query_pre)).astype(BF16)
    spread_rows(out_ref, rank, seq, 0, HEAD_DIM, query_cot)
    key_cot = (mm_rows(pairs_low, queries) * silu_slope(key_pre)).astype(BF16)
    spread_rows(out_ref, rank, seq, HEAD_DIM, HEAD_DIM, key_cot)
    running_cot = row_flow - written * ahead
    written_cot = ahead + own_cot * probs + scores_cot * own_pairs
    decay_cot = later_sum(running_cot) - written_cot * jnp.exp(log_decay)
    slot_cot = decay_cot * keep * GATE_SCALE * sigmoid(-slot_pre)
    padded = jnp.concatenate([slot_cot, jnp.zeros((LENGTH, SLOTS), F32)], axis=1).astype(BF16)
    spread_rows(out_ref, rank, seq, 3 * HEAD_DIM, 2 * SLOTS, padded)


def cost(microseconds):
    return pl.CostEstimate(
        flops=int(microseconds * 1.1e9), bytes_accessed=1 << 20, transcendentals=0
    )


def whole(shape):
    zeros = (0,) * len(shape)
    return pl.BlockSpec(shape, lambda seq, rank: zeros)


def one_seq(shape):
    return pl.BlockSpec((1,) + shape, lambda seq, rank: (seq, 0, 0))


TOKENS = RUNS * SEQS * RUN
WIDE = 3 * HEAD_DIM + 2 * SLOTS
WIDTH = 2048
ROWS_OWN = SEQS * RUN
RANK_SPEC = pl.BlockSpec(memory_space=pltpu.SMEM)


def mixer_backward(rank, pre, keep, mixing, probs, past, out_weight, branch):
    return pl.pallas_call(
        mixer_backward_kernel,
        grid_spec=pltpu.PrefetchScalarGridSpec(
            num_scalar_prefetch=1,
            grid=(SEQS,),
            in_specs=[
                whole((TOKENS, WIDE)),
                one_seq((LENGTH, 1)),
                one_seq((LENGTH, LENGTH)),
                one_seq((LENGTH, SLOTS)),
                one_seq((LENGTH, SLOTS)),
                pl.BlockSpec((HEAD_DIM, WIDTH), lambda seq, rank: (rank[0], 0)),
            ]
            + [whole((ROWS_OWN, WIDTH))] * 4,
            out_specs=whole((TOKENS, WIDE)),
            scratch_shapes=[pltpu.VMEM((TOKENS, HEAD_DIM), BF16)],
        ),
        out_shape=jax.ShapeDtypeStruct((TOKENS, WIDE), BF16),
        compiler_params=pltpu.CompilerParams(
            vmem_limit_bytes=48 * 1024 * 1024, dimension_semantics=("arbitrary",)
        ),
        cost_estimate=cost(13),
        name="mixer_backward",
    )(rank, pre, keep, mixing, probs, past, out_weight, *branch)


EPS = 1e-05
K_TILE = 512
ALL_SLOTS = 4 * SLOTS
TILE = 256
TILES = 3
HIDDEN = TILE * TILES


def project_step(step, rank, row_refs, gain, weight_refs, slot_ref, pre_ref, normed_ref, slots_ref, first):
    last = first + 2 * ROWS_OWN

    @pl.when(step == 0)
    def _():
        for i, ref in enumerate(row_refs):
            rows = ref[...].astype(F32)
            root = lax.rsqrt(jnp.mean(rows * rows, axis=1, keepdims=True) + EPS)
            start = first + i * ROWS_OWN
            normed_ref[start : start + ROWS_OWN] = (rows * root * gain).astype(BF16)
        pre_ref[first:last] = jnp.zeros((2 * ROWS_OWN, WIDE), F32)
        slots_ref[...] = jnp.zeros_like(slots_ref)

    left = normed_ref[first:last, pl.ds(pl.multiple_of(step * K_TILE, K_TILE), K_TILE)]
    for i, ref in enumerate(weight_refs):
        pre_ref[first:last, i * HEAD_DIM : (i + 1) * HEAD_DIM] += mm(left, ref[...])
    slots_ref[...] += mm(left, slot_ref[...])

    @pl.when(step == WIDTH // K_TILE - 1)
    def _():
        mine = jnp.zeros((2 * ROWS_OWN, SLOTS), F32)
        for head in range(4):
            mine = jnp.where(rank == head, slots_ref[:, head * SLOTS : (head + 1) * SLOTS], mine)
        pre_ref[first:last, 3 * HEAD_DIM :] = jnp.concatenate([mine, jnp.zeros_like(mine)], axis=1)


def project_near_kernel(
    rank_ref, own_ref, near_ref, gain_ref, query_ref, key_ref, value_ref, slot_ref,
    pre_ref, normed_ref, done_ref, slots_ref,
):
    step = pl.program_id(0)
    project_step(
        step, rank_ref[0], (own_ref, near_ref), gain_ref[...], (query_ref, key_ref, value_ref),
        slot_ref, pre_ref, normed_ref, slots_ref, 0,
    )
    done_ref[...] = jnp.zeros_like(done_ref)


def project_mix_kernel(
    rank_ref, far_ref, farthest_ref, gain_ref, query_ref, key_ref, value_ref, slot_ref,
    near_pre_ref, near_normed_ref, keep_ref,
    pre_ref, normed_ref, first_ref, second_ref, third_ref, fourth_ref,
    mixing_ref, probs_ref, past_ref, slots_ref, mixed_ref,
):
    step = pl.program_id(0)
    half = 2 * ROWS_OWN

    @pl.when(step == 0)
    def _():
        pre_ref[:half] = near_pre_ref[...]
        normed_ref[:half] = near_normed_ref[...]

    project_step(
        step, rank_ref[0], (far_ref, farthest_ref), gain_ref[...], (query_ref, key_ref, value_ref),
        slot_ref, pre_ref, normed_ref, slots_ref, half,
    )

    @pl.when(step == WIDTH // K_TILE - 1)
    def _():
        for seq in range(SEQS):
            mix_forward(
                rank_ref[0], seq, pre_ref, keep_ref[seq], mixed_ref, mixing_ref, probs_ref, past_ref
            )
        for i, ref in enumerate((first_ref, second_ref, third_ref, fourth_ref)):
            ref[...] = mixed_ref[i * ROWS_OWN : (i + 1) * ROWS_OWN]


def project(kernel, rank, pieces, gain, weights, extra, outs, scratch, micros, name):
    def fixed(shape):
        zeros = (0,) * len(shape)
        return pl.BlockSpec(shape, lambda k, rank: zeros)

    weight = pl.BlockSpec((K_TILE, HEAD_DIM), lambda k, rank: (k, rank[0]))
    return pl.pallas_call(
        kernel,
        grid_spec=pltpu.PrefetchScalarGridSpec(
            num_scalar_prefetch=1,
            grid=(WIDTH // K_TILE,),
            in_specs=[fixed(piece.shape) for piece in pieces]
            + [fixed((1, WIDTH)), weight, weight, weight]
            + [pl.BlockSpec((K_TILE, ALL_SLOTS), lambda k, rank: (k, 0))]
            + [fixed(array.shape) for array in extra],
            out_specs=[fixed(shape) for shape, _ in outs],
            scratch_shapes=[pltpu.VMEM((2 * ROWS_OWN, ALL_SLOTS), F32)] + scratch,
        ),
        out_shape=[jax.ShapeDtypeStruct(shape, dtype) for shape, dtype in outs],
        compiler_params=pltpu.CompilerParams(
            vmem_limit_bytes=48 * 1024 * 1024, dimension_semantics=("arbitrary",)
        ),
        cost_estimate=cost(micros),
        name=name,
    )(rank, *pieces, gain, *weights, *extra)


def project_near(rank, pieces, gain, weights):
    half = 2 * ROWS_OWN
    outs = [((half, WIDE), F32), ((half, WIDTH), BF16), ((8, 128), F32)]
    return project(
        project_near_kernel, rank, pieces, gain, weights, (), outs, [], 1, "project_near"
    )


def project_mix(rank, pieces, gain, weights, near_pre, near_normed, keep):
    outs = [((TOKENS, WIDE), F32), ((TOKENS, WIDTH), BF16)]
    outs += [((ROWS_OWN, HEAD_DIM), BF16)] * 4 + [((SEQS, LENGTH, LENGTH), BF16)]
    outs += [((SEQS, LENGTH, SLOTS), F32)] * 2
    return project(
        project_mix_kernel, rank, pieces, gain, weights, (near_pre, near_normed, keep), outs,
        [pltpu.VMEM((TOKENS, HEAD_DIM), BF16)], 13, "project_mix",
    )


def unproject_kernel(
    rank_ref, cots_ref, normed_ref, query_ref, key_ref, value_ref, slot_ref,
    own_ref, near_ref, far_ref, farthest_ref, gain_ref,
):
    total = mm_cols(cots_ref[:, :HEAD_DIM], query_ref[...])
    total += mm_cols(cots_ref[:, HEAD_DIM : 2 * HEAD_DIM], key_ref[...])
    total += mm_cols(cots_ref[:, 2 * HEAD_DIM : 3 * HEAD_DIM], value_ref[...])
    slots = cots_ref[:, 3 * HEAD_DIM : 3 * HEAD_DIM + SLOTS]
    spread = jnp.concatenate(
        [jnp.where(rank_ref[0] == head, slots, jnp.zeros_like(slots)) for head in range(4)],
        axis=1,
    )
    total += mm_cols(spread, slot_ref[...])
    for i, ref in enumerate((own_ref, near_ref, far_ref, farthest_ref)):
        ref[...] = total[i * ROWS_OWN : (i + 1) * ROWS_OWN].astype(BF16)
    gain_ref[...] = jnp.sum(total * normed_ref[...].astype(F32), axis=0, keepdims=True)


def unproject(rank, cots, normed, query_weight, key_weight, value_weight, slot_weight):
    weight = pl.BlockSpec((K_TILE, HEAD_DIM), lambda k, rank: (k, rank[0]))
    rows = pl.BlockSpec((ROWS_OWN, K_TILE), lambda k, rank: (0, k))
    return pl.pallas_call(
        unproject_kernel,
        grid_spec=pltpu.PrefetchScalarGridSpec(
            num_scalar_prefetch=1,
            grid=(WIDTH // K_TILE,),
            in_specs=[
                pl.BlockSpec((TOKENS, WIDE), lambda k, rank: (0, 0)),
                pl.BlockSpec((TOKENS, K_TILE), lambda k, rank: (0, k)),
                weight,
                weight,
                weight,
                pl.BlockSpec((K_TILE, ALL_SLOTS), lambda k, rank: (k, 0)),
            ],
            out_specs=[rows] * 4 + [pl.BlockSpec((1, K_TILE), lambda k, rank: (0, k))],
        ),
        out_shape=[jax.ShapeDtypeStruct((ROWS_OWN, WIDTH), BF16)] * 4
        + [jax.ShapeDtypeStruct((1, WIDTH), F32)],
        compiler_params=pltpu.CompilerParams(
            vmem_limit_bytes=48 * 1024 * 1024, dimension_semantics=("arbitrary",)
        ),
        cost_estimate=cost(7),
        name="unproject",
    )(rank, cots, normed, query_weight, key_weight, value_weight, slot_weight)


ALL_HIDDEN = 3 * HIDDEN
COLUMNS = HEAD_DIM + WIDE
CHUNK = 64
BLOCK_ROWS = WIDTH // 4


def mixer_grads_kernel(*refs):
    normed_ref, cots_ref, out_ref, block_ref = refs[1], refs[2], refs[-2], refs[-1]
    block_ref[:, :WIDE] = mm_rows(normed_ref[...], cots_ref[...]).astype(BF16)
    mixed = jnp.concatenate([ref[...] for ref in refs[3:7]], axis=0)
    branch = jnp.concatenate([ref[...] for ref in refs[7:11]], axis=0)
    block_ref[:, WIDE:] = mm_rows(mixed, branch).astype(BF16)
    for side in range(2):
        for z in range(4):
            source = (side * 4 + z) * CHUNK
            target = (z * 2 + side) * CHUNK
            out_ref[target : target + CHUNK] = block_ref[source : source + CHUNK]


def mixer_grads(rank, normed, cots, mixed, branch):
    return pl.pallas_call(
        mixer_grads_kernel,
        grid_spec=pltpu.PrefetchScalarGridSpec(
            num_scalar_prefetch=1,
            grid=(4,),
            in_specs=[
                pl.BlockSpec((TOKENS, BLOCK_ROWS), lambda y, rank: (0, y)),
                pl.BlockSpec((TOKENS, WIDE), lambda y, rank: (0, 0)),
            ]
            + [pl.BlockSpec((ROWS_OWN, BLOCK_ROWS), lambda y, rank: (0, y))] * 4
            + [pl.BlockSpec((ROWS_OWN, HEAD_DIM), lambda y, rank: (0, rank[0]))] * 4,
            out_specs=pl.BlockSpec((BLOCK_ROWS, COLUMNS), lambda y, rank: (y, 0)),
            scratch_shapes=[pltpu.VMEM((BLOCK_ROWS, COLUMNS), BF16)],
        ),
        out_shape=jax.ShapeDtypeStruct((WIDTH, COLUMNS), BF16),
        compiler_params=pltpu.CompilerParams(
            vmem_limit_bytes=56 * 1024 * 1024, dimension_semantics=("arbitrary",)
        ),
        cost_estimate=cost(10),
        name="mixer_grads",
    )(rank, normed, cots, *mixed, *branch)


def ffn_kernel(plan, *refs):
    weight_ref, inner_ref, cots_ref, grads_ref, rows_ref, sems = refs[-6:]
    step = pl.program_id(0)

    def copies(side):
        start = 0
        made = []
        for i, (at, first, rows) in enumerate(plan[side]):
            source = refs[at].at[pl.ds(first, rows)]
            place = rows_ref.at[side, pl.ds(start, rows)]
            made.append(pltpu.make_async_copy(source, place, sems.at[side, i]))
            start += rows
        return made

    @pl.when(step == 0)
    def _():
        for copy in copies(0) + copies(1):
            copy.start()
        for copy in copies(0):
            copy.wait()

    def halves_of(side, columns):
        return [
            mm(rows_ref[side, half * TOKENS : (half + 1) * TOKENS], weight_ref[:, columns])
            for half in range(2)
        ]

    both = halves_of(0, slice(0, 2 * TILE))

    @pl.when(step == 0)
    def _():
        for copy in copies(1):
            copy.wait()

    inner_cots = halves_of(1, slice(2 * TILE, 3 * TILE))
    for half in range(2):
        rows = slice(half * TOKENS, (half + 1) * TOKENS)
        gate_pre, up_pre = both[half][:, :TILE], both[half][:, TILE:]
        inner_cot = inner_cots[half]
        sigma = sigmoid(gate_pre)
        gate_act = gate_pre * sigma
        inner_ref[rows] = (gate_act * up_pre).astype(BF16)
        slope = sigma * (1.0 + gate_pre * (1.0 - sigma))
        cots_ref[rows, :TILE] = (inner_cot * up_pre * slope).astype(BF16)
        cots_ref[rows, TILE:] = (inner_cot * gate_act).astype(BF16)
    for m in range(4):
        cut = slice(m * BLOCK_ROWS, (m + 1) * BLOCK_ROWS)
        grads_ref[cut, : 2 * TILE] = mm_rows(rows_ref[0, :, cut], cots_ref[...]).astype(BF16)
        grads_ref[cut, 2 * TILE :] = mm_rows(rows_ref[1, :, cut], inner_ref[...]).astype(BF16)


def ffn(arrays, plan, weights):
    both = 2 * TOKENS
    return pl.pallas_call(
        functools.partial(ffn_kernel, plan),
        grid=(TILES,),
        in_specs=[pl.BlockSpec(memory_space=pl.ANY)] * len(arrays)
        + [pl.BlockSpec((WIDTH, 3 * TILE), lambda n: (0, n))],
        out_specs=[
            pl.BlockSpec((both, TILE), lambda n: (0, n)),
            pl.BlockSpec((both, 2 * TILE), lambda n: (0, n)),
            pl.BlockSpec((WIDTH, 3 * TILE), lambda n: (0, n)),
        ],
        out_shape=[
            jax.ShapeDtypeStruct((both, HIDDEN), BF16),
            jax.ShapeDtypeStruct((both, 2 * HIDDEN), BF16),
            jax.ShapeDtypeStruct((WIDTH, ALL_HIDDEN), BF16),
        ],
        scratch_shapes=[
            pltpu.VMEM((2, both, WIDTH), BF16),
            pltpu.SemaphoreType.DMA((2, len(plan[0]))),
        ],
        compiler_params=pltpu.CompilerParams(
            vmem_limit_bytes=56 * 1024 * 1024, dimension_semantics=("arbitrary",)
        ),
        cost_estimate=cost(24),
        name="ffn",
    )(*arrays, weights)


def back_product(cots_ref, weight_refs):
    total = None
    width = cots_ref.shape[1] // TILES
    for n, ref in enumerate(weight_refs):
        term = mm_cols(cots_ref[:, n * width : (n + 1) * width], ref[...])
        total = term if total is None else total + term
    return total


def away_kernel(cots_ref, *refs):
    refs[-1][...] = back_product(cots_ref, refs[:TILES]).astype(BF16)


def near_kernel(cots_ref, *refs):
    total = back_product(cots_ref, refs[:TILES]) + refs[TILES][...].astype(F32)
    for i, ref in enumerate(refs[-4:]):
        ref[...] = total[i * ROWS_OWN : (i + 1) * ROWS_OWN].astype(ref.dtype)


def pair_block(n):
    return pl.BlockSpec(
        (pl.Element(BLOCK_ROWS), pl.Element(2 * TILE)),
        lambda m: (m * BLOCK_ROWS, n * 3 * TILE),
    )


def down_block(n):
    return pl.BlockSpec((BLOCK_ROWS, TILE), lambda m: (m, 3 * n + 2))


def ffn_back(cots, weights, block, half, got=None, done=()):
    kernel = away_kernel if got is None else near_kernel
    own = jax.ShapeDtypeStruct((ROWS_OWN, WIDTH), F32)
    ends = jax.ShapeDtypeStruct((ROWS_OWN, WIDTH), BF16)
    away = jax.ShapeDtypeStruct((TOKENS, WIDTH), BF16)
    outs = [away] if got is None else [own, own, own, ends]
    extra = [] if got is None else [got]
    return pl.pallas_call(
        kernel,
        grid=(4,),
        in_specs=[pl.BlockSpec((TOKENS, cots.shape[1]), lambda m: (half, 0))]
        + [block(n) for n in range(TILES)]
        + [pl.BlockSpec((TOKENS, BLOCK_ROWS), lambda m: (0, m)) for _ in extra]
        + [pl.BlockSpec(memory_space=pl.ANY) for _ in done],
        out_specs=[pl.BlockSpec((out.shape[0], BLOCK_ROWS), lambda m: (0, m)) for out in outs],
        out_shape=outs,
        compiler_params=pltpu.CompilerParams(vmem_limit_bytes=48 * 1024 * 1024),
        cost_estimate=cost(5),
        name="ffn_back",
    )(cots, *[weights] * TILES, *extra, *done)


def mixer_out_kernel(pieces_ref, query_ref, key_ref, value_ref, slot_ref, out_ref):
    slots = []
    for head in range(4):
        block = pieces_ref[head].astype(F32) + pieces_ref[4 + head].astype(F32)
        columns = slice(head * HEAD_DIM, (head + 1) * HEAD_DIM)
        for i, ref in enumerate((query_ref, key_ref, value_ref)):
            ref[:, columns] = block[:, i * HEAD_DIM : (i + 1) * HEAD_DIM]
        slots.append(block[:, 3 * HEAD_DIM : 3 * HEAD_DIM + SLOTS])
        out_ref[:, columns] = block[:, WIDE:]
    slot_ref[...] = jnp.concatenate(slots, axis=1)


def mixer_out(pieces):
    rows = pieces.shape[1]
    widths = (WIDTH, WIDTH, WIDTH, ALL_SLOTS, WIDTH)
    return pl.pallas_call(
        mixer_out_kernel,
        grid=(1,),
        in_specs=[pl.BlockSpec(pieces.shape, lambda i: (0, 0, 0))],
        out_specs=[pl.BlockSpec((rows, width), lambda i: (0, 0)) for width in widths],
        out_shape=[jax.ShapeDtypeStruct((rows, width), F32) for width in widths],
        cost_estimate=cost(2),
        name="mixer_out",
    )(pieces)


def to_plane(value):
    parts = []
    for y in range(4):
        for z in range(4):
            for side in range(2):
                start = y * 8 * CHUNK + side * 4 * CHUNK + z * CHUNK
                parts.append(value[:, start : start + CHUNK])
    return jnp.concatenate(parts, axis=1)


def from_plane(value):
    parts = []
    for y in range(4):
        for side in range(2):
            for z in range(4):
                start = y * 8 * CHUNK + z * 2 * CHUNK + side * CHUNK
                parts.append(value[:, start : start + CHUNK])
    return jnp.concatenate(parts, axis=1)


def rms_parts(rows):
    root = lax.rsqrt(jnp.mean(rows * rows, axis=1, keepdims=True) + EPS)
    return rows * root, root


def rms_back(incoming, gain, unit, root):
    scaled = incoming * gain
    return root * (scaled - unit * jnp.mean(scaled * unit, axis=1, keepdims=True))


def mix_out_kernel(rank_ref, *refs):
    part_refs = refs[:4]
    weight_ref, input_ref, keep_ref, gain_ref, hidden_ref, ffn_in_ref, mixed_ref = refs[4:]
    step = pl.program_id(0)
    for k in range(4):

        @pl.when(step == k)
        def _():
            part = part_refs[k][...]
            place = pl.multiple_of((rank_ref[0] ^ k) * HEAD_DIM, HEAD_DIM)
            mixed_ref[:, pl.ds(place, HEAD_DIM)] = part
            product = mm(part, weight_ref[...])
            hidden_ref[...] = product if k == 0 else hidden_ref[...] + product

    @pl.when(step == 3)
    def _():
        hidden = input_ref[...].astype(F32) + keep_ref[...] * hidden_ref[...]
        hidden_ref[...] = hidden
        ffn_in_ref[...] = to_plane((rms_parts(hidden)[0] * gain_ref[...]).astype(BF16))


def mix_out(rank, parts, out_weight, block_input, keep, gain):
    def fixed(shape):
        return pl.BlockSpec(shape, lambda k, rank: (0, 0))

    own = (ROWS_OWN, WIDTH)
    return pl.pallas_call(
        mix_out_kernel,
        grid_spec=pltpu.PrefetchScalarGridSpec(
            num_scalar_prefetch=1,
            grid=(4,),
            in_specs=[fixed((ROWS_OWN, HEAD_DIM))] * 4
            + [
                pl.BlockSpec((HEAD_DIM, WIDTH), lambda k, rank: (rank[0] ^ k, 0)),
                fixed(own),
                fixed((ROWS_OWN, 1)),
                fixed((1, WIDTH)),
            ],
            out_specs=[fixed(own)] * 3,
        ),
        out_shape=[
            jax.ShapeDtypeStruct(own, F32),
            jax.ShapeDtypeStruct(own, BF16),
            jax.ShapeDtypeStruct(own, BF16),
        ],
        compiler_params=pltpu.CompilerParams(
            vmem_limit_bytes=48 * 1024 * 1024, dimension_semantics=("arbitrary",)
        ),
        cost_estimate=cost(6),
        name="mix_out",
    )(rank, *parts, out_weight, block_input, keep, gain)


def norm_back_kernel(
    own_ref, left_ref, right_ref, cot_ref, hidden_ref, keep_ref, gain_ref,
    hidden_cot_ref, branch_ref, gain_cot_ref,
):
    incoming = own_ref[...] + left_ref[...].astype(F32) + right_ref[...].astype(F32)
    incoming = from_plane(incoming)
    unit, root = rms_parts(hidden_ref[...])
    hidden_cot = cot_ref[...].astype(F32) + rms_back(incoming, gain_ref[...], unit, root)
    hidden_cot_ref[...] = hidden_cot
    branch_ref[...] = (keep_ref[...] * hidden_cot).astype(BF16)
    gain_cot_ref[...] = jnp.sum(incoming * unit, axis=0, keepdims=True)


def block_out_kernel(own_ref, left_ref, right_ref, hidden_ref, keep_ref, out_ref):
    down = own_ref[...] + left_ref[...].astype(F32) + right_ref[...].astype(F32)
    out_ref[...] = hidden_ref[...] + keep_ref[...] * from_plane(down)


def input_back_kernel(own_ref, near_ref, far_ref, input_ref, hidden_cot_ref, gain_ref, out_ref):
    incoming = own_ref[...].astype(F32) + near_ref[...].astype(F32) + far_ref[...].astype(F32)
    unit, root = rms_parts(input_ref[...].astype(F32))
    out_ref[...] = hidden_cot_ref[...] + rms_back(incoming, gain_ref[...], unit, root)


def own_rows(kernel, arrays, outs, name):
    def spec(shape):
        return pl.BlockSpec((min(shape[0], ROWS_OWN), shape[1]), lambda i: (0, 0))

    return pl.pallas_call(
        kernel,
        grid=(1,),
        in_specs=[spec(array.shape) for array in arrays],
        out_specs=[spec(shape) for shape, _ in outs],
        out_shape=[jax.ShapeDtypeStruct(shape, dtype) for shape, dtype in outs],
        compiler_params=pltpu.CompilerParams(vmem_limit_bytes=32 * 1024 * 1024),
        cost_estimate=cost(3),
        name=name,
    )(*arrays)


def norm_back(*arrays):
    own = (ROWS_OWN, WIDTH)
    return own_rows(
        norm_back_kernel, arrays, [(own, F32), (own, BF16), ((1, WIDTH), F32)], "norm_back"
    )


def block_out(*arrays):
    return own_rows(block_out_kernel, arrays, [((ROWS_OWN, WIDTH), F32)], "block_out")[0]


def input_back(*arrays):
    return own_rows(input_back_kernel, arrays, [((ROWS_OWN, WIDTH), F32)], "input_back")[0]


def halves_kernel(side_ref, gate_ref, up_ref, down_ref, keep_ref, give_ref):
    rows = gate_ref.shape[0]
    part = gate_ref.shape[1] // 2
    padding = jnp.zeros((rows, HIDDEN - part), BF16)
    down = down_ref[...]
    for half in range(2):
        cut = slice(half * part, (half + 1) * part)
        gate, up, turned = [
            jnp.concatenate([value, padding], axis=1)
            for value in (gate_ref[:, cut], up_ref[:, cut], down[:, cut])
        ]
        tiles = []
        for n in range(TILES):
            tiles += [value[:, n * TILE : (n + 1) * TILE] for value in (gate, up, turned)]
        packed = jnp.concatenate(tiles, axis=1)

        @pl.when(side_ref[0] == half)
        def _():
            keep_ref[...] = packed

        @pl.when(side_ref[0] != half)
        def _():
            give_ref[...] = packed


def weight_halves(side, gate_weight, up_weight, down_weight):
    shape = jax.ShapeDtypeStruct((gate_weight.shape[0], 3 * HIDDEN), BF16)
    return pl.pallas_call(
        halves_kernel,
        in_specs=[RANK_SPEC] + [pl.BlockSpec(memory_space=pltpu.VMEM)] * 3,
        out_specs=[pl.BlockSpec(memory_space=pltpu.VMEM)] * 2,
        out_shape=[shape, shape],
        cost_estimate=cost(2),
        name="weight_halves",
    )(side, gate_weight, up_weight, down_weight)


def turn_kernel(rows_ref, keep_ref, out_ref):
    kept = rows_ref[...].astype(F32) * keep_ref[...]
    out_ref[...] = to_plane(kept.astype(BF16))


def turn_rows(rows, keep):
    return own_rows(turn_kernel, [rows, keep], [(rows.shape, BF16)], "turn_rows")[0]


AXES = ("y", "xh", "z", "xl", "c")
DP = ("y", "xh", "z")
MP = ("xl", "c")
RING = ("xh", "xl")
PLANE = ("y", "z")
SWAP = ((0, 1), (1, 0))


def tied(value, token):
    return value + (0.0 * token[0, 0]).astype(value.dtype)


def after(value, *first):
    return lax.optimization_barrier((value,) + first)[0]


def other_core(value):
    return lax.ppermute(value, "c", SWAP)


def other_chip(value):
    return lax.ppermute(value, "xl", SWAP)


def along_ring(value, step):
    return lax.ppermute(value, RING, [(i, (i + step) % 4) for i in range(4)])


def gather_sides(own):
    return along_ring(own, 1), along_ring(own, -1), other_core(own)


def ring_opposite(opposite):
    half = opposite.shape[0] // 2
    return along_ring(opposite[:half], 1), along_ring(opposite[half:], -1)


def ring_sides(left, right, from_left, from_right):
    half = left.shape[0] // 2
    right = jnp.concatenate([right[:half] + from_left.astype(F32), right[half:]], axis=0)
    left = jnp.concatenate([left[:half], left[half:] + from_right.astype(F32)], axis=0)
    return left.astype(BF16), right.astype(BF16)


def ring_send(left, right):
    return along_ring(right, 1), along_ring(left, -1)


def add(left, right):
    return (left.astype(F32) + right.astype(F32)).astype(BF16)


def on_device(
    block_input,
    cotangent,
    pad_mask,
    seq_counts,
    gain_mix,
    query_weight,
    key_weight,
    value_weight,
    slot_weight,
    out_weight,
    gain_ffn,
    gate_weight,
    up_weight,
    down_weight,
):
    rows_own, width = block_input.shape
    rank = lax.axis_index(MP)
    side = lax.axis_index("xh")
    live = (jnp.arange(SEQS) < seq_counts[0]).astype(jnp.int32)
    keep_seq = (pad_mask[0] * live[:, None]).astype(F32)
    keep_own = lax.dynamic_slice_in_dim(keep_seq, rank * RUN, RUN, 1).reshape(rows_own, 1)

    rank_array = rank.reshape(1).astype(jnp.int32)

    hidden_part = gate_weight.shape[1] // 2
    kept, given = weight_halves(
        side.reshape(1).astype(jnp.int32), gate_weight, up_weight, down_weight.T
    )
    got = lax.ppermute(given, "xh", SWAP)
    paired = jnp.concatenate(
        [jnp.where(side == 0, kept, got), jnp.where(side == 0, got, kept)], axis=0
    )
    weights = lax.all_gather(paired, PLANE, axis=0, tiled=True)

    far = other_chip(after(block_input, got))
    cot_start = turn_rows(cotangent, keep_own)
    mixer_weights = (query_weight, key_weight, value_weight, slot_weight)
    near_input = other_core(block_input)
    keep_column = keep_seq[:, :, None]
    near_pre, near_normed, done = project_near(
        rank_array, (block_input, near_input), gain_mix[None], mixer_weights
    )
    farthest = other_core(tied(far, done))
    cot_sides = gather_sides(tied(cot_start, done))
    pre, normed_four, *blocks, mixing, probs, past = project_mix(
        rank_array, (far, farthest), gain_mix[None], mixer_weights,
        near_pre, near_normed, keep_column,
    )
    corner = cot_sides[0][:8, :128] + cot_sides[1][:8, :128] + blocks[0][:8, :128]
    mixed_parts = (
        blocks[0],
        other_core(blocks[1]),
        other_chip(tied(blocks[2], corner)),
        lax.ppermute(blocks[3], MP, [(i, 3 - i) for i in range(4)]),
    )
    hidden, ffn_own, mixed_own = mix_out(
        rank_array, mixed_parts, out_weight, block_input, keep_own, gain_ffn[None]
    )
    sides = gather_sides(ffn_own)
    half = rows_own // 2
    from_left = along_ring(jnp.concatenate([sides[0][:half], cot_sides[0][:half]], axis=0), 1)
    from_right = along_ring(jnp.concatenate([sides[1][half:], cot_sides[1][half:]], axis=0), -1)
    arrays = [ffn_own, *sides[:2], cot_start, *cot_sides[:2], from_left, from_right]
    arrays += [sides[2], *map(other_core, sides[:2])]
    arrays += [cot_sides[2], *map(other_core, cot_sides[:2])]
    arrays += [other_core(from_left), other_core(from_right)]
    plan = [
        [
            (core + at, first, count)
            for core in (0, 8)
            for at, first, count in (
                (3 * kind, 0, rows_own),
                (3 * kind + 1, 0, rows_own),
                (3 * kind + 2, 0, rows_own),
                (6, kind * half, half),
                (7, kind * half, half),
            )
        ]
        for kind in range(2)
    ]
    inner, cots, grads = ffn(arrays, plan, weights)
    ffn_sums = lax.psum_scatter(grads, PLANE, scatter_dimension=0, tiled=True)
    (away,) = ffn_back(cots, weights, pair_block, 1)
    (late_away,) = ffn_back(after(inner, away), weights, down_block, 1)
    got = other_core(away)
    own, left, right, ends = ffn_back(cots, weights, pair_block, 0, after(got, late_away))
    mixed_far = other_chip(tied(mixed_own, away))
    (late_near,) = ffn_back(
        after(inner, ends), weights, down_block, 0, done=(mixed_far, ends)
    )
    from_left, from_right, late_near = lax.optimization_barrier(
        ring_opposite(ends) + (late_near,)
    )
    left, right = ring_sides(left, right, from_left, from_right)
    from_left, from_right = ring_send(left, right)
    hidden_cot, branch_cot, gain_ffn_part = norm_back(
        own, from_left, from_right, cotangent, hidden, keep_own, gain_ffn[None]
    )
    branch_near = other_core(branch_cot)
    branch_far = other_chip(branch_cot)
    branch = (branch_cot, branch_near, branch_far, other_core(branch_far))
    head_cots = mixer_backward(
        rank_array, pre, keep_column, mixing, probs, past, out_weight, branch
    )
    mixed_all = (mixed_own, other_core(mixed_own), mixed_far, other_core(mixed_far))
    mixer_sums = lax.psum_scatter(
        mixer_grads(rank_array, normed_four, head_cots, mixed_all, branch),
        PLANE,
        scatter_dimension=0,
        tiled=True,
    )

    own, near, far, farthest, gain_mix_part = unproject(
        rank_array, after(head_cots, mixed_all[3]), normed_four, *mixer_weights
    )
    near = other_core(near)
    far = add(far, other_core(farthest))
    late_got = other_core(tied(late_away, gain_mix_part))
    gain_sums = jnp.stack([gain_mix_part[0] / gain_mix, gain_ffn_part[0]]).reshape(32, 128)
    for axis in ("c", "xl", "xh"):
        gain_sums = gain_sums + lax.ppermute(gain_sums, axis, SWAP)
    far = other_chip(tied(far, gain_sums))
    late_near = late_near.astype(F32) + late_got.astype(F32)
    late_own, late_left, late_right, late_ends = jnp.split(late_near, 4, axis=0)
    late_ends = ring_opposite(late_ends.astype(BF16))
    for axis in PLANE:
        for step in (1, 2):
            gain_sums = gain_sums + lax.ppermute(
                gain_sums, axis, [(i, i ^ step) for i in range(4)]
            )
    late_sides = ring_send(*ring_sides(late_left, late_right, *late_ends))
    gain_sums = gain_sums.reshape(2, width)
    input_grad = input_back(own, near, far, block_input, hidden_cot, gain_mix[None])
    block_output = block_out(late_own, *late_sides, hidden, keep_own)
    kept = lax.dynamic_slice_in_dim(ffn_sums, side * CHUNK, CHUNK, 0)
    given_back = lax.ppermute(
        lax.dynamic_slice_in_dim(ffn_sums, (1 - side) * CHUNK, CHUNK, 0), "xh", SWAP
    )
    mixer_sums, block_output, input_grad, gain_sums, given_back = lax.optimization_barrier(
        (mixer_sums, block_output, input_grad, gain_sums, given_back)
    )
    rows_out = rows_own // 8
    pieces = lax.all_to_all(
        mixer_sums.reshape(8, rows_out, COLUMNS), ("xh", "xl", "c"), 0, 0
    )
    query_grad, key_grad, value_grad, slot_grad, out_grad = mixer_out(pieces)

    def finish(tiles):
        mine, theirs = [
            jnp.concatenate([grads[:, n * TILE : (n + 1) * TILE] for n in tiles], axis=1)[
                :, :hidden_part
            ]
            for grads in (kept, given_back)
        ]
        return jnp.concatenate(
            [jnp.where(side == 0, mine, theirs), jnp.where(side == 0, theirs, mine)], axis=1
        ).astype(F32)

    return (
        block_output,
        input_grad,
        gain_sums[0],
        query_grad,
        key_grad,
        value_grad,
        slot_grad,
        out_grad,
        gain_sums[1],
        finish((0, 3, 6)),
        finish((1, 4, 7)),
        finish((2, 5, 8)).T,
    )


def solution(mesh):
    fine = jax.sharding.Mesh(mesh.devices.reshape(4, 2, 4, 2, 2), AXES)
    rows = P(AXES, None)
    return jax.shard_map(
        on_device,
        mesh=fine,
        in_specs=(
            rows,
            rows,
            P(DP, None, None),
            P(DP),
            P(),
            P(),
            P(),
            P(),
            P(),
            P(),
            P(),
            P(DP, MP),
            P(DP, MP),
            P(MP, DP),
        ),
        out_specs=(
            rows,
            rows,
            P(),
            rows,
            rows,
            rows,
            rows,
            rows,
            P(),
            P(DP, MP),
            P(DP, MP),
            P(MP, DP),
        ),
        check_vma=False,
    )
```

```python
import functools

import jax
import jax.numpy as jnp
from jax import lax
from jax.experimental import pallas as pl
from jax.experimental.pallas import tpu as pltpu
from jax.sharding import PartitionSpec as P

HEAD_DIM = 512
SLOTS = 64
LENGTH = 256
RUN = 64
RUNS = 4
SEQS = 2
LEVELS = (128, 64, 32, 16, 8, 4, 2, 1)
SCALE = HEAD_DIM ** (-0.5)
GATE_SCALE = 0.125
F32 = jnp.float32
BF16 = jnp.bfloat16


def mm(left, right):
    return jnp.dot(left, right, preferred_element_type=F32)


def mm_cols(left, right):
    return lax.dot_general(left, right, (((1,), (1,)), ((), ())), preferred_element_type=F32)


def mm_rows(left, right):
    return lax.dot_general(left, right, (((0,), (0,)), ((), ())), preferred_element_type=F32)


def halves(value):
    high = value.astype(BF16)
    return high, (value - high.astype(F32)).astype(BF16)


def fine_product(left, right):
    left_high, left_low = halves(left)
    right_high, right_low = halves(right)
    rows, width = left.shape[0], right.shape[1]
    out = mm(
        jnp.concatenate([left_high, left_low], axis=0),
        jnp.concatenate([right_high, right_low], axis=1),
    )
    return out[:rows, :width] + out[:rows, width:] + out[rows:, :width]


def fine_cols_product(left, right):
    left_high, left_low = halves(left)
    right_high, right_low = halves(right)
    return mm_cols(
        jnp.concatenate([left_high, left_low, left_high], axis=1),
        jnp.concatenate([right_high, right_high, right_low], axis=1),
    )


def decay_tables(slot_pre, keep):
    log_gate = jnp.minimum(slot_pre, 0.0) - jnp.log1p(jnp.exp(-jnp.abs(slot_pre)))
    log_decay = keep * log_gate * GATE_SCALE
    half = jnp.tanh(-0.5 * log_decay)
    written = 2.0 * half / (1.0 + half)
    rows = lax.broadcasted_iota(jnp.int32, log_decay.shape, 0)
    running = log_decay
    shift = 1
    while shift < LENGTH:
        running = running + jnp.where(rows >= shift, pltpu.roll(running, shift, 0), 0.0)
        shift *= 2
    return log_decay, written, running


def later_sum(value):
    rows = lax.broadcasted_iota(jnp.int32, value.shape, 0)
    shift = 1
    while shift < LENGTH:
        value = value + jnp.where(rows < LENGTH - shift, pltpu.roll(value, LENGTH - shift, 0), 0.0)
        shift *= 2
    return value


def level_factors(running):
    rows = lax.broadcasted_iota(jnp.int32, running.shape, 0)
    last = running
    factors = {}
    size = 1
    while size < LENGTH:
        odd = (rows & size) != 0
        before = pltpu.roll(last, size, 0)
        factor = jnp.exp(jnp.where(odd, running - before, last - running))
        factors[size] = (jnp.where(odd, factor, 0.0), jnp.where(odd, 0.0, factor))
        last = jnp.where(odd, last, pltpu.roll(last, LENGTH - size, 0))
        size *= 2
    return factors


def level_map(flip):
    rows = lax.broadcasted_iota(jnp.int32, (LENGTH, LENGTH), 0)
    cols = lax.broadcasted_iota(jnp.int32, (LENGTH, LENGTH), 1)
    later = rows < cols if flip else rows > cols
    return jnp.where(later, rows ^ cols, 0), rows == cols


def at_level(where_map, size):
    return (where_map >= size) & (where_map < 2 * size)


def gather_rows(ref, rank, seq, start, width):
    parts = []
    for run in range(RUNS):
        first = pl.multiple_of(((rank ^ run) * SEQS + seq) * RUN, RUN)
        parts.append(ref[pl.ds(first, RUN), start : start + width])
    return jnp.concatenate(parts, axis=0)


def spread_rows(ref, rank, seq, start, width, value):
    for run in range(RUNS):
        first = pl.multiple_of(((rank ^ run) * SEQS + seq) * RUN, RUN)
        ref[pl.ds(first, RUN), start : start + width] = value[run * RUN : (run + 1) * RUN]


def sigmoid(value):
    return 1.0 / (1.0 + jnp.exp(-value))


def silu(value):
    return value * sigmoid(value)


def silu_slope(pre):
    sigma = sigmoid(pre)
    return sigma * (1.0 + pre * (1.0 - sigma))


def mix_forward(rank, seq, pre_ref, keep, mixed_ref, mixing_ref, probs_ref, past_ref):
    queries = silu(gather_rows(pre_ref, rank, seq, 0, HEAD_DIM)).astype(BF16)
    keys = silu(gather_rows(pre_ref, rank, seq, HEAD_DIM, HEAD_DIM)).astype(BF16)
    values = gather_rows(pre_ref, rank, seq, 2 * HEAD_DIM, HEAD_DIM).astype(BF16)
    slot_pre = gather_rows(pre_ref, rank, seq, 3 * HEAD_DIM, SLOTS)
    _, written, running = decay_tables(slot_pre, keep)
    factors = level_factors(running)
    where_map, own = level_map(False)
    pairs = mm_cols(queries, keys)
    own_pairs = jnp.sum(jnp.where(own, pairs, 0.0), axis=1, keepdims=True)
    past = jnp.zeros((LENGTH, SLOTS), F32)
    for size in LEVELS:
        after, before = factors[size]
        past = past + after * fine_product(
            jnp.where(at_level(where_map, size), pairs, 0.0), before * written
        )
    past = SCALE * past
    scores = past + SCALE * own_pairs * written
    grown = jnp.exp(scores - jnp.max(scores, axis=1, keepdims=True))
    probs = grown / jnp.sum(grown, axis=1, keepdims=True)
    mixing = jnp.where(own, jnp.sum(probs * written, axis=1, keepdims=True), 0.0)
    for size in LEVELS:
        after, before = factors[size]
        mixing = jnp.where(
            at_level(where_map, size),
            fine_cols_product(probs * after, before * written),
            mixing,
        )
    mixing = mixing.astype(BF16)
    mixed = mm(mixing, values).astype(BF16)
    spread_rows(mixed_ref, rank, seq, 0, HEAD_DIM, mixed)
    mixing_ref[seq] = mixing
    probs_ref[seq] = probs
    past_ref[seq] = past


def mixer_backward_kernel(
    rank_ref, pre_ref, keep_ref, mixing_ref, probs_ref, past_ref, weight_ref,
    own_ref, near_ref, far_ref, farthest_ref, out_ref, cot_ref,
):
    rank = rank_ref[0]
    seq = pl.program_id(0)

    @pl.when(seq == 0)
    def _():
        branch = [ref[...] for ref in (own_ref, near_ref, far_ref, farthest_ref)]
        cot_ref[...] = mm_cols(jnp.concatenate(branch, axis=0), weight_ref[...]).astype(BF16)

    query_pre = gather_rows(pre_ref, rank, seq, 0, HEAD_DIM)
    key_pre = gather_rows(pre_ref, rank, seq, HEAD_DIM, HEAD_DIM)
    queries = silu(query_pre).astype(BF16)
    keys = silu(key_pre).astype(BF16)
    values = gather_rows(pre_ref, rank, seq, 2 * HEAD_DIM, HEAD_DIM).astype(BF16)
    slot_pre = gather_rows(pre_ref, rank, seq, 3 * HEAD_DIM, SLOTS)
    cot = gather_rows(cot_ref, rank, seq, 0, HEAD_DIM)
    keep = keep_ref[0]
    log_decay, written, running = decay_tables(slot_pre, keep)
    factors = level_factors(running)
    where_map, own = level_map(False)
    where_flip, _ = level_map(True)
    probs = probs_ref[0]
    past = past_ref[0]
    mixing = mixing_ref[0]
    spread_rows(
        out_ref, rank, seq, 2 * HEAD_DIM, HEAD_DIM, mm_rows(mixing, cot).astype(BF16)
    )
    pairs_flip = mm_cols(keys, queries) * SCALE
    cot_flip = mm_cols(values, cot)
    mixing_cot = mm_cols(cot, values)
    own_cot = jnp.sum(jnp.where(own, mixing_cot, 0.0), axis=1, keepdims=True)
    own_pairs = jnp.sum(jnp.where(own, pairs_flip, 0.0), axis=1, keepdims=True)
    past_cot = jnp.zeros((LENGTH, SLOTS), F32)
    for size in LEVELS:
        after, before = factors[size]
        past_cot = past_cot + after * fine_product(
            jnp.where(at_level(where_map, size), mixing_cot, 0.0), before * written
        )
    probs_cot = past_cot + own_cot * written
    scores_cot = probs * (probs_cot - jnp.sum(probs * probs_cot, axis=1, keepdims=True))
    row_flow = probs * past_cot + scores_cot * past
    pairs_cot = jnp.where(own, jnp.sum(scores_cot * written, axis=1, keepdims=True), 0.0)
    ahead = jnp.zeros((LENGTH, SLOTS), F32)
    both_flip = jnp.concatenate([cot_flip, pairs_flip], axis=1)
    where_both = jnp.concatenate([where_flip, where_flip], axis=1)
    for size in LEVELS:
        after, before = factors[size]
        pairs_cot = jnp.where(
            at_level(where_map, size),
            fine_cols_product(scores_cot * after, before * written),
            pairs_cot,
        )
        ahead = ahead + before * fine_product(
            jnp.where(at_level(where_both, size), both_flip, 0.0),
            jnp.concatenate([probs * after, scores_cot * after], axis=0),
        )
    pairs_low = (SCALE * pairs_cot).astype(BF16)
    query_cot = (mm(pairs_low, keys) * silu_slope(query_pre)).astype(BF16)
    spread_rows(out_ref, rank, seq, 0, HEAD_DIM, query_cot)
    key_cot = (mm_rows(pairs_low, queries) * silu_slope(key_pre)).astype(BF16)
    spread_rows(out_ref, rank, seq, HEAD_DIM, HEAD_DIM, key_cot)
    running_cot = row_flow - written * ahead
    written_cot = ahead + own_cot * probs + scores_cot * own_pairs
    decay_cot = later_sum(running_cot) - written_cot * jnp.exp(log_decay)
    slot_cot = decay_cot * keep * GATE_SCALE * sigmoid(-slot_pre)
    padded = jnp.concatenate([slot_cot, jnp.zeros((LENGTH, SLOTS), F32)], axis=1).astype(BF16)
    spread_rows(out_ref, rank, seq, 3 * HEAD_DIM, 2 * SLOTS, padded)


def cost(microseconds):
    return pl.CostEstimate(
        flops=int(microseconds * 1.1e9), bytes_accessed=1 << 20, transcendentals=0
    )


def whole(shape):
    zeros = (0,) * len(shape)
    return pl.BlockSpec(shape, lambda seq, rank: zeros)


def one_seq(shape):
    return pl.BlockSpec((1,) + shape, lambda seq, rank: (seq, 0, 0))


TOKENS = RUNS * SEQS * RUN
WIDE = 3 * HEAD_DIM + 2 * SLOTS
WIDTH = 2048
ROWS_OWN = SEQS * RUN
RANK_SPEC = pl.BlockSpec(memory_space=pltpu.SMEM)


def mixer_backward(rank, pre, keep, mixing, probs, past, out_weight, branch):
    return pl.pallas_call(
        mixer_backward_kernel,
        grid_spec=pltpu.PrefetchScalarGridSpec(
            num_scalar_prefetch=1,
            grid=(SEQS,),
            in_specs=[
                whole((TOKENS, WIDE)),
                one_seq((LENGTH, 1)),
                one_seq((LENGTH, LENGTH)),
                one_seq((LENGTH, SLOTS)),
                one_seq((LENGTH, SLOTS)),
                pl.BlockSpec((HEAD_DIM, WIDTH), lambda seq, rank: (rank[0], 0)),
            ]
            + [whole((ROWS_OWN, WIDTH))] * 4,
            out_specs=whole((TOKENS, WIDE)),
            scratch_shapes=[pltpu.VMEM((TOKENS, HEAD_DIM), BF16)],
        ),
        out_shape=jax.ShapeDtypeStruct((TOKENS, WIDE), BF16),
        compiler_params=pltpu.CompilerParams(
            vmem_limit_bytes=48 * 1024 * 1024, dimension_semantics=("arbitrary",)
        ),
        cost_estimate=cost(13),
        name="mixer_backward",
    )(rank, pre, keep, mixing, probs, past, out_weight, *branch)


EPS = 1e-05
K_TILE = 512
ALL_SLOTS = 4 * SLOTS
TILE = 256
TILES = 3
HIDDEN = TILE * TILES


def project_step(step, rank, row_refs, gain, weight_refs, slot_ref, pre_ref, normed_ref, slots_ref, first):
    last = first + 2 * ROWS_OWN

    @pl.when(step == 0)
    def _():
        for i, ref in enumerate(row_refs):
            rows = ref[...].astype(F32)
            root = lax.rsqrt(jnp.mean(rows * rows, axis=1, keepdims=True) + EPS)
            start = first + i * ROWS_OWN
            normed_ref[start : start + ROWS_OWN] = (rows * root * gain).astype(BF16)
        pre_ref[first:last] = jnp.zeros((2 * ROWS_OWN, WIDE), F32)
        slots_ref[...] = jnp.zeros_like(slots_ref)

    left = normed_ref[first:last, pl.ds(pl.multiple_of(step * K_TILE, K_TILE), K_TILE)]
    for i, ref in enumerate(weight_refs):
        pre_ref[first:last, i * HEAD_DIM : (i + 1) * HEAD_DIM] += mm(left, ref[...])
    slots_ref[...] += mm(left, slot_ref[...])

    @pl.when(step == WIDTH // K_TILE - 1)
    def _():
        mine = jnp.zeros((2 * ROWS_OWN, SLOTS), F32)
        for head in range(4):
            mine = jnp.where(rank == head, slots_ref[:, head * SLOTS : (head + 1) * SLOTS], mine)
        pre_ref[first:last, 3 * HEAD_DIM :] = jnp.concatenate([mine, jnp.zeros_like(mine)], axis=1)


def project_near_kernel(
    rank_ref, own_ref, near_ref, gain_ref, query_ref, key_ref, value_ref, slot_ref,
    pre_ref, normed_ref, done_ref, slots_ref,
):
    step = pl.program_id(0)
    project_step(
        step, rank_ref[0], (own_ref, near_ref), gain_ref[...], (query_ref, key_ref, value_ref),
        slot_ref, pre_ref, normed_ref, slots_ref, 0,
    )
    done_ref[...] = jnp.zeros_like(done_ref)


def project_mix_kernel(
    rank_ref, far_ref, farthest_ref, gain_ref, query_ref, key_ref, value_ref, slot_ref,
    near_pre_ref, near_normed_ref, keep_ref,
    pre_ref, normed_ref, first_ref, second_ref, third_ref, fourth_ref,
    mixing_ref, probs_ref, past_ref, slots_ref, mixed_ref,
):
    step = pl.program_id(0)
    half = 2 * ROWS_OWN

    @pl.when(step == 0)
    def _():
        pre_ref[:half] = near_pre_ref[...]
        normed_ref[:half] = near_normed_ref[...]

    project_step(
        step, rank_ref[0], (far_ref, farthest_ref), gain_ref[...], (query_ref, key_ref, value_ref),
        slot_ref, pre_ref, normed_ref, slots_ref, half,
    )

    @pl.when(step == WIDTH // K_TILE - 1)
    def _():
        for seq in range(SEQS):
            mix_forward(
                rank_ref[0], seq, pre_ref, keep_ref[seq], mixed_ref, mixing_ref, probs_ref, past_ref
            )
        for i, ref in enumerate((first_ref, second_ref, third_ref, fourth_ref)):
            ref[...] = mixed_ref[i * ROWS_OWN : (i + 1) * ROWS_OWN]


def project(kernel, rank, pieces, gain, weights, extra, outs, scratch, micros, name):
    def fixed(shape):
        zeros = (0,) * len(shape)
        return pl.BlockSpec(shape, lambda k, rank: zeros)

    weight = pl.BlockSpec((K_TILE, HEAD_DIM), lambda k, rank: (k, rank[0]))
    return pl.pallas_call(
        kernel,
        grid_spec=pltpu.PrefetchScalarGridSpec(
            num_scalar_prefetch=1,
            grid=(WIDTH // K_TILE,),
            in_specs=[fixed(piece.shape) for piece in pieces]
            + [fixed((1, WIDTH)), weight, weight, weight]
            + [pl.BlockSpec((K_TILE, ALL_SLOTS), lambda k, rank: (k, 0))]
            + [fixed(array.shape) for array in extra],
            out_specs=[fixed(shape) for shape, _ in outs],
            scratch_shapes=[pltpu.VMEM((2 * ROWS_OWN, ALL_SLOTS), F32)] + scratch,
        ),
        out_shape=[jax.ShapeDtypeStruct(shape, dtype) for shape, dtype in outs],
        compiler_params=pltpu.CompilerParams(
            vmem_limit_bytes=48 * 1024 * 1024, dimension_semantics=("arbitrary",)
        ),
        cost_estimate=cost(micros),
        name=name,
    )(rank, *pieces, gain, *weights, *extra)


def project_near(rank, pieces, gain, weights):
    half = 2 * ROWS_OWN
    outs = [((half, WIDE), F32), ((half, WIDTH), BF16), ((8, 128), F32)]
    return project(
        project_near_kernel, rank, pieces, gain, weights, (), outs, [], 1, "project_near"
    )


def project_mix(rank, pieces, gain, weights, near_pre, near_normed, keep):
    outs = [((TOKENS, WIDE), F32), ((TOKENS, WIDTH), BF16)]
    outs += [((ROWS_OWN, HEAD_DIM), BF16)] * 4 + [((SEQS, LENGTH, LENGTH), BF16)]
    outs += [((SEQS, LENGTH, SLOTS), F32)] * 2
    return project(
        project_mix_kernel, rank, pieces, gain, weights, (near_pre, near_normed, keep), outs,
        [pltpu.VMEM((TOKENS, HEAD_DIM), BF16)], 13, "project_mix",
    )


def unproject_kernel(
    rank_ref, cots_ref, normed_ref, query_ref, key_ref, value_ref, slot_ref,
    own_ref, near_ref, far_ref, farthest_ref, gain_ref,
):
    total = mm_cols(cots_ref[:, :HEAD_DIM], query_ref[...])
    total += mm_cols(cots_ref[:, HEAD_DIM : 2 * HEAD_DIM], key_ref[...])
    total += mm_cols(cots_ref[:, 2 * HEAD_DIM : 3 * HEAD_DIM], value_ref[...])
    slots = cots_ref[:, 3 * HEAD_DIM : 3 * HEAD_DIM + SLOTS]
    spread = jnp.concatenate(
        [jnp.where(rank_ref[0] == head, slots, jnp.zeros_like(slots)) for head in range(4)],
        axis=1,
    )
    total += mm_cols(spread, slot_ref[...])
    for i, ref in enumerate((own_ref, near_ref, far_ref, farthest_ref)):
        ref[...] = total[i * ROWS_OWN : (i + 1) * ROWS_OWN].astype(BF16)
    gain_ref[...] = jnp.sum(total * normed_ref[...].astype(F32), axis=0, keepdims=True)


def unproject(rank, cots, normed, query_weight, key_weight, value_weight, slot_weight):
    weight = pl.BlockSpec((K_TILE, HEAD_DIM), lambda k, rank: (k, rank[0]))
    rows = pl.BlockSpec((ROWS_OWN, K_TILE), lambda k, rank: (0, k))
    return pl.pallas_call(
        unproject_kernel,
        grid_spec=pltpu.PrefetchScalarGridSpec(
            num_scalar_prefetch=1,
            grid=(WIDTH // K_TILE,),
            in_specs=[
                pl.BlockSpec((TOKENS, WIDE), lambda k, rank: (0, 0)),
                pl.BlockSpec((TOKENS, K_TILE), lambda k, rank: (0, k)),
                weight,
                weight,
                weight,
                pl.BlockSpec((K_TILE, ALL_SLOTS), lambda k, rank: (k, 0)),
            ],
            out_specs=[rows] * 4 + [pl.BlockSpec((1, K_TILE), lambda k, rank: (0, k))],
        ),
        out_shape=[jax.ShapeDtypeStruct((ROWS_OWN, WIDTH), BF16)] * 4
        + [jax.ShapeDtypeStruct((1, WIDTH), F32)],
        compiler_params=pltpu.CompilerParams(
            vmem_limit_bytes=48 * 1024 * 1024, dimension_semantics=("arbitrary",)
        ),
        cost_estimate=cost(7),
        name="unproject",
    )(rank, cots, normed, query_weight, key_weight, value_weight, slot_weight)


ALL_HIDDEN = 3 * HIDDEN
COLUMNS = HEAD_DIM + WIDE
CHUNK = 64
BLOCK_ROWS = WIDTH // 4


def mixer_grads_kernel(*refs):
    normed_ref, cots_ref, out_ref, block_ref = refs[1], refs[2], refs[-2], refs[-1]
    block_ref[:, :WIDE] = mm_rows(normed_ref[...], cots_ref[...]).astype(BF16)
    mixed = jnp.concatenate([ref[...] for ref in refs[3:7]], axis=0)
    branch = jnp.concatenate([ref[...] for ref in refs[7:11]], axis=0)
    block_ref[:, WIDE:] = mm_rows(mixed, branch).astype(BF16)
    for side in range(2):
        for z in range(4):
            source = (side * 4 + z) * CHUNK
            target = (z * 2 + side) * CHUNK
            out_ref[target : target + CHUNK] = block_ref[source : source + CHUNK]


def mixer_grads(rank, normed, cots, mixed, branch):
    return pl.pallas_call(
        mixer_grads_kernel,
        grid_spec=pltpu.PrefetchScalarGridSpec(
            num_scalar_prefetch=1,
            grid=(4,),
            in_specs=[
                pl.BlockSpec((TOKENS, BLOCK_ROWS), lambda y, rank: (0, y)),
                pl.BlockSpec((TOKENS, WIDE), lambda y, rank: (0, 0)),
            ]
            + [pl.BlockSpec((ROWS_OWN, BLOCK_ROWS), lambda y, rank: (0, y))] * 4
            + [pl.BlockSpec((ROWS_OWN, HEAD_DIM), lambda y, rank: (0, rank[0]))] * 4,
            out_specs=pl.BlockSpec((BLOCK_ROWS, COLUMNS), lambda y, rank: (y, 0)),
            scratch_shapes=[pltpu.VMEM((BLOCK_ROWS, COLUMNS), BF16)],
        ),
        out_shape=jax.ShapeDtypeStruct((WIDTH, COLUMNS), BF16),
        compiler_params=pltpu.CompilerParams(
            vmem_limit_bytes=56 * 1024 * 1024, dimension_semantics=("arbitrary",)
        ),
        cost_estimate=cost(10),
        name="mixer_grads",
    )(rank, normed, cots, *mixed, *branch)


def ffn_kernel(plan, *refs):
    weight_ref, inner_ref, cots_ref, grads_ref, rows_ref, sems = refs[-6:]
    step = pl.program_id(0)

    def copies(side):
        start = 0
        made = []
        for i, (at, first, rows) in enumerate(plan[side]):
            source = refs[at].at[pl.ds(first, rows)]
            place = rows_ref.at[side, pl.ds(start, rows)]
            made.append(pltpu.make_async_copy(source, place, sems.at[side, i]))
            start += rows
        return made

    @pl.when(step == 0)
    def _():
        for copy in copies(0) + copies(1):
            copy.start()
        for copy in copies(0):
            copy.wait()

    def halves_of(side, columns):
        return [
            mm(rows_ref[side, half * TOKENS : (half + 1) * TOKENS], weight_ref[:, columns])
            for half in range(2)
        ]

    both = halves_of(0, slice(0, 2 * TILE))

    @pl.when(step == 0)
    def _():
        for copy in copies(1):
            copy.wait()

    inner_cots = halves_of(1, slice(2 * TILE, 3 * TILE))
    for half in range(2):
        rows = slice(half * TOKENS, (half + 1) * TOKENS)
        gate_pre, up_pre = both[half][:, :TILE], both[half][:, TILE:]
        inner_cot = inner_cots[half]
        sigma = sigmoid(gate_pre)
        gate_act = gate_pre * sigma
        inner_ref[rows] = (gate_act * up_pre).astype(BF16)
        slope = sigma * (1.0 + gate_pre * (1.0 - sigma))
        cots_ref[rows, :TILE] = (inner_cot * up_pre * slope).astype(BF16)
        cots_ref[rows, TILE:] = (inner_cot * gate_act).astype(BF16)
    for m in range(4):
        cut = slice(m * BLOCK_ROWS, (m + 1) * BLOCK_ROWS)
        grads_ref[cut, : 2 * TILE] = mm_rows(rows_ref[0, :, cut], cots_ref[...]).astype(BF16)
        grads_ref[cut, 2 * TILE :] = mm_rows(rows_ref[1, :, cut], inner_ref[...]).astype(BF16)


def ffn(arrays, plan, weights):
    both = 2 * TOKENS
    return pl.pallas_call(
        functools.partial(ffn_kernel, plan),
        grid=(TILES,),
        in_specs=[pl.BlockSpec(memory_space=pl.ANY)] * len(arrays)
        + [pl.BlockSpec((WIDTH, 3 * TILE), lambda n: (0, n))],
        out_specs=[
            pl.BlockSpec((both, TILE), lambda n: (0, n)),
            pl.BlockSpec((both, 2 * TILE), lambda n: (0, n)),
            pl.BlockSpec((WIDTH, 3 * TILE), lambda n: (0, n)),
        ],
        out_shape=[
            jax.ShapeDtypeStruct((both, HIDDEN), BF16),
            jax.ShapeDtypeStruct((both, 2 * HIDDEN), BF16),
            jax.ShapeDtypeStruct((WIDTH, ALL_HIDDEN), BF16),
        ],
        scratch_shapes=[
            pltpu.VMEM((2, both, WIDTH), BF16),
            pltpu.SemaphoreType.DMA((2, len(plan[0]))),
        ],
        compiler_params=pltpu.CompilerParams(
            vmem_limit_bytes=56 * 1024 * 1024, dimension_semantics=("arbitrary",)
        ),
        cost_estimate=cost(24),
        name="ffn",
    )(*arrays, weights)


def back_product(cots_ref, weight_refs):
    total = None
    width = cots_ref.shape[1] // TILES
    for n, ref in enumerate(weight_refs):
        term = mm_cols(cots_ref[:, n * width : (n + 1) * width], ref[...])
        total = term if total is None else total + term
    return total


def away_kernel(cots_ref, *refs):
    refs[-1][...] = back_product(cots_ref, refs[:TILES]).astype(BF16)


def near_kernel(cots_ref, *refs):
    total = back_product(cots_ref, refs[:TILES]) + refs[TILES][...].astype(F32)
    for i, ref in enumerate(refs[-4:]):
        ref[...] = total[i * ROWS_OWN : (i + 1) * ROWS_OWN].astype(ref.dtype)


def pair_block(n):
    return pl.BlockSpec(
        (pl.Element(BLOCK_ROWS), pl.Element(2 * TILE)),
        lambda m: (m * BLOCK_ROWS, n * 3 * TILE),
    )


def down_block(n):
    return pl.BlockSpec((BLOCK_ROWS, TILE), lambda m: (m, 3 * n + 2))


def ffn_back(cots, weights, block, half, got=None, done=()):
    kernel = away_kernel if got is None else near_kernel
    own = jax.ShapeDtypeStruct((ROWS_OWN, WIDTH), F32)
    ends = jax.ShapeDtypeStruct((ROWS_OWN, WIDTH), BF16)
    away = jax.ShapeDtypeStruct((TOKENS, WIDTH), BF16)
    outs = [away] if got is None else [own, own, own, ends]
    extra = [] if got is None else [got]
    return pl.pallas_call(
        kernel,
        grid=(4,),
        in_specs=[pl.BlockSpec((TOKENS, cots.shape[1]), lambda m: (half, 0))]
        + [block(n) for n in range(TILES)]
        + [pl.BlockSpec((TOKENS, BLOCK_ROWS), lambda m: (0, m)) for _ in extra]
        + [pl.BlockSpec(memory_space=pl.ANY) for _ in done],
        out_specs=[pl.BlockSpec((out.shape[0], BLOCK_ROWS), lambda m: (0, m)) for out in outs],
        out_shape=outs,
        compiler_params=pltpu.CompilerParams(vmem_limit_bytes=48 * 1024 * 1024),
        cost_estimate=cost(5),
        name="ffn_back",
    )(cots, *[weights] * TILES, *extra, *done)


def mixer_out_kernel(pieces_ref, query_ref, key_ref, value_ref, slot_ref, out_ref):
    slots = []
    for head in range(4):
        block = pieces_ref[head].astype(F32) + pieces_ref[4 + head].astype(F32)
        columns = slice(head * HEAD_DIM, (head + 1) * HEAD_DIM)
        for i, ref in enumerate((query_ref, key_ref, value_ref)):
            ref[:, columns] = block[:, i * HEAD_DIM : (i + 1) * HEAD_DIM]
        slots.append(block[:, 3 * HEAD_DIM : 3 * HEAD_DIM + SLOTS])
        out_ref[:, columns] = block[:, WIDE:]
    slot_ref[...] = jnp.concatenate(slots, axis=1)


def mixer_out(pieces):
    rows = pieces.shape[1]
    widths = (WIDTH, WIDTH, WIDTH, ALL_SLOTS, WIDTH)
    return pl.pallas_call(
        mixer_out_kernel,
        grid=(1,),
        in_specs=[pl.BlockSpec(pieces.shape, lambda i: (0, 0, 0))],
        out_specs=[pl.BlockSpec((rows, width), lambda i: (0, 0)) for width in widths],
        out_shape=[jax.ShapeDtypeStruct((rows, width), F32) for width in widths],
        cost_estimate=cost(2),
        name="mixer_out",
    )(pieces)


def to_plane(value):
    parts = []
    for y in range(4):
        for z in range(4):
            for side in range(2):
                start = y * 8 * CHUNK + side * 4 * CHUNK + z * CHUNK
                parts.append(value[:, start : start + CHUNK])
    return jnp.concatenate(parts, axis=1)


def from_plane(value):
    parts = []
    for y in range(4):
        for side in range(2):
            for z in range(4):
                start = y * 8 * CHUNK + z * 2 * CHUNK + side * CHUNK
                parts.append(value[:, start : start + CHUNK])
    return jnp.concatenate(parts, axis=1)


def rms_parts(rows):
    root = lax.rsqrt(jnp.mean(rows * rows, axis=1, keepdims=True) + EPS)
    return rows * root, root


def rms_back(incoming, gain, unit, root):
    scaled = incoming * gain
    return root * (scaled - unit * jnp.mean(scaled * unit, axis=1, keepdims=True))


def mix_out_kernel(
    rank_ref, first_ref, second_ref, third_ref, fourth_ref, weight_ref, input_ref, keep_ref,
    gain_ref, hidden_ref, ffn_in_ref, mixed_ref,
):
    branch = None
    for k, ref in enumerate((first_ref, second_ref, third_ref, fourth_ref)):
        part = ref[...]
        place = pl.multiple_of((rank_ref[0] ^ k) * HEAD_DIM, HEAD_DIM)
        mixed_ref[:, pl.ds(place, HEAD_DIM)] = part
        product = mm(part, weight_ref[pl.ds(place, HEAD_DIM), :])
        branch = product if branch is None else branch + product
    hidden = input_ref[...].astype(F32) + keep_ref[...] * branch
    hidden_ref[...] = hidden
    ffn_in_ref[...] = to_plane((rms_parts(hidden)[0] * gain_ref[...]).astype(BF16))


def mix_out(rank, parts, out_weight, block_input, keep, gain):
    own = (ROWS_OWN, WIDTH)
    vmem = pl.BlockSpec(memory_space=pltpu.VMEM)
    return pl.pallas_call(
        mix_out_kernel,
        in_specs=[RANK_SPEC] + [vmem] * 8,
        out_specs=[vmem] * 3,
        out_shape=[
            jax.ShapeDtypeStruct(own, F32),
            jax.ShapeDtypeStruct(own, BF16),
            jax.ShapeDtypeStruct(own, BF16),
        ],
        compiler_params=pltpu.CompilerParams(vmem_limit_bytes=24 * 1024 * 1024),
        cost_estimate=cost(3),
        name="mix_out",
    )(rank, *parts, out_weight, block_input, keep, gain)


def norm_back_kernel(
    own_ref, left_ref, right_ref, cot_ref, hidden_ref, keep_ref, gain_ref,
    hidden_cot_ref, branch_ref, gain_cot_ref,
):
    incoming = own_ref[...] + left_ref[...].astype(F32) + right_ref[...].astype(F32)
    incoming = from_plane(incoming)
    unit, root = rms_parts(hidden_ref[...])
    hidden_cot = cot_ref[...].astype(F32) + rms_back(incoming, gain_ref[...], unit, root)
    hidden_cot_ref[...] = hidden_cot
    branch_ref[...] = (keep_ref[...] * hidden_cot).astype(BF16)
    gain_cot_ref[...] = jnp.sum(incoming * unit, axis=0, keepdims=True)


def block_out_kernel(own_ref, left_ref, right_ref, hidden_ref, keep_ref, out_ref):
    down = own_ref[...] + left_ref[...].astype(F32) + right_ref[...].astype(F32)
    out_ref[...] = hidden_ref[...] + keep_ref[...] * from_plane(down)


def input_back_kernel(own_ref, near_ref, far_ref, input_ref, hidden_cot_ref, gain_ref, out_ref):
    incoming = own_ref[...].astype(F32) + near_ref[...].astype(F32) + far_ref[...].astype(F32)
    unit, root = rms_parts(input_ref[...].astype(F32))
    out_ref[...] = hidden_cot_ref[...] + rms_back(incoming, gain_ref[...], unit, root)


def own_rows(kernel, arrays, outs, name):
    def spec(shape):
        return pl.BlockSpec((min(shape[0], ROWS_OWN), shape[1]), lambda i: (0, 0))

    return pl.pallas_call(
        kernel,
        grid=(1,),
        in_specs=[spec(array.shape) for array in arrays],
        out_specs=[spec(shape) for shape, _ in outs],
        out_shape=[jax.ShapeDtypeStruct(shape, dtype) for shape, dtype in outs],
        compiler_params=pltpu.CompilerParams(vmem_limit_bytes=32 * 1024 * 1024),
        cost_estimate=cost(3),
        name=name,
    )(*arrays)


def norm_back(*arrays):
    own = (ROWS_OWN, WIDTH)
    return own_rows(
        norm_back_kernel, arrays, [(own, F32), (own, BF16), ((1, WIDTH), F32)], "norm_back"
    )


def block_out(*arrays):
    return own_rows(block_out_kernel, arrays, [((ROWS_OWN, WIDTH), F32)], "block_out")[0]


def input_back(*arrays):
    return own_rows(input_back_kernel, arrays, [((ROWS_OWN, WIDTH), F32)], "input_back")[0]


def halves_kernel(side_ref, gate_ref, up_ref, down_ref, keep_ref, give_ref):
    rows = gate_ref.shape[0]
    part = gate_ref.shape[1] // 2
    padding = jnp.zeros((rows, HIDDEN - part), BF16)
    down = down_ref[...]
    for half in range(2):
        cut = slice(half * part, (half + 1) * part)
        gate, up, turned = [
            jnp.concatenate([value, padding], axis=1)
            for value in (gate_ref[:, cut], up_ref[:, cut], down[:, cut])
        ]
        tiles = []
        for n in range(TILES):
            tiles += [value[:, n * TILE : (n + 1) * TILE] for value in (gate, up, turned)]
        packed = jnp.concatenate(tiles, axis=1)

        @pl.when(side_ref[0] == half)
        def _():
            keep_ref[...] = packed

        @pl.when(side_ref[0] != half)
        def _():
            give_ref[...] = packed


def weight_halves(side, gate_weight, up_weight, down_weight):
    shape = jax.ShapeDtypeStruct((gate_weight.shape[0], 3 * HIDDEN), BF16)
    return pl.pallas_call(
        halves_kernel,
        in_specs=[RANK_SPEC] + [pl.BlockSpec(memory_space=pltpu.VMEM)] * 3,
        out_specs=[pl.BlockSpec(memory_space=pltpu.VMEM)] * 2,
        out_shape=[shape, shape],
        cost_estimate=cost(2),
        name="weight_halves",
    )(side, gate_weight, up_weight, down_weight)


def turn_kernel(rows_ref, keep_ref, out_ref):
    kept = rows_ref[...].astype(F32) * keep_ref[...]
    out_ref[...] = to_plane(kept.astype(BF16))


def turn_rows(rows, keep):
    return own_rows(turn_kernel, [rows, keep], [(rows.shape, BF16)], "turn_rows")[0]


AXES = ("y", "xh", "z", "xl", "c")
DP = ("y", "xh", "z")
MP = ("xl", "c")
RING = ("xh", "xl")
PLANE = ("y", "z")
SWAP = ((0, 1), (1, 0))


def tied(value, token):
    return value + (0.0 * token[0, 0]).astype(value.dtype)


def after(value, *first):
    return lax.optimization_barrier((value,) + first)[0]


def other_core(value):
    return lax.ppermute(value, "c", SWAP)


def other_chip(value):
    return lax.ppermute(value, "xl", SWAP)


def along_ring(value, step):
    return lax.ppermute(value, RING, [(i, (i + step) % 4) for i in range(4)])


def gather_sides(own):
    return along_ring(own, 1), along_ring(own, -1), other_core(own)


def ring_opposite(opposite):
    half = opposite.shape[0] // 2
    return along_ring(opposite[:half], 1), along_ring(opposite[half:], -1)


def ring_sides(left, right, from_left, from_right):
    half = left.shape[0] // 2
    right = jnp.concatenate([right[:half] + from_left.astype(F32), right[half:]], axis=0)
    left = jnp.concatenate([left[:half], left[half:] + from_right.astype(F32)], axis=0)
    return left.astype(BF16), right.astype(BF16)


def ring_send(left, right):
    return along_ring(right, 1), along_ring(left, -1)


def add(left, right):
    return (left.astype(F32) + right.astype(F32)).astype(BF16)


def on_device(
    block_input,
    cotangent,
    pad_mask,
    seq_counts,
    gain_mix,
    query_weight,
    key_weight,
    value_weight,
    slot_weight,
    out_weight,
    gain_ffn,
    gate_weight,
    up_weight,
    down_weight,
):
    rows_own, width = block_input.shape
    rank = lax.axis_index(MP)
    side = lax.axis_index("xh")
    live = (jnp.arange(SEQS) < seq_counts[0]).astype(jnp.int32)
    keep_seq = (pad_mask[0] * live[:, None]).astype(F32)
    keep_own = lax.dynamic_slice_in_dim(keep_seq, rank * RUN, RUN, 1).reshape(rows_own, 1)

    rank_array = rank.reshape(1).astype(jnp.int32)

    hidden_part = gate_weight.shape[1] // 2
    kept, given = weight_halves(
        side.reshape(1).astype(jnp.int32), gate_weight, up_weight, down_weight.T
    )
    got = lax.ppermute(given, "xh", SWAP)
    paired = jnp.concatenate(
        [jnp.where(side == 0, kept, got), jnp.where(side == 0, got, kept)], axis=0
    )
    weights = lax.all_gather(paired, PLANE, axis=0, tiled=True)

    far = other_chip(after(block_input, got))
    cot_start = turn_rows(cotangent, keep_own)
    mixer_weights = (query_weight, key_weight, value_weight, slot_weight)
    near_input = other_core(block_input)
    keep_column = keep_seq[:, :, None]
    near_pre, near_normed, done = project_near(
        rank_array, (block_input, near_input), gain_mix[None], mixer_weights
    )
    farthest = other_core(tied(far, done))
    cot_sides = gather_sides(tied(cot_start, done))
    pre, normed_four, *blocks, mixing, probs, past = project_mix(
        rank_array, (far, farthest), gain_mix[None], mixer_weights,
        near_pre, near_normed, keep_column,
    )
    corner = cot_sides[0][:8, :128] + cot_sides[1][:8, :128] + blocks[0][:8, :128]
    mixed_parts = (
        blocks[0],
        other_core(blocks[1]),
        other_chip(tied(blocks[2], corner)),
        lax.ppermute(blocks[3], MP, [(i, 3 - i) for i in range(4)]),
    )
    hidden, ffn_own, mixed_own = mix_out(
        rank_array, mixed_parts, out_weight, block_input, keep_own, gain_ffn[None]
    )
    sides = gather_sides(ffn_own)
    half = rows_own // 2
    from_left = along_ring(jnp.concatenate([sides[0][:half], cot_sides[0][:half]], axis=0), 1)
    from_right = along_ring(jnp.concatenate([sides[1][half:], cot_sides[1][half:]], axis=0), -1)
    arrays = [ffn_own, *sides[:2], cot_start, *cot_sides[:2], from_left, from_right]
    arrays += [sides[2], *map(other_core, sides[:2])]
    arrays += [cot_sides[2], *map(other_core, cot_sides[:2])]
    arrays += [other_core(from_left), other_core(from_right)]
    plan = [
        [
            (core + at, first, count)
            for core in (0, 8)
            for at, first, count in (
                (3 * kind, 0, rows_own),
                (3 * kind + 1, 0, rows_own),
                (3 * kind + 2, 0, rows_own),
                (6, kind * half, half),
                (7, kind * half, half),
            )
        ]
        for kind in range(2)
    ]
    inner, cots, grads = ffn(arrays, plan, weights)
    ffn_sums = lax.psum_scatter(grads, PLANE, scatter_dimension=0, tiled=True)
    (away,) = ffn_back(cots, weights, pair_block, 1)
    (late_away,) = ffn_back(after(inner, away), weights, down_block, 1)
    got = other_core(away)
    own, left, right, ends = ffn_back(cots, weights, pair_block, 0, after(got, late_away))
    mixed_far = other_chip(tied(mixed_own, away))
    (late_near,) = ffn_back(
        after(inner, ends), weights, down_block, 0, done=(mixed_far, ends)
    )
    from_left, from_right, late_near = lax.optimization_barrier(
        ring_opposite(ends) + (late_near,)
    )
    left, right = ring_sides(left, right, from_left, from_right)
    from_left, from_right = ring_send(left, right)
    hidden_cot, branch_cot, gain_ffn_part = norm_back(
        own, from_left, from_right, cotangent, hidden, keep_own, gain_ffn[None]
    )
    branch_near = other_core(branch_cot)
    branch_far = other_chip(branch_cot)
    branch = (branch_cot, branch_near, branch_far, other_core(branch_far))
    head_cots = mixer_backward(
        rank_array, pre, keep_column, mixing, probs, past, out_weight, branch
    )
    mixed_all = (mixed_own, other_core(mixed_own), mixed_far, other_core(mixed_far))
    mixer_sums = lax.psum_scatter(
        mixer_grads(rank_array, normed_four, head_cots, mixed_all, branch),
        PLANE,
        scatter_dimension=0,
        tiled=True,
    )

    own, near, far, farthest, gain_mix_part = unproject(
        rank_array, after(head_cots, mixed_all[3]), normed_four, *mixer_weights
    )
    near = other_core(near)
    far = add(far, other_core(farthest))
    late_got = other_core(tied(late_away, gain_mix_part))
    gain_sums = jnp.stack([gain_mix_part[0] / gain_mix, gain_ffn_part[0]]).reshape(32, 128)
    for axis in ("c", "xl", "xh"):
        gain_sums = gain_sums + lax.ppermute(gain_sums, axis, SWAP)
    far = other_chip(tied(far, gain_sums))
    late_near = late_near.astype(F32) + late_got.astype(F32)
    late_own, late_left, late_right, late_ends = jnp.split(late_near, 4, axis=0)
    late_ends = ring_opposite(late_ends.astype(BF16))
    for axis in PLANE:
        for step in (1, 2):
            gain_sums = gain_sums + lax.ppermute(
                gain_sums, axis, [(i, i ^ step) for i in range(4)]
            )
    late_sides = ring_send(*ring_sides(late_left, late_right, *late_ends))
    gain_sums = gain_sums.reshape(2, width)
    input_grad = input_back(own, near, far, block_input, hidden_cot, gain_mix[None])
    block_output = block_out(late_own, *late_sides, hidden, keep_own)
    kept = lax.dynamic_slice_in_dim(ffn_sums, side * CHUNK, CHUNK, 0)
    given_back = lax.ppermute(
        lax.dynamic_slice_in_dim(ffn_sums, (1 - side) * CHUNK, CHUNK, 0), "xh", SWAP
    )
    mixer_sums, block_output, input_grad, gain_sums, given_back = lax.optimization_barrier(
        (mixer_sums, block_output, input_grad, gain_sums, given_back)
    )
    rows_out = rows_own // 8
    pieces = lax.all_to_all(
        mixer_sums.reshape(8, rows_out, COLUMNS), ("xh", "xl", "c"), 0, 0
    )
    query_grad, key_grad, value_grad, slot_grad, out_grad = mixer_out(pieces)

    def finish(tiles):
        mine, theirs = [
            jnp.concatenate([grads[:, n * TILE : (n + 1) * TILE] for n in tiles], axis=1)[
                :, :hidden_part
            ]
            for grads in (kept, given_back)
        ]
        return jnp.concatenate(
            [jnp.where(side == 0, mine, theirs), jnp.where(side == 0, theirs, mine)], axis=1
        ).astype(F32)

    return (
        block_output,
        input_grad,
        gain_sums[0],
        query_grad,
        key_grad,
        value_grad,
        slot_grad,
        out_grad,
        gain_sums[1],
        finish((0, 3, 6)),
        finish((1, 4, 7)),
        finish((2, 5, 8)).T,
    )


def solution(mesh):
    fine = jax.sharding.Mesh(mesh.devices.reshape(4, 2, 4, 2, 2), AXES)
    rows = P(AXES, None)
    return jax.shard_map(
        on_device,
        mesh=fine,
        in_specs=(
            rows,
            rows,
            P(DP, None, None),
            P(DP),
            P(),
            P(),
            P(),
            P(),
            P(),
            P(),
            P(),
            P(DP, MP),
            P(DP, MP),
            P(MP, DP),
        ),
        out_specs=(
            rows,
            rows,
            P(),
            rows,
            rows,
            rows,
            rows,
            rows,
            P(),
            P(DP, MP),
            P(DP, MP),
            P(MP, DP),
        ),
        check_vma=False,
    )
```
